256 devices in a mesh: dp: 16 (over x_lo, z), tensor: 16 (over y, x_hi, core).
Axes of the slice: x: 4 (x_hi: 2, x_lo: 2; x = x_hi * 2 + x_lo), y: 4, z: 8, core: 2. Of those that a mesh axis runs over, the one named last changes fastest.
Arguments:
- tokens: bfloat16 [2048, 65536], P('dp', 'tensor'), may hold values from -6 to 6
- cotangent: bfloat16 [2048, 65536], P('dp', 'tensor'), may hold values from -6 to 6
- diag_factor: bfloat16 [64, 65536], P(None, 'tensor'), may hold values from -0.3125 to 0.3125
- section_factors: bfloat16 [4, 64, 65536], P(None, None, 'tensor'), may hold values from -0.3125 to 0.3125
- low_down: bfloat16 [65536, 128], P('tensor'), may hold values from -0.0234375 to 0.0234375
- low_up: bfloat16 [128, 65536], P(None, 'tensor'), may hold values from -0.21875 to 0.21875
Outputs:
- token_grad: bfloat16 [2048, 65536], P('dp', 'tensor')
- diag_grad: float32 [64, 65536], P(None, ('tensor', 'dp'))
- section_grad: float32 [4, 64, 65536], P(None, None, ('tensor', 'dp'))
- low_down_grad: float32 [65536, 128], P(('tensor', 'dp'))
- low_up_grad: float32 [128, 65536], P(None, ('tensor', 'dp'))
The draws below stay inside these ranges and needn't reach their ends.
All inputs are finite; a program needn't handle non-finite values.
Results may differ from the reference program's by a relative error of at most 0.0057.
Values may be sent and summed in bfloat16 or wider, within the bound.
No kernel may reach another device: no remote copies, remote signals or barrier semaphores. Data moves between devices by JAX's collectives and lax.ppermute only.
A program may use at most 128 MiB of HBM per device.

```python
import math
import jax
import jax.numpy as jnp
from jax import lax

HID = 65536
BLOCK = 64
RANK = 128
TOK_DEV = 128
TOKENS = 2048
SECTIONS = 4
N_DP = 16
N_TENSOR = 16


def spiked(drawn, stream_key, source, target, shards_of, factor):
    def block_of(dim):
        return (jnp.arange(drawn.shape[dim]) // (drawn.shape[dim] // shards_of)).reshape((-1,) + (1,) * (drawn.ndim - 1 - dim))

    first = jax.random.permutation(stream_key, shards_of)[block_of(target)]
    second = (block_of(target) + shards_of // 2) % shards_of
    return jnp.where((block_of(source) == first) | (block_of(source) == second), factor * drawn, drawn)


def block_levels(rng, shape, pieces, low, top_value):
    gain, own = 1.0, jax.random.fold_in(rng, 6)
    for position, parts in pieces:
        draws = jnp.exp(jax.random.uniform(jax.random.fold_in(own, position), (parts,), jnp.float32, low / len(pieces), top_value / len(pieces)))
        gain = gain * jnp.repeat(draws, shape[position] // parts).reshape([-1 if axis == position else 1 for axis in range(len(shape))])
    return gain


def centred(stream_key, dims, deviation, most, split=(), dtype=jnp.bfloat16):
    entries = jax.random.normal(stream_key, dims, jnp.float32) * deviation
    if len(split) > 0:
        entries = block_levels(stream_key, dims, split, -0.22, 0.18) * entries
    return jnp.clip(entries, min=-most, max=most).astype(dtype)


def heavy_noise(own_key, dims, scale, most, shards, heavy, dtype=jnp.bfloat16):
    result = scale * jax.random.normal(own_key, dims, jnp.float32)
    if shards:
        result = result * block_levels(own_key, dims, shards, -0.22, 0.18)
    return jnp.clip(spiked(result, jax.random.fold_in(own_key, 3), *heavy), -most, most).astype(dtype)


def setup_inputs(seed: int = 0) -> dict:
    splits = jax.random.split(jax.random.key(seed), 7)
    tokens = heavy_noise(splits[0], (TOKENS, HID), 1.0, 6.0, ((0, 16), (1, 16)), (0, 1, 16, 2.0))
    cotangent = centred(splits[1], (TOKENS, HID), 1.0, 6.0, ((0, 16), (1, 16)))
    diag_factor = centred(splits[2], (BLOCK, HID), (BLOCK * (SECTIONS + 2)) ** -0.5, 0.3125, ((1, 16),))
    section_factors = centred(splits[3], (SECTIONS, BLOCK, HID), (BLOCK * (SECTIONS + 2)) ** -0.5, 0.3125, ((2, 16),))
    low_down = centred(splits[4], (HID, RANK), HID ** -0.5, 0.0234375, ((0, 16),))
    low_up = centred(splits[5], (RANK, HID), (RANK * (SECTIONS + 2)) ** -0.5, 0.21875, ((1, 16),))
    return {"tokens": tokens, "cotangent": cotangent, "diag_factor": diag_factor, "section_factors": section_factors, "low_down": low_down, "low_up": low_up}


def gelu_slope(values):
    return 0.5 * (1.0 + jax.scipy.special.erf(values * 0.7071067811865476)) + values * jnp.exp(-0.5 * values * values) * 0.3989422804014327

def partner_blocks(values, section_bit):
    span = 2 ** section_bit
    rows = values.shape[0]
    shaped = values.reshape(rows, N_TENSOR // (2 * span), 2, span, HID // N_TENSOR)
    return shaped[:, :, ::-1].reshape(rows, HID)

def block_apply(left, factor):
    rows = left.shape[0]
    lhs = left.reshape(rows, HID // BLOCK, BLOCK).astype(jnp.float32)
    rhs = factor.reshape(BLOCK, HID // BLOCK, BLOCK).astype(jnp.float32)
    return jnp.einsum('tbi,ibo->tbo', lhs, rhs).reshape(rows, HID)

def block_back(right, factor):
    rows = right.shape[0]
    lhs = right.reshape(rows, HID // BLOCK, BLOCK).astype(jnp.float32)
    rhs = factor.reshape(BLOCK, HID // BLOCK, BLOCK).astype(jnp.float32)
    return jnp.einsum('tbo,ibo->tbi', lhs, rhs).reshape(rows, HID)

def block_outer(left, right):
    rows = left.shape[0]
    lhs = left.reshape(rows, HID // BLOCK, BLOCK).astype(jnp.float32)
    rhs = right.reshape(rows, HID // BLOCK, BLOCK).astype(jnp.float32)
    return jnp.einsum('tbi,tbo->ibo', lhs, rhs).reshape(BLOCK, HID)

def reference(tokens, cotangent, diag_factor, section_factors, low_down, low_up):
    factor_scale = 1.0 / math.sqrt(TOKENS)

    def one_group(carry, inputs):
        group_tokens, group_cot = inputs
        moved = [partner_blocks(group_tokens, section_bit) for section_bit in range(SECTIONS)]
        latent = jnp.dot(group_tokens, low_down, preferred_element_type=jnp.float32).astype(jnp.bfloat16)
        preact = block_apply(group_tokens, diag_factor)
        for section_bit in range(SECTIONS):
            preact = preact + block_apply(moved[section_bit], section_factors[section_bit])
        preact = preact + jnp.dot(latent, low_up, preferred_element_type=jnp.float32)
        slope_grad = (group_cot.astype(jnp.float32) * gelu_slope(preact)).astype(jnp.bfloat16)
        latent_grad = jnp.dot(slope_grad, low_up.T, preferred_element_type=jnp.float32).astype(jnp.bfloat16)
        token_grad = block_back(slope_grad, diag_factor)
        for section_bit in range(SECTIONS):
            back_part = block_back(slope_grad, section_factors[section_bit]).astype(jnp.bfloat16)
            token_grad = token_grad + partner_blocks(back_part, section_bit).astype(jnp.float32)
        token_grad = token_grad + jnp.dot(latent_grad, low_down.T, preferred_element_type=jnp.float32)
        diag_part = block_outer(group_tokens, slope_grad) * factor_scale
        section_part = jnp.stack([block_outer(moved[section_bit], slope_grad) * factor_scale for section_bit in range(SECTIONS)])
        down_part = jnp.dot(group_tokens.T, latent_grad, preferred_element_type=jnp.float32) * factor_scale
        up_part = jnp.dot(latent.T, slope_grad, preferred_element_type=jnp.float32) * factor_scale
        carry = (carry[0] + diag_part, carry[1] + section_part, carry[2] + down_part, carry[3] + up_part)
        return (carry, token_grad.astype(jnp.bfloat16))
    start = (jnp.zeros((BLOCK, HID), jnp.float32), jnp.zeros((SECTIONS, BLOCK, HID), jnp.float32), jnp.zeros((HID, RANK), jnp.float32), jnp.zeros((RANK, HID), jnp.float32))
    inputs = (tokens.reshape(N_DP, TOK_DEV, HID), cotangent.reshape(N_DP, TOK_DEV, HID))
    totals, token_grads = lax.scan(one_group, start, inputs)
    return (token_grads.reshape(TOKENS, HID), totals[0], totals[1], totals[2], totals[3])
```

```python
import jax
import jax.numpy as jnp
from jax import lax
from jax.experimental import pallas as pl
from jax.experimental.pallas import tpu as pltpu
from jax.sharding import PartitionSpec as P

BLOCK = 64
CHUNK = 256
STEP = 512
RING = 8
F32 = jnp.float32
BF16 = jnp.bfloat16


def dot(a, b, ca, cb):
    return lax.dot_general(a, b, (((ca,), (cb,)), ((), ())), preferred_element_type=F32)


def gelu_slope(values):
    return (
        0.5 * (1.0 + lax.erf(values * 0.7071067811865476))
        + values * jnp.exp(-0.5 * values * values) * 0.3989422804014327
    )


def block_mask():
    row = lax.broadcasted_iota(jnp.int32, (CHUNK, CHUNK), 0) // BLOCK
    col = lax.broadcasted_iota(jnp.int32, (CHUNK, CHUNK), 1) // BLOCK
    return row == col


def spread(factor, mask):
    tall = jnp.concatenate([factor] * (CHUNK // BLOCK), axis=0)
    return jnp.where(mask, tall, jnp.zeros_like(tall))


def gather_blocks(full, mask):
    kept = jnp.where(mask, full, jnp.zeros_like(full))
    return sum(kept[i * BLOCK : (i + 1) * BLOCK] for i in range(CHUNK // BLOCK))


def main_kernel(
    tok, m1, m2, m4, m8, cot, diag, sec, latent, up,
    slope_out, b1, b2, b4, b8, grads, lat_out,
):
    mask = block_mask()
    lat = latent[...]
    lat_sum = jnp.zeros((lat.shape[0], up.shape[0]), F32)
    for c in range(STEP // CHUNK):
        cs = slice(c * CHUNK, (c + 1) * CHUNK)
        up_c = up[:, cs]
        factors = [spread(diag[:, cs], mask)] + [spread(sec[b, :, cs], mask) for b in range(4)]
        sides = [tok[:, cs], m1[:, cs], m2[:, cs], m4[:, cs], m8[:, cs]]
        left = jnp.concatenate(sides + [lat], axis=1)
        right = jnp.concatenate(factors + [up_c], axis=0)
        pre = dot(left, right, 1, 0)
        slope = (cot[:, cs].astype(F32) * gelu_slope(pre)).astype(BF16)
        slope_out[:, cs] = slope
        lat_sum = lat_sum + dot(slope, up_c, 1, 1)
        for b, ref in enumerate((b1, b2, b4, b8)):
            ref[:, cs] = dot(slope, factors[b + 1], 1, 1).astype(BF16)
        for k in range(5):
            part = gather_blocks(dot(sides[k], slope, 0, 0), mask)
            grads[c, k * BLOCK : (k + 1) * BLOCK, :] = part.astype(BF16)
        grads[c, 5 * BLOCK :, :] = dot(lat, slope, 0, 0).astype(BF16)

    @pl.when(pl.program_id(0) == 0)
    def _():
        lat_out[...] = lat_sum

    @pl.when(pl.program_id(0) > 0)
    def _():
        lat_out[...] += lat_sum


def run_main(part, tokens, moved, cotangent, diag, section, latent, up):
    rows, width = moved[0].shape
    rank = up.shape[0]
    steps = width // STEP
    base = part * steps
    whole = lambda r: pl.BlockSpec((r, STEP), lambda i: (0, base + i))
    local = pl.BlockSpec((rows, STEP), lambda i: (0, i))
    per = STEP // CHUNK
    count = width // CHUNK
    grad_rows = 5 * BLOCK + rank
    wide = jax.ShapeDtypeStruct((rows, width), BF16)
    return pl.pallas_call(
        main_kernel,
        grid=(steps,),
        in_specs=[
            whole(rows), local, local, local, local, whole(rows), whole(BLOCK),
            pl.BlockSpec((4, BLOCK, STEP), lambda i: (0, 0, base + i)),
            pl.BlockSpec((rows, rank), lambda i: (0, 0)),
            whole(rank),
        ],
        out_specs=[local] * 5
        + [
            pl.BlockSpec((per, grad_rows, CHUNK), lambda i: (i, 0, 0)),
            pl.BlockSpec((rows, rank), lambda i: (0, 0)),
        ],
        out_shape=[wide] * 5
        + [
            jax.ShapeDtypeStruct((count, grad_rows, CHUNK), BF16),
            jax.ShapeDtypeStruct((rows, rank), F32),
        ],
        compiler_params=pltpu.CompilerParams(vmem_limit_bytes=24 << 20),
        cost_estimate=pl.CostEstimate(flops=6_000_000_000, bytes_accessed=10 << 20, transcendentals=0),
        name="main_part",
    )(tokens, *moved, cotangent, diag, section, latent, up)


def down_kernel(tok, lat, out):
    for c in range(tok.shape[1] // CHUNK):
        full = dot(tok[:, c * CHUNK : (c + 1) * CHUNK], lat[...], 0, 0)
        half = CHUNK // 2
        out[c] = jnp.concatenate([full[:half], full[half:]], axis=1).astype(BF16)


def run_down(tokens, latent_grad):
    rows, width = tokens.shape
    rank = latent_grad.shape[1]
    wide = 1024
    return pl.pallas_call(
        down_kernel,
        grid=(width // wide,),
        in_specs=[pl.BlockSpec((rows, wide), lambda i: (0, i)), pl.BlockSpec((rows, rank), lambda i: (0, 0))],
        out_specs=pl.BlockSpec((wide // CHUNK, CHUNK // 2, 2 * rank), lambda i: (i, 0, 0)),
        out_shape=jax.ShapeDtypeStruct((width // CHUNK, CHUNK // 2, 2 * rank), BF16),
        cost_estimate=pl.CostEstimate(flops=300_000_000, bytes_accessed=2 << 20, transcendentals=0),
        name="down_part",
    )(tokens, latent_grad)


def final_kernel(s0, s1, r1, r2, r4, r8, diag, down, lat, out):
    mask = block_mask()
    first = pl.program_id(0) < pl.num_programs(0) // 2
    for c in range(STEP // CHUNK):
        cs = slice(c * CHUNK, (c + 1) * CHUNK)
        slope = jnp.where(first, s0[:, cs], s1[:, cs])
        total = dot(slope, spread(diag[:, cs], mask), 1, 1)
        total = total + dot(lat[...], down[cs, :], 1, 1)
        for ref in (r1, r2, r4, r8):
            total = total + ref[:, cs].astype(F32)
        out[:, cs] = total.astype(BF16)


def run_final(slopes, received, diag, low_down, latent_grad):
    rows, width = received[0].shape
    rank = latent_grad.shape[1]
    steps = width // STEP
    half = steps // 2
    col = lambda r: pl.BlockSpec((r, STEP), lambda i: (0, i))
    return pl.pallas_call(
        final_kernel,
        grid=(steps,),
        in_specs=[
            pl.BlockSpec((rows, STEP), lambda i: (0, jnp.minimum(i, half - 1))),
            pl.BlockSpec((rows, STEP), lambda i: (0, jnp.maximum(i - half, 0))),
        ]
        + [col(rows)] * 4
        + [
            col(BLOCK),
            pl.BlockSpec((STEP, rank), lambda i: (i, 0)),
            pl.BlockSpec((rows, rank), lambda i: (0, 0)),
        ],
        out_specs=col(rows),
        out_shape=jax.ShapeDtypeStruct((rows, width), BF16),
        cost_estimate=pl.CostEstimate(flops=2_000_000_000, bytes_accessed=9 << 20, transcendentals=0),
        name="token_grad",
    )(*slopes, *received, diag, low_down, latent_grad)


def flip(value, mask):
    return lax.ppermute(value, "tensor", [(i, i ^ mask) for i in range(16)])


def tensor_sum(value):
    for mask in (4, 12, 2, 1):
        value = value + flip(value, mask)
    return value


def z_move(value, by):
    pairs = [(i, i // RING * RING + (i + by) % RING) for i in range(2 * RING)]
    return lax.ppermute(value, "dp", pairs)


def ring_sum(parts, z, sign):
    pick = lambda off: lax.dynamic_index_in_dim(parts, (z + off) % RING, 0, keepdims=False)
    add = lambda a, off: (a.astype(F32) + pick(off).astype(F32)).astype(BF16)
    far = z_move(pick(4 * sign), sign)
    near = z_move(pick(-3 * sign), -sign)
    far = z_move(add(far, 3 * sign), sign)
    near = z_move(add(near, -2 * sign), -sign)
    far = z_move(add(far, 2 * sign), sign)
    near = z_move(add(near, -sign), -sign)
    far = z_move(add(far, sign), sign)
    return pick(0).astype(F32) + far.astype(F32) + near.astype(F32)


def pair_sum(low, high, x):
    mine = jnp.where(x == 0, low, high)
    other = jnp.where(x == 0, high, low).astype(BF16)
    return mine + lax.ppermute(other, "dp", [(i, i ^ RING) for i in range(2 * RING)]).astype(F32)


def per_device(tokens, cotangent, diag_factor, section_factors, low_down, low_up):
    rows, width = tokens.shape
    scale = (rows * lax.axis_size("dp")) ** -0.5
    position = lax.axis_index("dp")
    z, x = position % RING, position // RING
    half = width // 2
    halves = [tokens[:, :half], tokens[:, half:]]

    latent = tensor_sum(jnp.dot(tokens, low_down, preferred_element_type=F32)).astype(BF16)
    moved = []
    for part in halves:
        m4 = flip(part, 4)
        moved.append((flip(part, 1), flip(part, 2), m4, flip(m4, 12)))

    slopes, backs, sums, lat_parts = [], [], [], []
    for p in range(2):
        out = run_main(p, tokens, moved[p], cotangent, diag_factor, section_factors, latent, low_up)
        slopes.append(out[0])
        backs.append(out[1:5])
        lat_parts.append(out[6])
        sums.append(ring_sum(out[5], z, 1 - 2 * p))

    latent_grad = tensor_sum(lat_parts[0] + lat_parts[1]).astype(BF16)
    received = [
        flip(jnp.concatenate([backs[0][b], backs[1][b]], axis=1), 1 << b) for b in range(4)
    ]
    down = run_down(tokens, latent_grad)
    down_sum = pair_sum(ring_sum(down[:RING], z, 1), ring_sum(down[RING:], z, -1), x) * scale
    token_grad = run_final(slopes, received, diag_factor, low_down, latent_grad)
    grads = pair_sum(sums[0], sums[1], x) * scale
    rank = low_up.shape[0]
    down_grad = jnp.concatenate([down_sum[:, :rank], down_sum[:, rank:]], axis=0)
    return (
        token_grad,
        grads[:BLOCK],
        grads[BLOCK : 5 * BLOCK].reshape(4, BLOCK, CHUNK),
        down_grad,
        grads[5 * BLOCK :],
    )


def solution(mesh):
    placed = (
        P("dp", "tensor"),
        P("dp", "tensor"),
        P(None, "tensor"),
        P(None, None, "tensor"),
        P("tensor", None),
        P(None, "tensor"),
    )
    return jax.shard_map(
        per_device,
        mesh=mesh,
        in_specs=placed,
        out_specs=(
            P("dp", "tensor"),
            P(None, ("tensor", "dp")),
            P(None, None, ("tensor", "dp")),
            P(("tensor", "dp"), None),
            P(None, ("tensor", "dp")),
        ),
        check_vma=False,
    )
```

```python
import jax
import jax.numpy as jnp
from jax import lax
from jax.experimental import pallas as pl
from jax.experimental.pallas import tpu as pltpu
from jax.sharding import PartitionSpec as P

BLOCK = 64
CHUNK = 256
STEP = 512
RING = 8
VMEM = 56 << 20
F32 = jnp.float32
BF16 = jnp.bfloat16


def dot(a, b, ca, cb):
    return lax.dot_general(a, b, (((ca,), (cb,)), ((), ())), preferred_element_type=F32)


def gelu_slope(values):
    return (
        0.5 * (1.0 + lax.erf(values * 0.7071067811865476))
        + values * jnp.exp(-0.5 * values * values) * 0.3989422804014327
    )


def block_mask():
    row = lax.broadcasted_iota(jnp.int32, (CHUNK, CHUNK), 0) // BLOCK
    col = lax.broadcasted_iota(jnp.int32, (CHUNK, CHUNK), 1) // BLOCK
    return row == col


def spread(factor, mask):
    tall = jnp.concatenate([factor] * (CHUNK // BLOCK), axis=0)
    return jnp.where(mask, tall, jnp.zeros_like(tall))


def slope_kernel(tok, m1, m2, m4, m8, cot, diag, sec, latent, up, slope_out, lat_out):
    mask = block_mask()
    lat = latent[...]
    lat_sum = jnp.zeros((lat.shape[0], up.shape[0]), F32)
    for c in range(STEP // CHUNK):
        cs = slice(c * CHUNK, (c + 1) * CHUNK)
        up_c = up[:, cs]
        factors = [spread(diag[:, cs], mask)] + [spread(sec[b, :, cs], mask) for b in range(4)]
        left = jnp.concatenate([tok[:, cs], m1[:, cs], m2[:, cs], m4[:, cs], m8[:, cs], lat], axis=1)
        right = jnp.concatenate(factors + [up_c], axis=0)
        pre = dot(left, right, 1, 0)
        slope = (cot[:, cs].astype(F32) * gelu_slope(pre)).astype(BF16)
        slope_out[:, cs] = slope
        lat_sum = lat_sum + dot(slope, up_c, 1, 1)

    @pl.when(pl.program_id(0) == 0)
    def _():
        lat_out[...] = lat_sum

    @pl.when(pl.program_id(0) > 0)
    def _():
        lat_out[...] += lat_sum


def product_kernel(slope_in, tok, m1, m2, m4, m8, sec, latent, b1, b2, b4, b8, grads):
    mask = block_mask()
    rows = tok.shape[0]
    lat = latent[...]
    group = CHUNK // BLOCK
    owner = lax.broadcasted_iota(jnp.int32, (group * rows, CHUNK), 0) // rows
    tall_mask = owner == lax.broadcasted_iota(jnp.int32, (group * rows, CHUNK), 1) // BLOCK
    for c in range(STEP // CHUNK):
        cs = slice(c * CHUNK, (c + 1) * CHUNK)
        slope = slope_in[:, cs]
        for b, ref in enumerate((b1, b2, b4, b8)):
            ref[:, cs] = dot(slope, spread(sec[b, :, cs], mask), 1, 1).astype(BF16)
        tall = jnp.concatenate([slope] * group, axis=0)
        tall = jnp.where(tall_mask, tall, jnp.zeros_like(tall))
        for k, side in enumerate((tok, m1, m2, m4, m8)):
            turned = side[:, cs].T
            wide = jnp.concatenate([turned[i * BLOCK : (i + 1) * BLOCK] for i in range(group)], axis=1)
            grads[c, k * BLOCK : (k + 1) * BLOCK, :] = dot(wide, tall, 1, 0).astype(BF16)
        grads[c, 5 * BLOCK :, :] = dot(lat, slope, 0, 0).astype(BF16)


def specs_of(part, rows, width, rank):
    steps = width // STEP
    base = part * steps
    whole = lambda r: pl.BlockSpec((r, STEP), lambda i: (0, base + i))
    local = pl.BlockSpec((rows, STEP), lambda i: (0, i))
    square = pl.BlockSpec((rows, rank), lambda i: (0, 0))
    section = pl.BlockSpec((4, BLOCK, STEP), lambda i: (0, 0, base + i))
    return steps, whole, local, square, section


def run_slope(part, tokens, moved, cotangent, diag, section, latent, up):
    rows, width = moved[2].shape
    rank = up.shape[0]
    steps, whole, local, square, sec_spec = specs_of(part, rows, width, rank)
    return pl.pallas_call(
        slope_kernel,
        grid=(steps,),
        in_specs=[whole(rows), whole(rows), local, local, local, whole(rows), whole(BLOCK), sec_spec, square, whole(rank)],
        out_specs=[local, square],
        out_shape=[jax.ShapeDtypeStruct((rows, width), BF16), jax.ShapeDtypeStruct((rows, rank), F32)],
        compiler_params=pltpu.CompilerParams(vmem_limit_bytes=VMEM),
        cost_estimate=pl.CostEstimate(flops=2_000_000_000, bytes_accessed=6 << 20, transcendentals=0),
        name="slope_part",
    )(tokens, *moved, cotangent, diag, section, latent, up)


def run_products(part, slope, tokens, moved, section, latent):
    rows, width = slope.shape
    rank = latent.shape[1]
    steps, whole, local, square, sec_spec = specs_of(part, rows, width, rank)
    per = STEP // CHUNK
    grad_rows = 5 * BLOCK + rank
    return pl.pallas_call(
        product_kernel,
        grid=(steps,),
        in_specs=[local, whole(rows), whole(rows), local, local, local, sec_spec, square],
        out_specs=[local] * 4 + [pl.BlockSpec((per, grad_rows, CHUNK), lambda i: (i, 0, 0))],
        out_shape=[jax.ShapeDtypeStruct((rows, width), BF16)] * 4
        + [jax.ShapeDtypeStruct((width // CHUNK, grad_rows, CHUNK), BF16)],
        compiler_params=pltpu.CompilerParams(vmem_limit_bytes=VMEM),
        cost_estimate=pl.CostEstimate(flops=3_000_000_000, bytes_accessed=9 << 20, transcendentals=0),
        name="product_part",
    )(slope, tokens, *moved, section, latent)


def down_kernel(tok, lat, out):
    for c in range(tok.shape[1] // CHUNK):
        full = dot(tok[:, c * CHUNK : (c + 1) * CHUNK], lat[...], 0, 0)
        half = CHUNK // 2
        out[c] = jnp.concatenate([full[:half], full[half:]], axis=1).astype(BF16)


def run_down(tokens, latent_grad):
    rows, width = tokens.shape
    rank = latent_grad.shape[1]
    wide = 1024
    return pl.pallas_call(
        down_kernel,
        grid=(width // wide,),
        in_specs=[pl.BlockSpec((rows, wide), lambda i: (0, i)), pl.BlockSpec((rows, rank), lambda i: (0, 0))],
        out_specs=pl.BlockSpec((wide // CHUNK, CHUNK // 2, 2 * rank), lambda i: (i, 0, 0)),
        out_shape=jax.ShapeDtypeStruct((width // CHUNK, CHUNK // 2, 2 * rank), BF16),
        cost_estimate=pl.CostEstimate(flops=300_000_000, bytes_accessed=2 << 20, transcendentals=0),
        name="down_part",
    )(tokens, latent_grad)


def final_kernel(slope_in, r1, r2, r48, diag, down, lat, out):
    mask = block_mask()
    for c in range(STEP // CHUNK):
        cs = slice(c * CHUNK, (c + 1) * CHUNK)
        total = dot(slope_in[:, cs], spread(diag[:, cs], mask), 1, 1)
        total = total + dot(lat[...], down[cs, :], 1, 1)
        for ref in (r1, r2, r48):
            total = total + ref[:, cs].astype(F32)
        out[:, cs] = total.astype(BF16)


def final_second(slope_in, r1, r2, r48, diag, down, lat, held, out):
    final_kernel(slope_in, r1, r2, r48, diag, down, lat, out)


def run_final(part, slope, received, diag, low_down, latent_grad, held):
    rows, width = slope.shape
    rank = latent_grad.shape[1]
    steps, whole, local, square, _ = specs_of(part, rows, width, rank)
    base = part * steps
    down_spec = pl.BlockSpec((STEP, rank), lambda i: (base + i, 0))
    in_specs = [local] * 4 + [whole(BLOCK), down_spec, square]
    args = [slope, *received, diag, low_down, latent_grad]
    if held is not None:
        in_specs.append(pl.BlockSpec(memory_space=pl.ANY))
        args.append(held)
    return pl.pallas_call(
        final_kernel if held is None else final_second,
        grid=(steps,),
        in_specs=in_specs,
        out_specs=whole(rows),
        out_shape=jax.ShapeDtypeStruct((rows, diag.shape[1]), BF16),
        input_output_aliases={} if held is None else {7: 0},
        compiler_params=pltpu.CompilerParams(vmem_limit_bytes=VMEM),
        cost_estimate=pl.CostEstimate(flops=1_000_000_000, bytes_accessed=4 << 20, transcendentals=0),
        name="token_grad",
    )(*args)


def flip(value, mask):
    return lax.ppermute(value, "tensor", [(i, i ^ mask) for i in range(16)])


def after(value, *events):
    return lax.optimization_barrier((value, *events))[0]


def z_move(value, by):
    pairs = [(i, i // RING * RING + (i + by) % RING) for i in range(2 * RING)]
    return lax.ppermute(value, "dp", pairs)


class Ring:
    def __init__(self, parts, z, sign):
        self.parts, self.z, self.sign, self.left = parts, z, sign, 4
        self.far = z_move(self.pick(4 * sign), sign)
        self.near = z_move(self.pick(-3 * sign), -sign)

    def pick(self, off):
        return lax.dynamic_index_in_dim(self.parts, (self.z + off) % RING, 0, keepdims=False)

    def step(self, event):
        self.left -= 1
        off = self.left
        add = lambda a, o: (after(a, event).astype(F32) + self.pick(o).astype(F32)).astype(BF16)
        far = add(self.far, off * self.sign)
        self.far = z_move(far, self.sign)
        if off > 1:
            near = add(self.near, -(off - 1) * self.sign)
            self.near = z_move(near, -self.sign)
        return far

    def total(self):
        return self.pick(0).astype(F32) + self.far.astype(F32) + self.near.astype(F32)


def pair_sum(low, high, x):
    mine = jnp.where(x == 0, low, high)
    other = jnp.where(x == 0, high, low).astype(BF16)
    return mine + lax.ppermute(other, "dp", [(i, i ^ RING) for i in range(2 * RING)]).astype(F32)


def per_device(tokens, cotangent, diag_factor, section_factors, low_down, low_up):
    rows, width = tokens.shape
    scale = (rows * lax.axis_size("dp")) ** -0.5
    position = lax.axis_index("dp")
    z, x = position % RING, position // RING
    half = width // 2
    h0, h1 = tokens[:, :half], tokens[:, half:]

    m4_0 = flip(h0, 4)
    m1 = flip(tokens, 1)
    part = jnp.dot(tokens, low_down, preferred_element_type=F32)
    part = part + flip(part, 1)
    part = part + flip(part, 2)
    m2_0 = flip(after(h0, part), 2)
    m8_0 = flip(after(m4_0, part), 12)
    part = part + flip(part, 4)
    m4_1 = flip(after(h1, m4_0, part), 4)
    part = part + flip(part, 12)
    latent = part.astype(BF16)
    m2_1 = flip(after(h1, m2_0), 2)
    m8_1 = flip(m4_1, 12)

    moved0 = (m1, m2_0, m4_0, m8_0)
    slope0, lat0 = run_slope(0, tokens, moved0, cotangent, diag_factor, section_factors, latent, low_up)
    back0 = run_products(0, slope0, tokens, moved0, section_factors, latent)
    ring0 = Ring(back0[4], z, 1)
    q0 = flip(back0[3], 12)
    x0 = flip(back0[1], 2)

    moved1 = (m1, m2_1, m4_1, after(m8_1, back0[4]))
    slope1, lat1 = run_slope(1, tokens, moved1, cotangent, diag_factor, section_factors, latent, low_up)
    part = lat0 + lat1
    arrived = flip(part, 4)
    back1 = run_products(1, slope1, tokens, moved1, section_factors, latent)
    part = part + after(arrived, back1[4])
    ring1 = Ring(back1[4], z, -1)
    event = ring0.step(part)
    part = part + after(flip(part, 12), event)
    event = ring0.step(part)
    part = part + after(flip(part, 2), event)
    event = ring1.step(part)
    part = part + after(flip(part, 1), event)
    latent_grad = part.astype(BF16)
    down = run_down(tokens, latent_grad)
    down0, down1 = Ring(down[:RING], z, 1), Ring(down[RING:], z, -1)
    s0 = flip(after(back0[2], latent_grad) + q0, 4)
    q1 = flip(after(back1[3], latent_grad), 12)
    c0 = flip(after(back0[0], latent_grad), 1)
    c1 = flip(after(back1[0], latent_grad), 1)
    x1 = flip(after(back1[1], latent_grad), 2)
    event = ring0.step(down)
    event = ring1.step(event)
    event = down0.step(event)
    event = down1.step(event)
    event = ring1.step(event)
    event = down0.step(event)
    event = down1.step(event)
    grads = pair_sum(ring0.total(), ring1.total(), x) * scale
    event = down0.step(event)
    event = down1.step(event)
    down_sum = pair_sum(down0.total(), down1.total(), x) * scale
    s1 = flip(back1[2] + q1, 4)
    token_grad = run_final(0, slope0, (c0, x0, s0), diag_factor, low_down, latent_grad, None)
    token_grad = run_final(1, slope1, (c1, x1, s1), diag_factor, low_down, latent_grad, token_grad)
    rank = low_up.shape[0]
    down_grad = jnp.concatenate([down_sum[:, :rank], down_sum[:, rank:]], axis=0)
    return (
        token_grad,
        grads[:BLOCK],
        grads[BLOCK : 5 * BLOCK].reshape(4, BLOCK, CHUNK),
        down_grad,
        grads[5 * BLOCK :],
    )


def solution(mesh):
    placed = (
        P("dp", "tensor"),
        P("dp", "tensor"),
        P(None, "tensor"),
        P(None, None, "tensor"),
        P("tensor", None),
        P(None, "tensor"),
    )
    return jax.shard_map(
        per_device,
        mesh=mesh,
        in_specs=placed,
        out_specs=(
            P("dp", "tensor"),
            P(None, ("tensor", "dp")),
            P(None, None, ("tensor", "dp")),
            P(("tensor", "dp"), None),
            P(None, ("tensor", "dp")),
        ),
        check_vma=False,
    )
```

```python
import jax
import jax.numpy as jnp
from jax import lax
from jax.experimental import pallas as pl
from jax.experimental.pallas import tpu as pltpu
from jax.sharding import PartitionSpec as P

BLOCK = 64
CHUNK = 256
STEP = 512
RING = 8
VMEM = 56 << 20
F32 = jnp.float32
BF16 = jnp.bfloat16


def dot(a, b, ca, cb):
    return lax.dot_general(a, b, (((ca,), (cb,)), ((), ())), preferred_element_type=F32)


def gelu_slope(values):
    return (
        0.5 * (1.0 + lax.erf(values * 0.7071067811865476))
        + values * jnp.exp(-0.5 * values * values) * 0.3989422804014327
    )


def block_mask():
    row = lax.broadcasted_iota(jnp.int32, (CHUNK, CHUNK), 0) // BLOCK
    col = lax.broadcasted_iota(jnp.int32, (CHUNK, CHUNK), 1) // BLOCK
    return row == col


def spread(factor, mask):
    tall = jnp.concatenate([factor] * (CHUNK // BLOCK), axis=0)
    return jnp.where(mask, tall, jnp.zeros_like(tall))


def slope_kernel(tok, m1, m2, m4, m8, cot, diag, sec, latent, up, slope_out, lat_out):
    mask = block_mask()
    lat = latent[...]
    lat_sum = jnp.zeros((lat.shape[0], up.shape[0]), F32)
    for c in range(STEP // CHUNK):
        cs = slice(c * CHUNK, (c + 1) * CHUNK)
        up_c = up[:, cs]
        factors = [spread(diag[:, cs], mask)] + [spread(sec[b, :, cs], mask) for b in range(4)]
        left = jnp.concatenate([tok[:, cs], m1[:, cs], m2[:, cs], m4[:, cs], m8[:, cs], lat], axis=1)
        right = jnp.concatenate(factors + [up_c], axis=0)
        pre = dot(left, right, 1, 0)
        slope = (cot[:, cs].astype(F32) * gelu_slope(pre)).astype(BF16)
        slope_out[:, cs] = slope
        lat_sum = lat_sum + dot(slope, up_c, 1, 1)

    @pl.when(pl.program_id(0) == 0)
    def _():
        lat_out[...] = lat_sum

    @pl.when(pl.program_id(0) > 0)
    def _():
        lat_out[...] += lat_sum


def outer_kernel(slope_in, tok, m1, m2, m4, m8, latent, *refs):
    grads = refs[-1]
    rows = tok.shape[0]
    lat = latent[...]
    group = CHUNK // BLOCK
    owner = lax.broadcasted_iota(jnp.int32, (group * rows, CHUNK), 0) // rows
    tall_mask = owner == lax.broadcasted_iota(jnp.int32, (group * rows, CHUNK), 1) // BLOCK
    for c in range(STEP // CHUNK):
        cs = slice(c * CHUNK, (c + 1) * CHUNK)
        slope = slope_in[:, cs]
        tall = jnp.concatenate([slope] * group, axis=0)
        tall = jnp.where(tall_mask, tall, jnp.zeros_like(tall))
        for k, side in enumerate((tok, m1, m2, m4, m8)):
            turned = side[:, cs].T
            wide = jnp.concatenate([turned[i * BLOCK : (i + 1) * BLOCK] for i in range(group)], axis=1)
            grads[c, 0, k * BLOCK : (k + 1) * BLOCK, :] = dot(wide, tall, 1, 0).astype(BF16)
        grads[c, 0, 5 * BLOCK :, :] = dot(lat, slope, 0, 0).astype(BF16)


def pick_half(low, high):
    first = pl.program_id(0) < pl.num_programs(0) // 2
    return jnp.where(first, low[...], high[...])


def half_specs(rows, steps):
    half = steps // 2
    return [
        pl.BlockSpec((rows, STEP), lambda i: (0, jnp.minimum(i, half - 1))),
        pl.BlockSpec((rows, STEP), lambda i: (0, jnp.maximum(i - half, 0))),
    ]


def back_kernel(low, high, sec, b1, b2, b4, b8):
    mask = block_mask()
    slope = pick_half(low, high)
    for c in range(STEP // CHUNK):
        cs = slice(c * CHUNK, (c + 1) * CHUNK)
        for b, ref in enumerate((b1, b2, b4, b8)):
            ref[:, cs] = dot(slope[:, cs], spread(sec[b, :, cs], mask), 1, 1).astype(BF16)


def run_back(slopes, section):
    rows = slopes[0].shape[0]
    width = section.shape[2]
    steps = width // STEP
    return pl.pallas_call(
        back_kernel,
        grid=(steps,),
        in_specs=half_specs(rows, steps) + [pl.BlockSpec((4, BLOCK, STEP), lambda i: (0, 0, i))],
        out_specs=[pl.BlockSpec((rows, STEP), lambda i: (0, i))] * 4,
        out_shape=[jax.ShapeDtypeStruct((rows, width), BF16)] * 4,
        compiler_params=pltpu.CompilerParams(vmem_limit_bytes=VMEM),
        cost_estimate=pl.CostEstimate(flops=3_000_000_000, bytes_accessed=7 << 20, transcendentals=0),
        name="back_products",
    )(*slopes, section)


def specs_of(part, rows, width, rank):
    steps = width // STEP
    base = part * steps
    whole = lambda r: pl.BlockSpec((r, STEP), lambda i: (0, base + i))
    local = pl.BlockSpec((rows, STEP), lambda i: (0, i))
    square = pl.BlockSpec((rows, rank), lambda i: (0, 0))
    section = pl.BlockSpec((4, BLOCK, STEP), lambda i: (0, 0, base + i))
    return steps, whole, local, square, section


def run_slope(part, tokens, moved, cotangent, diag, section, latent, up):
    rows, width = moved[2].shape
    rank = up.shape[0]
    steps, whole, local, square, sec_spec = specs_of(part, rows, width, rank)
    return pl.pallas_call(
        slope_kernel,
        grid=(steps,),
        in_specs=[whole(rows), whole(rows), local, local, local, whole(rows), whole(BLOCK), sec_spec, square, whole(rank)],
        out_specs=[local, square],
        out_shape=[jax.ShapeDtypeStruct((rows, width), BF16), jax.ShapeDtypeStruct((rows, rank), F32)],
        compiler_params=pltpu.CompilerParams(vmem_limit_bytes=VMEM),
        cost_estimate=pl.CostEstimate(flops=2_000_000_000, bytes_accessed=6 << 20, transcendentals=0),
        name="slope_part",
    )(tokens, *moved, cotangent, diag, section, latent, up)


def run_outer(part, slope, tokens, moved, latent, held):
    rows, width = slope.shape
    rank = latent.shape[1]
    steps, whole, local, square, _ = specs_of(part, rows, width, rank)
    per = STEP // CHUNK
    grad_rows = 5 * BLOCK + rank
    in_specs = [local, whole(rows), whole(rows), local, local, local, square]
    args = [slope, tokens, *moved, latent]
    if held is not None:
        in_specs.append(pl.BlockSpec(memory_space=pl.ANY))
        args.append(held)
    return pl.pallas_call(
        outer_kernel,
        grid=(steps,),
        in_specs=in_specs,
        out_specs=pl.BlockSpec((per, 1, grad_rows, CHUNK), lambda i: (i, part, 0, 0)),
        out_shape=jax.ShapeDtypeStruct((RING, 2, grad_rows, CHUNK), BF16),
        input_output_aliases={} if held is None else {7: 0},
        compiler_params=pltpu.CompilerParams(vmem_limit_bytes=VMEM),
        cost_estimate=pl.CostEstimate(flops=2_000_000_000, bytes_accessed=5 << 20, transcendentals=0),
        name="outer_part",
    )(*args)


def down_kernel(tok, lat, out):
    for c in range(tok.shape[1] // CHUNK):
        full = dot(tok[:, c * CHUNK : (c + 1) * CHUNK], lat[...], 0, 0)
        half = CHUNK // 2
        out[c] = jnp.concatenate([full[:half], full[half:]], axis=1).astype(BF16)


def run_down(tokens, latent_grad):
    rows, width = tokens.shape
    rank = latent_grad.shape[1]
    wide = 1024
    return pl.pallas_call(
        down_kernel,
        grid=(width // wide,),
        in_specs=[pl.BlockSpec((rows, wide), lambda i: (0, i)), pl.BlockSpec((rows, rank), lambda i: (0, 0))],
        out_specs=pl.BlockSpec((wide // CHUNK, CHUNK // 2, 2 * rank), lambda i: (i, 0, 0)),
        out_shape=jax.ShapeDtypeStruct((width // CHUNK, CHUNK // 2, 2 * rank), BF16),
        cost_estimate=pl.CostEstimate(flops=300_000_000, bytes_accessed=2 << 20, transcendentals=0),
        name="down_part",
    )(tokens, latent_grad)


def final_kernel(low, high, r1, r2, r4, r8, diag, down, lat, out):
    mask = block_mask()
    slope = pick_half(low, high)
    for c in range(STEP // CHUNK):
        cs = slice(c * CHUNK, (c + 1) * CHUNK)
        total = dot(slope[:, cs], spread(diag[:, cs], mask), 1, 1)
        total = total + dot(lat[...], down[cs, :], 1, 1)
        for ref in (r1, r2, r4, r8):
            total = total + ref[:, cs].astype(F32)
        out[:, cs] = total.astype(BF16)


def run_final(slopes, received, diag, low_down, latent_grad):
    rows, width = received[0].shape
    rank = latent_grad.shape[1]
    steps = width // STEP
    col = lambda r: pl.BlockSpec((r, STEP), lambda i: (0, i))
    return pl.pallas_call(
        final_kernel,
        grid=(steps,),
        in_specs=half_specs(rows, steps)
        + [col(rows)] * 4
        + [
            col(BLOCK),
            pl.BlockSpec((STEP, rank), lambda i: (i, 0)),
            pl.BlockSpec((rows, rank), lambda i: (0, 0)),
        ],
        out_specs=col(rows),
        out_shape=jax.ShapeDtypeStruct((rows, width), BF16),
        compiler_params=pltpu.CompilerParams(vmem_limit_bytes=VMEM),
        cost_estimate=pl.CostEstimate(flops=2_000_000_000, bytes_accessed=9 << 20, transcendentals=0),
        name="token_grad",
    )(*slopes, *received, diag, low_down, latent_grad)


def flip(value, mask):
    return lax.ppermute(value, "tensor", [(i, i ^ mask) for i in range(16)])


def after(value, *events):
    return lax.optimization_barrier((value, *events))[0]


def ring_sum(grads):
    ring, sides, rows, width = grads.shape
    groups = [[x * RING + z for z in range(RING)] for x in range(2)]
    total = lax.psum_scatter(
        grads.reshape(ring * sides * rows, width), "dp", scatter_dimension=0, axis_index_groups=groups, tiled=True
    )
    return total.reshape(sides, rows, width)


def pair_sum(low, high, x):
    mine = jnp.where(x == 0, low, high).astype(F32)
    other = jnp.where(x == 0, high, low)
    return mine + lax.ppermute(other, "dp", [(i, i ^ RING) for i in range(2 * RING)]).astype(F32)


def per_device(tokens, cotangent, diag_factor, section_factors, low_down, low_up):
    rows, width = tokens.shape
    rank = low_up.shape[0]
    scale = (rows * lax.axis_size("dp")) ** -0.5
    x = lax.axis_index("dp") // RING
    half = width // 2

    m4_0 = flip(tokens[:, :half], 4)
    m1 = flip(tokens, 1)
    part = jnp.dot(tokens, low_down, preferred_element_type=F32)
    part = part + flip(part, 1)
    h1 = after(tokens, part)[:, half:]
    part = part + flip(part, 2)
    m2_0 = flip(after(tokens, part)[:, :half], 2)
    part = part + flip(part, 4)
    m8_0 = flip(after(m4_0, part), 12)
    m4_1 = flip(after(h1, m4_0, part), 4)
    arrived = flip(part, 12)
    m2_1 = flip(after(h1, m2_0), 2)
    m8_1 = flip(m4_1, 12)
    part = part + after(arrived, m2_0, m4_1)
    latent = part.astype(BF16)

    moved0 = (m1, m2_0, m4_0, m8_0)
    slope0, lat0 = run_slope(0, tokens, moved0, cotangent, diag_factor, section_factors, latent, low_up)
    grads = run_outer(0, slope0, tokens, moved0, latent, None)
    moved1 = (m1, m2_1, m4_1, after(m8_1, grads))
    slope1, lat1 = run_slope(1, tokens, moved1, cotangent, diag_factor, section_factors, latent, low_up)
    part = lat0 + lat1
    arrived = flip(part, 4)
    grads = run_outer(1, slope1, tokens, moved1, latent, grads)
    summed = ring_sum(grads)
    part = part + after(arrived, grads)
    arrived = flip(part, 12)
    slopes = (slope0, after(slope1, part))
    back = run_back(slopes, section_factors)
    part = part + after(arrived, back[0])
    sent = after(back[2], part)
    r4, r8, r1 = flip(sent, 4), flip(after(back[3], part), 8), flip(after(back[0], part), 1)
    part = part + flip(part, 2)
    r2 = flip(after(back[1], part), 2)
    part = part + flip(part, 1)
    latent_grad = part.astype(BF16)
    down = run_down(tokens, latent_grad)
    down_all = lax.all_to_all(down, "dp", 0, 0, tiled=True)
    down_sum = jnp.sum(down_all.astype(F32), axis=0) * scale
    down_grad = jnp.concatenate([down_sum[:, :rank], down_sum[:, rank:]], axis=0)
    token_grad = run_final((slope0, slope1), (r1, r2, r4, r8), diag_factor, low_down, latent_grad)
    grads = pair_sum(summed[0], summed[1], x) * scale
    return (
        token_grad,
        grads[:BLOCK],
        grads[BLOCK : 5 * BLOCK].reshape(4, BLOCK, CHUNK),
        down_grad,
        grads[5 * BLOCK :],
    )


def solution(mesh):
    placed = (
        P("dp", "tensor"),
        P("dp", "tensor"),
        P(None, "tensor"),
        P(None, None, "tensor"),
        P("tensor", None),
        P(None, "tensor"),
    )
    return jax.shard_map(
        per_device,
        mesh=mesh,
        in_specs=placed,
        out_specs=(
            P("dp", "tensor"),
            P(None, ("tensor", "dp")),
            P(None, None, ("tensor", "dp")),
            P(("tensor", "dp"), None),
            P(None, ("tensor", "dp")),
        ),
        check_vma=False,
    )
```

```python
import functools

import jax
import jax.numpy as jnp
from jax import lax
from jax.experimental import pallas as pl
from jax.experimental.pallas import tpu as pltpu
from jax.sharding import PartitionSpec as P

BLOCK = 64
CHUNK = 256
MAIN_STEP, BACK_STEP, FINAL_STEP = 512, 1024, 2048
RING = 8
VMEM = 60 << 20
F32 = jnp.float32
BF16 = jnp.bfloat16


def dot(a, b, ca, cb):
    return lax.dot_general(a, b, (((ca,), (cb,)), ((), ())), preferred_element_type=F32)


def gelu_slope(values):
    return (
        0.5 * (1.0 + lax.erf(values * 0.7071067811865476))
        + values * jnp.exp(-0.5 * values * values) * 0.3989422804014327
    )


def block_mask():
    row = lax.broadcasted_iota(jnp.int32, (CHUNK, CHUNK), 0) // BLOCK
    col = lax.broadcasted_iota(jnp.int32, (CHUNK, CHUNK), 1) // BLOCK
    return row == col


def spread(factor, mask):
    tall = jnp.concatenate([factor] * (CHUNK // BLOCK), axis=0)
    return jnp.where(mask, tall, jnp.zeros_like(tall))


def main_kernel(tok, m1, m2, m4, m8, cot, diag, sec, latent, up, *refs):
    slope_out, lat_out, grads = refs[-3:]
    mask = block_mask()
    lat = latent[...]
    group = CHUNK // BLOCK
    lat_sum = jnp.zeros((lat.shape[0], up.shape[0]), F32)
    for c in range(MAIN_STEP // CHUNK):
        cs = slice(c * CHUNK, (c + 1) * CHUNK)
        up_c = up[:, cs]
        sides = [tok[:, cs], m1[:, cs], m2[:, cs], m4[:, cs], m8[:, cs]]
        factors = [spread(diag[:, cs], mask)] + [spread(sec[b, :, cs], mask) for b in range(4)]
        left = jnp.concatenate(sides + [lat], axis=1)
        right = jnp.concatenate(factors + [up_c], axis=0)
        pre = dot(left, right, 1, 0)
        slope = (cot[:, cs].astype(F32) * gelu_slope(pre)).astype(BF16)
        slope_out[:, cs] = slope
        lat_sum = lat_sum + dot(slope, up_c, 1, 1)
        for k, side in enumerate(sides):
            full = dot(side, slope, 0, 0)
            kept = jnp.where(mask, full, jnp.zeros_like(full))
            part = sum(kept[i * BLOCK : (i + 1) * BLOCK] for i in range(group))
            grads[c, 0, k * BLOCK : (k + 1) * BLOCK, :] = part.astype(BF16)
        grads[c, 0, 5 * BLOCK :, :] = dot(lat, slope, 0, 0).astype(BF16)

    @pl.when(pl.program_id(0) == 0)
    def _():
        lat_out[...] = lat_sum

    @pl.when(pl.program_id(0) > 0)
    def _():
        lat_out[...] += lat_sum


def run_main(part, tokens, moved, cotangent, diag, section, latent, up, held):
    rows, width = moved[2].shape
    rank = up.shape[0]
    steps = width // MAIN_STEP
    base = part * steps
    whole = lambda r: pl.BlockSpec((r, MAIN_STEP), lambda i: (0, base + i))
    local = pl.BlockSpec((rows, MAIN_STEP), lambda i: (0, i))
    square = pl.BlockSpec((rows, rank), lambda i: (0, 0))
    section_spec = pl.BlockSpec((4, BLOCK, MAIN_STEP), lambda i: (0, 0, base + i))
    grad_rows = 5 * BLOCK + rank
    in_specs = [whole(rows), whole(rows), local, local, local, whole(rows), whole(BLOCK), section_spec, square, whole(rank)]
    args = [tokens, *moved, cotangent, diag, section, latent, up]
    if held is not None:
        in_specs.append(pl.BlockSpec(memory_space=pl.ANY))
        args.append(held)
    return pl.pallas_call(
        main_kernel,
        grid=(steps,),
        in_specs=in_specs,
        out_specs=[local, square, pl.BlockSpec((MAIN_STEP // CHUNK, 1, grad_rows, CHUNK), lambda i: (i, part, 0, 0))],
        out_shape=[
            jax.ShapeDtypeStruct((rows, width), BF16),
            jax.ShapeDtypeStruct((rows, rank), F32),
            jax.ShapeDtypeStruct((RING, 2, grad_rows, CHUNK), BF16),
        ],
        input_output_aliases={} if held is None else {10: 2},
        compiler_params=pltpu.CompilerParams(vmem_limit_bytes=VMEM),
        cost_estimate=pl.CostEstimate(flops=2_000_000_000, bytes_accessed=28 << 20, transcendentals=0),
        name="main_part",
    )(*args)


def pick_half(low, high):
    first = pl.program_id(0) < pl.num_programs(0) // 2
    return jnp.where(first, low[...], high[...])


def half_specs(rows, steps):
    half = steps // 2
    return [
        pl.BlockSpec((rows, FINAL_STEP), lambda i: (0, jnp.minimum(i, half - 1))),
        pl.BlockSpec((rows, FINAL_STEP), lambda i: (0, jnp.maximum(i - half, 0))),
    ]


def back_kernel(slope, sec, b1, b2, b4, b8):
    mask = block_mask()
    for c in range(slope.shape[1] // CHUNK):
        cs = slice(c * CHUNK, (c + 1) * CHUNK)
        for b, ref in enumerate((b1, b2, b4, b8)):
            ref[:, cs] = dot(slope[:, cs], spread(sec[b, :, cs], mask), 1, 1).astype(BF16)


def run_back(part, slope, section):
    rows, width = slope.shape
    steps = width // BACK_STEP
    base = part * steps
    local = pl.BlockSpec((rows, BACK_STEP), lambda i: (0, i))
    return pl.pallas_call(
        back_kernel,
        grid=(steps,),
        in_specs=[local, pl.BlockSpec((4, BLOCK, BACK_STEP), lambda i: (0, 0, base + i))],
        out_specs=[local] * 4,
        out_shape=[jax.ShapeDtypeStruct((rows, width), BF16)] * 4,
        compiler_params=pltpu.CompilerParams(vmem_limit_bytes=VMEM),
        cost_estimate=pl.CostEstimate(flops=1_000_000_000, bytes_accessed=13 << 20, transcendentals=0),
        name="back_products",
    )(slope, section)


def down_kernel(tok, lat, out):
    for c in range(tok.shape[1] // CHUNK):
        out[0, c] = dot(lat[...], tok[:, c * CHUNK : (c + 1) * CHUNK], 0, 0).astype(BF16)


def run_down(tokens, latent_grad):
    rows, width = tokens.shape
    rank = latent_grad.shape[1]
    half = width // 2
    return pl.pallas_call(
        down_kernel,
        grid=(2,),
        in_specs=[pl.BlockSpec((rows, half), lambda i: (0, i)), pl.BlockSpec((rows, rank), lambda i: (0, 0))],
        out_specs=pl.BlockSpec((1, RING, rank, CHUNK), lambda i: (i, 0, 0, 0)),
        out_shape=jax.ShapeDtypeStruct((2, RING, rank, CHUNK), BF16),
        cost_estimate=pl.CostEstimate(flops=300_000_000, bytes_accessed=10 << 20, transcendentals=0),
        name="down_part",
    )(tokens, latent_grad)


def final_kernel(*refs):
    pairs, (diag, down, lat, out) = refs[:8], refs[8:]
    mask = block_mask()
    slope, r1, r2, r48 = (pick_half(pairs[2 * k], pairs[2 * k + 1]) for k in range(4))
    for c in range(FINAL_STEP // CHUNK):
        cs = slice(c * CHUNK, (c + 1) * CHUNK)
        total = dot(slope[:, cs], spread(diag[:, cs], mask), 1, 1)
        total = total + dot(lat[...], down[cs, :], 1, 1)
        for value in (r1, r2, r48):
            total = total + value[:, cs].astype(F32)
        out[:, cs] = total.astype(BF16)


def run_final(pairs, diag, low_down, latent_grad):
    rows, half_width = pairs[0][0].shape
    width = 2 * half_width
    rank = latent_grad.shape[1]
    steps = width // FINAL_STEP
    col = lambda r: pl.BlockSpec((r, FINAL_STEP), lambda i: (0, i))
    return pl.pallas_call(
        final_kernel,
        grid=(steps,),
        in_specs=half_specs(rows, steps) * 4
        + [
            col(BLOCK),
            pl.BlockSpec((FINAL_STEP, rank), lambda i: (i, 0)),
            pl.BlockSpec((rows, rank), lambda i: (0, 0)),
        ],
        out_specs=col(rows),
        out_shape=jax.ShapeDtypeStruct((rows, width), BF16),
        compiler_params=pltpu.CompilerParams(vmem_limit_bytes=VMEM),
        cost_estimate=pl.CostEstimate(flops=2_000_000_000, bytes_accessed=17 << 20, transcendentals=0),
        name="token_grad",
    )(*[value for pair in pairs for value in pair], diag, low_down, latent_grad)


def finish_kernel(scale, side, summed, arrived, diag, section, up):
    total = (summed[0].astype(F32) + arrived[...].astype(F32)) * scale
    diag[...] = total[:BLOCK]
    for b in range(4):
        section[b] = total[(b + 1) * BLOCK : (b + 2) * BLOCK]
    up[...] = total[5 * BLOCK :]


def run_finish(x, summed, arrived, scale):
    _, rows, width = summed.shape
    rank = rows - 5 * BLOCK
    return pl.pallas_call(
        functools.partial(finish_kernel, scale),
        grid_spec=pltpu.PrefetchScalarGridSpec(
            num_scalar_prefetch=1,
            grid=(1,),
            in_specs=[
                pl.BlockSpec((1, rows, width), lambda i, side: (side[0], 0, 0)),
                pl.BlockSpec((rows, width), lambda i, side: (0, 0)),
            ],
            out_specs=[
                pl.BlockSpec((BLOCK, width), lambda i, side: (0, 0)),
                pl.BlockSpec((4, BLOCK, width), lambda i, side: (0, 0, 0)),
                pl.BlockSpec((rank, width), lambda i, side: (0, 0)),
            ],
        ),
        out_shape=[
            jax.ShapeDtypeStruct((BLOCK, width), F32),
            jax.ShapeDtypeStruct((4, BLOCK, width), F32),
            jax.ShapeDtypeStruct((rank, width), F32),
        ],
        cost_estimate=pl.CostEstimate(flops=300_000, bytes_accessed=4 << 20, transcendentals=0),
        name="finish",
    )(jnp.full((1,), x, jnp.int32), summed, arrived)


def flip(value, mask):
    return lax.ppermute(value, "tensor", [(i, i ^ mask) for i in range(16)])


def after(value, *events):
    return lax.optimization_barrier((value, *events))[0]


def ring_sum(grads):
    ring, sides, rows, width = grads.shape
    groups = [[x * RING + z for z in range(RING)] for x in range(2)]
    total = lax.psum_scatter(
        grads.reshape(ring * sides * rows, width), "dp", scatter_dimension=0, axis_index_groups=groups, tiled=True
    )
    return total.reshape(sides, rows, width)


def cross(value):
    return lax.ppermute(value, "dp", [(i, i ^ RING) for i in range(2 * RING)])


def per_device(tokens, cotangent, diag_factor, section_factors, low_down, low_up):
    rows, width = tokens.shape
    scale = (rows * lax.axis_size("dp")) ** -0.5
    x = lax.axis_index("dp") // RING
    half = width // 2

    h0 = tokens[:, :half]
    m4_0 = flip(h0, 4)
    m2_0 = flip(h0, 2)
    m1 = flip(tokens, 1)
    part = jnp.dot(tokens, low_down, preferred_element_type=F32)
    part = part + flip(part, 12)
    h1 = after(tokens, part)[:, half:]
    part = part + flip(part, 1)
    part = part + flip(part, 2)
    m4_1 = flip(after(h1, m4_0), 4)
    m8_0 = flip(m4_0, 12)
    m2_1 = flip(after(h1, m2_0), 2)
    part = part + flip(part, 4)
    m8_1 = flip(m4_1, 12)
    latent = part.astype(BF16)

    factors = (cotangent, diag_factor, section_factors, latent, low_up)
    slope0, lat0, grads = run_main(0, tokens, (m1, m2_0, m4_0, m8_0), *factors, None)
    b1_0, b2_0, b4_0, b8_0 = run_back(0, slope0, section_factors)
    moved1 = (m1, m2_1, m4_1, after(m8_1, b8_0))
    slope1, lat1, grads = run_main(1, tokens, moved1, *factors, grads)
    summed = ring_sum(grads)

    part = lat0 + lat1
    arrived = flip(part, 4)
    b1_1, b2_1, b4_1, b8_1 = run_back(1, slope1, section_factors)
    part = part + after(arrived, b8_1)
    part = part + flip(part, 12)
    q0, q1 = flip(after(b8_0, part), 12), flip(after(b8_1, part), 12)
    part = part + flip(part, 2)
    r2_0, r1_0 = flip(after(b2_0, part), 2), flip(after(b1_0, part), 1)
    part = part + flip(part, 1)
    latent_grad = part.astype(BF16)

    down = run_down(after(tokens, q0), latent_grad)
    keep = lax.dynamic_index_in_dim(down, x, 0, keepdims=False)
    send = lax.dynamic_index_in_dim(down, 1 - x, 0, keepdims=False)
    s0 = flip(b4_0 + q0, 4)
    pair = (keep.astype(F32) + after(cross(after(send, r2_0, r1_0)), q1).astype(F32)).astype(BF16)
    r2_1, r1_1 = flip(after(b2_1, pair), 2), flip(after(b1_1, pair), 1)
    groups = [[side * RING + z for z in range(RING)] for side in range(2)]
    pair = lax.all_to_all(pair, "dp", 0, 0, axis_index_groups=groups, tiled=True)
    down_grad = (jnp.sum(pair.astype(F32), axis=0) * scale).T
    s1 = flip(b4_1 + q1, 4)
    pairs = ((slope0, slope1), (r1_0, r1_1), (r2_0, r2_1), (s0, s1))
    token_grad = run_final(pairs, diag_factor, low_down, latent_grad)
    arrived = cross(lax.dynamic_index_in_dim(summed, 1 - x, 0, keepdims=False))
    diag_grad, section_grad, up_grad = run_finish(x, summed, arrived, scale)
    return token_grad, diag_grad, section_grad, down_grad, up_grad


def solution(mesh):
    placed = (
        P("dp", "tensor"),
        P("dp", "tensor"),
        P(None, "tensor"),
        P(None, None, "tensor"),
        P("tensor", None),
        P(None, "tensor"),
    )
    return jax.shard_map(
        per_device,
        mesh=mesh,
        in_specs=placed,
        out_specs=(
            P("dp", "tensor"),
            P(None, ("tensor", "dp")),
            P(None, None, ("tensor", "dp")),
            P(("tensor", "dp"), None),
            P(None, ("tensor", "dp")),
        ),
        check_vma=False,
    )
```

```python
import functools

import jax
import jax.numpy as jnp
from jax import lax
from jax.experimental import pallas as pl
from jax.experimental.pallas import tpu as pltpu
from jax.sharding import PartitionSpec as P

BLOCK = 64
CHUNK = 256
MAIN_STEP, BACK_STEP, FINAL_STEP = 512, 1024, 2048
RING = 8
VMEM = 60 << 20
F32 = jnp.float32
BF16 = jnp.bfloat16


def dot(a, b, ca, cb):
    return lax.dot_general(a, b, (((ca,), (cb,)), ((), ())), preferred_element_type=F32)


def gelu_slope(values):
    return (
        0.5 * (1.0 + lax.erf(values * 0.7071067811865476))
        + values * jnp.exp(-0.5 * values * values) * 0.3989422804014327
    )


def block_mask():
    row = lax.broadcasted_iota(jnp.int32, (CHUNK, CHUNK), 0) // BLOCK
    col = lax.broadcasted_iota(jnp.int32, (CHUNK, CHUNK), 1) // BLOCK
    return row == col


def spread(factor, mask):
    tall = jnp.concatenate([factor] * (CHUNK // BLOCK), axis=0)
    return jnp.where(mask, tall, jnp.zeros_like(tall))


def main_kernel(tok, m1, m2, m4, m8, cot, diag, sec, latent, up, *refs):
    slope_out, lat_out, grads = refs[-3:]
    mask = block_mask()
    lat = latent[...]
    group = CHUNK // BLOCK
    lat_sum = jnp.zeros((lat.shape[0], up.shape[0]), F32)
    for c in range(MAIN_STEP // CHUNK):
        cs = slice(c * CHUNK, (c + 1) * CHUNK)
        up_c = up[:, cs]
        sides = [tok[:, cs], m1[:, cs], m2[:, cs], m4[:, cs], m8[:, cs]]
        factors = [spread(diag[:, cs], mask)] + [spread(sec[b, :, cs], mask) for b in range(4)]
        left = jnp.concatenate(sides + [lat], axis=1)
        right = jnp.concatenate(factors + [up_c], axis=0)
        pre = dot(left, right, 1, 0)
        slope = (cot[:, cs].astype(F32) * gelu_slope(pre)).astype(BF16)
        slope_out[:, cs] = slope
        lat_sum = lat_sum + dot(slope, up_c, 1, 1)
        for k, side in enumerate(sides):
            full = dot(side, slope, 0, 0)
            kept = jnp.where(mask, full, jnp.zeros_like(full))
            part = sum(kept[i * BLOCK : (i + 1) * BLOCK] for i in range(group))
            grads[c, 0, k * BLOCK : (k + 1) * BLOCK, :] = part.astype(BF16)
        grads[c, 0, 5 * BLOCK :, :] = dot(lat, slope, 0, 0).astype(BF16)

    @pl.when(pl.program_id(0) == 0)
    def _():
        lat_out[...] = lat_sum

    @pl.when(pl.program_id(0) > 0)
    def _():
        lat_out[...] += lat_sum


def run_main(part, tokens, moved, cotangent, diag, section, latent, up, held):
    rows, width = moved[2].shape
    rank = up.shape[0]
    steps = width // MAIN_STEP
    base = part * steps
    whole = lambda r: pl.BlockSpec((r, MAIN_STEP), lambda i: (0, base + i))
    local = pl.BlockSpec((rows, MAIN_STEP), lambda i: (0, i))
    square = pl.BlockSpec((rows, rank), lambda i: (0, 0))
    section_spec = pl.BlockSpec((4, BLOCK, MAIN_STEP), lambda i: (0, 0, base + i))
    grad_rows = 5 * BLOCK + rank
    in_specs = [whole(rows), whole(rows), local, local, local, whole(rows), whole(BLOCK), section_spec, square, whole(rank)]
    args = [tokens, *moved, cotangent, diag, section, latent, up]
    if held is not None:
        in_specs.append(pl.BlockSpec(memory_space=pl.ANY))
        args.append(held)
    return pl.pallas_call(
        main_kernel,
        grid=(steps,),
        in_specs=in_specs,
        out_specs=[local, square, pl.BlockSpec((MAIN_STEP // CHUNK, 1, grad_rows, CHUNK), lambda i: (i, part, 0, 0))],
        out_shape=[
            jax.ShapeDtypeStruct((rows, width), BF16),
            jax.ShapeDtypeStruct((rows, rank), F32),
            jax.ShapeDtypeStruct((RING, 2, grad_rows, CHUNK), BF16),
        ],
        input_output_aliases={} if held is None else {10: 2},
        compiler_params=pltpu.CompilerParams(vmem_limit_bytes=VMEM),
        cost_estimate=pl.CostEstimate(flops=2_000_000_000, bytes_accessed=28 << 20, transcendentals=0),
        name="main_part",
    )(*args)


def pick_half(low, high):
    first = pl.program_id(0) < pl.num_programs(0) // 2
    return jnp.where(first, low[...], high[...])


def half_specs(rows, steps):
    half = steps // 2
    return [
        pl.BlockSpec((rows, FINAL_STEP), lambda i: (0, jnp.minimum(i, half - 1))),
        pl.BlockSpec((rows, FINAL_STEP), lambda i: (0, jnp.maximum(i - half, 0))),
    ]


def back_kernel(slope, sec, b1, b2, b4, b8):
    mask = block_mask()
    for c in range(slope.shape[1] // CHUNK):
        cs = slice(c * CHUNK, (c + 1) * CHUNK)
        for b, ref in enumerate((b1, b2, b4, b8)):
            ref[:, cs] = dot(slope[:, cs], spread(sec[b, :, cs], mask), 1, 1).astype(BF16)


def run_back(part, slope, section):
    rows, width = slope.shape
    steps = width // BACK_STEP
    base = part * steps
    local = pl.BlockSpec((rows, BACK_STEP), lambda i: (0, i))
    return pl.pallas_call(
        back_kernel,
        grid=(steps,),
        in_specs=[local, pl.BlockSpec((4, BLOCK, BACK_STEP), lambda i: (0, 0, base + i))],
        out_specs=[local] * 4,
        out_shape=[jax.ShapeDtypeStruct((rows, width), BF16)] * 4,
        compiler_params=pltpu.CompilerParams(vmem_limit_bytes=VMEM),
        cost_estimate=pl.CostEstimate(flops=1_000_000_000, bytes_accessed=13 << 20, transcendentals=0),
        name="back_products",
    )(slope, section)


def down_kernel(side, tok, lat, keep, send):
    def fill(out):
        for c in range(tok.shape[1] // CHUNK):
            out[c] = dot(lat[...], tok[:, c * CHUNK : (c + 1) * CHUNK], 0, 0).astype(BF16)

    pl.when(pl.program_id(0) == 0)(lambda: fill(send))
    pl.when(pl.program_id(0) == 1)(lambda: fill(keep))


def run_down(x, tokens, latent_grad):
    rows, width = tokens.shape
    rank = latent_grad.shape[1]
    half = width // 2
    block = pl.BlockSpec((RING, rank, CHUNK), lambda i, side: (0, 0, 0))
    return pl.pallas_call(
        down_kernel,
        grid_spec=pltpu.PrefetchScalarGridSpec(
            num_scalar_prefetch=1,
            grid=(2,),
            in_specs=[
                pl.BlockSpec((rows, half), lambda i, side: (0, (1 + i + side[0]) % 2)),
                pl.BlockSpec((rows, rank), lambda i, side: (0, 0)),
            ],
            out_specs=[block, block],
        ),
        out_shape=[jax.ShapeDtypeStruct((RING, rank, CHUNK), BF16)] * 2,
        cost_estimate=pl.CostEstimate(flops=300_000_000, bytes_accessed=10 << 20, transcendentals=0),
        name="down_part",
    )(jnp.full((1,), x, jnp.int32), tokens, latent_grad)


def final_kernel(*refs):
    pairs, (diag, down, lat, out) = refs[:8], refs[8:]
    mask = block_mask()
    slope, r1, r2, r48 = (pick_half(pairs[2 * k], pairs[2 * k + 1]) for k in range(4))
    for c in range(FINAL_STEP // CHUNK):
        cs = slice(c * CHUNK, (c + 1) * CHUNK)
        total = dot(slope[:, cs], spread(diag[:, cs], mask), 1, 1)
        total = total + dot(lat[...], down[cs, :], 1, 1)
        for value in (r1, r2, r48):
            total = total + value[:, cs].astype(F32)
        out[:, cs] = total.astype(BF16)


def run_final(pairs, diag, low_down, latent_grad):
    rows, half_width = pairs[0][0].shape
    width = 2 * half_width
    rank = latent_grad.shape[1]
    steps = width // FINAL_STEP
    col = lambda r: pl.BlockSpec((r, FINAL_STEP), lambda i: (0, i))
    return pl.pallas_call(
        final_kernel,
        grid=(steps,),
        in_specs=half_specs(rows, steps) * 4
        + [
            col(BLOCK),
            pl.BlockSpec((FINAL_STEP, rank), lambda i: (i, 0)),
            pl.BlockSpec((rows, rank), lambda i: (0, 0)),
        ],
        out_specs=col(rows),
        out_shape=jax.ShapeDtypeStruct((rows, width), BF16),
        compiler_params=pltpu.CompilerParams(vmem_limit_bytes=VMEM),
        cost_estimate=pl.CostEstimate(flops=2_000_000_000, bytes_accessed=17 << 20, transcendentals=0),
        name="token_grad",
    )(*[value for pair in pairs for value in pair], diag, low_down, latent_grad)


def finish_kernel(scale, side, summed, arrived, diag, section, up):
    total = (summed[0].astype(F32) + arrived[...].astype(F32)) * scale
    diag[...] = total[:BLOCK]
    for b in range(4):
        section[b] = total[(b + 1) * BLOCK : (b + 2) * BLOCK]
    up[...] = total[5 * BLOCK :]


def run_finish(x, summed, arrived, scale):
    _, rows, width = summed.shape
    rank = rows - 5 * BLOCK
    return pl.pallas_call(
        functools.partial(finish_kernel, scale),
        grid_spec=pltpu.PrefetchScalarGridSpec(
            num_scalar_prefetch=1,
            grid=(1,),
            in_specs=[
                pl.BlockSpec((1, rows, width), lambda i, side: (side[0], 0, 0)),
                pl.BlockSpec((rows, width), lambda i, side: (0, 0)),
            ],
            out_specs=[
                pl.BlockSpec((BLOCK, width), lambda i, side: (0, 0)),
                pl.BlockSpec((4, BLOCK, width), lambda i, side: (0, 0, 0)),
                pl.BlockSpec((rank, width), lambda i, side: (0, 0)),
            ],
        ),
        out_shape=[
            jax.ShapeDtypeStruct((BLOCK, width), F32),
            jax.ShapeDtypeStruct((4, BLOCK, width), F32),
            jax.ShapeDtypeStruct((rank, width), F32),
        ],
        cost_estimate=pl.CostEstimate(flops=300_000, bytes_accessed=4 << 20, transcendentals=0),
        name="finish",
    )(jnp.full((1,), x, jnp.int32), summed, arrived)


def flip(value, mask):
    return lax.ppermute(value, "tensor", [(i, i ^ mask) for i in range(16)])


def after(value, *events):
    return lax.optimization_barrier((value, *events))[0]


def ring_sum(grads):
    ring, sides, rows, width = grads.shape
    groups = [[x * RING + z for z in range(RING)] for x in range(2)]
    total = lax.psum_scatter(
        grads.reshape(ring * sides * rows, width), "dp", scatter_dimension=0, axis_index_groups=groups, tiled=True
    )
    return total.reshape(sides, rows, width)


def cross(value):
    return lax.ppermute(value, "dp", [(i, i ^ RING) for i in range(2 * RING)])


def per_device(tokens, cotangent, diag_factor, section_factors, low_down, low_up):
    rows, width = tokens.shape
    scale = (rows * lax.axis_size("dp")) ** -0.5
    x = lax.axis_index("dp") // RING
    half = width // 2

    h0 = tokens[:, :half]
    m4_0 = flip(h0, 4)
    m1 = flip(tokens, 1)
    part = jnp.dot(tokens, low_down, preferred_element_type=F32)
    part = part + flip(part, 12)
    part = part + flip(part, 1)
    h1 = after(tokens, part)[:, half:]
    m4_1 = flip(after(h1, m4_0, part), 4)
    m8_0 = flip(after(m4_0, part), 12)
    part = part + flip(part, 2)
    m2_0 = flip(after(h0, part), 2)
    part = part + flip(part, 4)
    m8_1 = flip(m4_1, 12)
    m2_1 = flip(after(h1, m2_0), 2)
    latent = part.astype(BF16)

    factors = (cotangent, diag_factor, section_factors, latent, low_up)
    slope0, lat0, grads = run_main(0, tokens, (m1, m2_0, m4_0, m8_0), *factors, None)
    b1_0, b2_0, b4_0, b8_0 = run_back(0, slope0, section_factors)
    moved1 = (m1, m2_1, m4_1, after(m8_1, b8_0))
    slope1, lat1, grads = run_main(1, tokens, moved1, *factors, grads)
    summed = ring_sum(grads)

    part = lat0 + lat1
    arrived = flip(part, 2)
    b1_1, b2_1, b4_1, b8_1 = run_back(1, slope1, section_factors)
    part = part + after(arrived, b8_1)
    r2_0, r1_0 = flip(after(b2_0, part), 2), flip(after(b1_0, part), 1)
    part = part + flip(part, 4)
    part = part + flip(part, 12)
    q0, q1 = flip(after(b8_0, part), 12), flip(after(b8_1, part), 12)
    part = part + after(flip(part, 1), r2_0, r1_0)
    latent_grad = part.astype(BF16)

    keep, send = run_down(x, tokens, latent_grad)
    pair = (keep.astype(F32) + after(cross(send), q0, q1).astype(F32)).astype(BF16)
    s0 = flip(b4_0 + q0, 4)
    r2_1, r1_1 = flip(after(b2_1, pair), 2), flip(after(b1_1, pair), 1)
    groups = [[side * RING + z for z in range(RING)] for side in range(2)]
    pair = lax.all_to_all(pair, "dp", 0, 0, axis_index_groups=groups, tiled=True)
    down_grad = (jnp.sum(pair.astype(F32), axis=0) * scale).T
    s1 = flip(b4_1 + q1, 4)
    pairs = ((slope0, slope1), (r1_0, r1_1), (r2_0, r2_1), (s0, s1))
    token_grad = run_final(pairs, diag_factor, low_down, latent_grad)
    arrived = cross(lax.dynamic_index_in_dim(summed, 1 - x, 0, keepdims=False))
    diag_grad, section_grad, up_grad = run_finish(x, summed, arrived, scale)
    return token_grad, diag_grad, section_grad, down_grad, up_grad


def solution(mesh):
    placed = (
        P("dp", "tensor"),
        P("dp", "tensor"),
        P(None, "tensor"),
        P(None, None, "tensor"),
        P("tensor", None),
        P(None, "tensor"),
    )
    return jax.shard_map(
        per_device,
        mesh=mesh,
        in_specs=placed,
        out_specs=(
            P("dp", "tensor"),
            P(None, ("tensor", "dp")),
            P(None, None, ("tensor", "dp")),
            P(("tensor", "dp"), None),
            P(None, ("tensor", "dp")),
        ),
        check_vma=False,
    )
```

```python
import functools

import jax
import jax.numpy as jnp
from jax import lax
from jax.experimental import pallas as pl
from jax.experimental.pallas import tpu as pltpu
from jax.sharding import PartitionSpec as P

BLOCK = 64
CHUNK = 256
MAIN_STEP, FINAL_STEP = 512, 2048
RING = 8
VMEM = 62 << 20
F32 = jnp.float32
BF16 = jnp.bfloat16


def dot(a, b, ca, cb):
    return lax.dot_general(a, b, (((ca,), (cb,)), ((), ())), preferred_element_type=F32)


def gelu_slope(values):
    return (
        0.5 * (1.0 + lax.erf(values * 0.7071067811865476))
        + values * jnp.exp(-0.5 * values * values) * 0.3989422804014327
    )


def block_mask():
    row = lax.broadcasted_iota(jnp.int32, (CHUNK, CHUNK), 0) // BLOCK
    col = lax.broadcasted_iota(jnp.int32, (CHUNK, CHUNK), 1) // BLOCK
    return row == col


def spread(factor, mask):
    tall = jnp.concatenate([factor] * (CHUNK // BLOCK), axis=0)
    return jnp.where(mask, tall, jnp.zeros_like(tall))


def main_kernel(tok, m1, m2, m4, m8, cot, diag, sec, latent, up, *refs):
    slope_out, lat_out, grads = refs[-3:]
    mask = block_mask()
    lat = latent[...]
    group = CHUNK // BLOCK
    lat_sum = jnp.zeros((lat.shape[0], up.shape[0]), F32)
    for c in range(MAIN_STEP // CHUNK):
        cs = slice(c * CHUNK, (c + 1) * CHUNK)
        up_c = up[:, cs]
        sides = [tok[:, cs], m1[:, cs], m2[:, cs], m4[:, cs], m8[:, cs]]
        factors = [spread(diag[:, cs], mask)] + [spread(sec[b, :, cs], mask) for b in range(4)]
        left = jnp.concatenate(sides + [lat], axis=1)
        right = jnp.concatenate(factors + [up_c], axis=0)
        pre = dot(left, right, 1, 0)
        slope = (cot[:, cs].astype(F32) * gelu_slope(pre)).astype(BF16)
        slope_out[:, cs] = slope
        lat_sum = lat_sum + dot(slope, up_c, 1, 1)
        for k, side in enumerate(sides):
            full = dot(side, slope, 0, 0)
            kept = jnp.where(mask, full, jnp.zeros_like(full))
            part = sum(kept[i * BLOCK : (i + 1) * BLOCK] for i in range(group))
            grads[c, 0, k * BLOCK : (k + 1) * BLOCK, :] = part.astype(BF16)
        grads[c, 0, 5 * BLOCK :, :] = dot(lat, slope, 0, 0).astype(BF16)

    @pl.when(pl.program_id(0) == 0)
    def _():
        lat_out[...] = lat_sum

    @pl.when(pl.program_id(0) > 0)
    def _():
        lat_out[...] += lat_sum


def run_main(part, tokens, moved, cotangent, diag, section, latent, up, held):
    rows, width = moved[2].shape
    rank = up.shape[0]
    steps = width // MAIN_STEP
    base = part * steps
    whole = lambda r: pl.BlockSpec((r, MAIN_STEP), lambda i: (0, base + i))
    local = pl.BlockSpec((rows, MAIN_STEP), lambda i: (0, i))
    square = pl.BlockSpec((rows, rank), lambda i: (0, 0))
    section_spec = pl.BlockSpec((4, BLOCK, MAIN_STEP), lambda i: (0, 0, base + i))
    grad_rows = 5 * BLOCK + rank
    in_specs = [whole(rows), whole(rows), local, local, local, whole(rows), whole(BLOCK), section_spec, square, whole(rank)]
    args = [tokens, *moved, cotangent, diag, section, latent, up]
    if held is not None:
        in_specs.append(pl.BlockSpec(memory_space=pl.ANY))
        args.append(held)
    return pl.pallas_call(
        main_kernel,
        grid=(steps,),
        in_specs=in_specs,
        out_specs=[local, square, pl.BlockSpec((MAIN_STEP // CHUNK, 1, grad_rows, CHUNK), lambda i: (i, part, 0, 0))],
        out_shape=[
            jax.ShapeDtypeStruct((rows, width), BF16),
            jax.ShapeDtypeStruct((rows, rank), F32),
            jax.ShapeDtypeStruct((RING, 2, grad_rows, CHUNK), BF16),
        ],
        input_output_aliases={} if held is None else {10: 2},
        compiler_params=pltpu.CompilerParams(vmem_limit_bytes=VMEM),
        cost_estimate=pl.CostEstimate(flops=2_000_000_000, bytes_accessed=28 << 20, transcendentals=0),
        name="main_part",
    )(*args)


def pick_half(low, high):
    first = pl.program_id(0) < pl.num_programs(0) // 2
    return jnp.where(first, low[...], high[...])


def half_specs(rows, steps):
    half = steps // 2
    return [
        pl.BlockSpec((rows, FINAL_STEP), lambda i: (0, jnp.minimum(i, half - 1))),
        pl.BlockSpec((rows, FINAL_STEP), lambda i: (0, jnp.maximum(i - half, 0))),
    ]


def back_kernel(low, high, sec, b1, *halves):
    mask = block_mask()

    def fill(slope, outs):
        for c in range(slope.shape[1] // CHUNK):
            cs = slice(c * CHUNK, (c + 1) * CHUNK)
            for b, out in enumerate(outs):
                out[:, cs] = dot(slope[:, cs], spread(sec[b, :, cs], mask), 1, 1).astype(BF16)

    pl.when(pl.program_id(0) == 0)(lambda: fill(low, (b1, *halves[0::2])))
    pl.when(pl.program_id(0) == 1)(lambda: fill(high, (b1, *halves[1::2])))


def run_back(slopes, section):
    rows, half = slopes[0].shape
    fixed = pl.BlockSpec((rows, half), lambda i: (0, 0))
    moving = pl.BlockSpec((rows, half), lambda i: (0, i))
    return pl.pallas_call(
        back_kernel,
        grid=(2,),
        in_specs=[fixed, fixed, pl.BlockSpec((4, BLOCK, half), lambda i: (0, 0, i))],
        out_specs=[moving] + [fixed] * 6,
        out_shape=[jax.ShapeDtypeStruct((rows, 2 * half), BF16)] + [jax.ShapeDtypeStruct((rows, half), BF16)] * 6,
        compiler_params=pltpu.CompilerParams(vmem_limit_bytes=VMEM),
        cost_estimate=pl.CostEstimate(flops=2_000_000_000, bytes_accessed=20 << 20, transcendentals=0),
        name="back_products",
    )(*slopes, section)


def down_kernel(side, tok, lat, keep, send):
    def fill(out):
        for c in range(tok.shape[1] // CHUNK):
            out[c] = dot(lat[...], tok[:, c * CHUNK : (c + 1) * CHUNK], 0, 0).astype(BF16)

    pl.when(pl.program_id(0) == 0)(lambda: fill(send))
    pl.when(pl.program_id(0) == 1)(lambda: fill(keep))


def run_down(x, tokens, latent_grad):
    rows, width = tokens.shape
    rank = latent_grad.shape[1]
    half = width // 2
    block = pl.BlockSpec((RING, rank, CHUNK), lambda i, side: (0, 0, 0))
    return pl.pallas_call(
        down_kernel,
        grid_spec=pltpu.PrefetchScalarGridSpec(
            num_scalar_prefetch=1,
            grid=(2,),
            in_specs=[
                pl.BlockSpec((rows, half), lambda i, side: (0, (1 + i + side[0]) % 2)),
                pl.BlockSpec((rows, rank), lambda i, side: (0, 0)),
            ],
            out_specs=[block, block],
        ),
        out_shape=[jax.ShapeDtypeStruct((RING, rank, CHUNK), BF16)] * 2,
        cost_estimate=pl.CostEstimate(flops=300_000_000, bytes_accessed=10 << 20, transcendentals=0),
        name="down_part",
    )(jnp.full((1,), x, jnp.int32), tokens, latent_grad)


def final_kernel(*refs):
    pairs, (r1, diag, down, lat, out) = refs[:6], refs[6:]
    mask = block_mask()
    slope, r2, r48 = (pick_half(pairs[2 * k], pairs[2 * k + 1]) for k in range(3))
    for c in range(FINAL_STEP // CHUNK):
        cs = slice(c * CHUNK, (c + 1) * CHUNK)
        total = dot(slope[:, cs], spread(diag[:, cs], mask), 1, 1)
        total = total + dot(lat[...], down[cs, :], 1, 1)
        for value in (r1, r2, r48):
            total = total + value[:, cs].astype(F32)
        out[:, cs] = total.astype(BF16)


def run_final(pairs, r1, diag, low_down, latent_grad):
    rows, half_width = pairs[0][0].shape
    width = 2 * half_width
    rank = latent_grad.shape[1]
    steps = width // FINAL_STEP
    col = lambda r: pl.BlockSpec((r, FINAL_STEP), lambda i: (0, i))
    return pl.pallas_call(
        final_kernel,
        grid=(steps,),
        in_specs=half_specs(rows, steps) * 3
        + [
            col(rows),
            col(BLOCK),
            pl.BlockSpec((FINAL_STEP, rank), lambda i: (i, 0)),
            pl.BlockSpec((rows, rank), lambda i: (0, 0)),
        ],
        out_specs=col(rows),
        out_shape=jax.ShapeDtypeStruct((rows, width), BF16),
        compiler_params=pltpu.CompilerParams(vmem_limit_bytes=VMEM),
        cost_estimate=pl.CostEstimate(flops=2_000_000_000, bytes_accessed=17 << 20, transcendentals=0),
        name="token_grad",
    )(*[value for pair in pairs for value in pair], r1, diag, low_down, latent_grad)


def finish_kernel(scale, side, summed, arrived, diag, section, up):
    total = (summed[0].astype(F32) + arrived[...].astype(F32)) * scale
    diag[...] = total[:BLOCK]
    for b in range(4):
        section[b] = total[(b + 1) * BLOCK : (b + 2) * BLOCK]
    up[...] = total[5 * BLOCK :]


def run_finish(x, summed, arrived, scale):
    _, rows, width = summed.shape
    rank = rows - 5 * BLOCK
    return pl.pallas_call(
        functools.partial(finish_kernel, scale),
        grid_spec=pltpu.PrefetchScalarGridSpec(
            num_scalar_prefetch=1,
            grid=(1,),
            in_specs=[
                pl.BlockSpec((1, rows, width), lambda i, side: (side[0], 0, 0)),
                pl.BlockSpec((rows, width), lambda i, side: (0, 0)),
            ],
            out_specs=[
                pl.BlockSpec((BLOCK, width), lambda i, side: (0, 0)),
                pl.BlockSpec((4, BLOCK, width), lambda i, side: (0, 0, 0)),
                pl.BlockSpec((rank, width), lambda i, side: (0, 0)),
            ],
        ),
        out_shape=[
            jax.ShapeDtypeStruct((BLOCK, width), F32),
            jax.ShapeDtypeStruct((4, BLOCK, width), F32),
            jax.ShapeDtypeStruct((rank, width), F32),
        ],
        cost_estimate=pl.CostEstimate(flops=300_000, bytes_accessed=4 << 20, transcendentals=0),
        name="finish",
    )(jnp.full((1,), x, jnp.int32), summed, arrived)


def flip(value, mask):
    return lax.ppermute(value, "tensor", [(i, i ^ mask) for i in range(16)])


def after(value, *events):
    return lax.optimization_barrier((value, *events))[0]


def ring_sum(grads):
    ring, sides, rows, width = grads.shape
    groups = [[x * RING + z for z in range(RING)] for x in range(2)]
    total = lax.psum_scatter(
        grads.reshape(ring * sides * rows, width), "dp", scatter_dimension=0, axis_index_groups=groups, tiled=True
    )
    return total.reshape(sides, rows, width)


def cross(value):
    return lax.ppermute(value, "dp", [(i, i ^ RING) for i in range(2 * RING)])


def per_device(tokens, cotangent, diag_factor, section_factors, low_down, low_up):
    rows, width = tokens.shape
    scale = (rows * lax.axis_size("dp")) ** -0.5
    x = lax.axis_index("dp") // RING
    half = width // 2

    h0 = tokens[:, :half]
    m4_0 = flip(h0, 4)
    m1 = flip(tokens, 1)
    part = jnp.dot(tokens, low_down, preferred_element_type=F32)
    part = part + flip(part, 12)
    part = part + flip(part, 1)
    h1 = after(tokens, part)[:, half:]
    m4_1 = flip(after(h1, m4_0, part), 4)
    m8_0 = flip(after(m4_0, part), 12)
    part = part + flip(part, 2)
    m2_0 = flip(after(h0, part), 2)
    part = part + flip(part, 4)
    m8_1 = flip(after(m4_1, part), 12)
    m2_1 = flip(after(h1, m2_0), 2)
    latent = part.astype(BF16)

    factors = (cotangent, diag_factor, section_factors, latent, low_up)
    slope0, lat0, grads = run_main(0, tokens, (m1, m2_0, m4_0, m8_0), *factors, None)
    slope1, lat1, grads = run_main(1, tokens, (m1, m2_1, m4_1, m8_1), *factors, grads)
    summed = ring_sum(grads)

    part = lat0 + lat1
    arrived = flip(part, 2)
    b1, b2_0, b2_1, b4_0, b4_1, b8_0, b8_1 = run_back((slope0, slope1), section_factors)
    part = part + after(arrived, b1)
    r2_0, r1 = flip(after(b2_0, part), 2), flip(after(b1, part), 1)
    part = part + flip(part, 12)
    q0, q1 = flip(after(b8_0, part), 12), flip(after(b8_1, part), 12)
    part = part + flip(part, 4)
    part = part + after(flip(part, 1), r2_0, r1)
    latent_grad = part.astype(BF16)

    keep, send = run_down(x, tokens, latent_grad)
    s0 = flip(b4_0 + q0, 4)
    pair = (keep.astype(F32) + after(cross(send), q1, s0).astype(F32)).astype(BF16)
    r2_1 = flip(after(b2_1, send), 2)
    groups = [[side * RING + z for z in range(RING)] for side in range(2)]
    pair = lax.all_to_all(pair, "dp", 0, 0, axis_index_groups=groups, tiled=True)
    down_grad = (jnp.sum(pair.astype(F32), axis=0) * scale).T
    s1 = flip(b4_1 + q1, 4)
    arrived = cross(lax.dynamic_index_in_dim(summed, 1 - x, 0, keepdims=False))
    pairs = ((slope0, slope1), (r2_0, r2_1), (s0, after(s1, arrived)))
    token_grad = run_final(pairs, r1, diag_factor, low_down, latent_grad)
    diag_grad, section_grad, up_grad = run_finish(x, summed, arrived, scale)
    return token_grad, diag_grad, section_grad, down_grad, up_grad


def solution(mesh):
    placed = (
        P("dp", "tensor"),
        P("dp", "tensor"),
        P(None, "tensor"),
        P(None, None, "tensor"),
        P("tensor", None),
        P(None, "tensor"),
    )
    return jax.shard_map(
        per_device,
        mesh=mesh,
        in_specs=placed,
        out_specs=(
            P("dp", "tensor"),
            P(None, ("tensor", "dp")),
            P(None, None, ("tensor", "dp")),
            P(("tensor", "dp"), None),
            P(None, ("tensor", "dp")),
        ),
        check_vma=False,
    )
```

```python
import functools

import jax
import jax.numpy as jnp
from jax import lax
from jax.experimental import pallas as pl
from jax.experimental.pallas import tpu as pltpu
from jax.sharding import PartitionSpec as P

BLOCK = 64
CHUNK = 256
MAIN_STEP, FINAL_STEP = 512, 2048
RING = 8
VMEM = 62 << 20
F32 = jnp.float32
BF16 = jnp.bfloat16


def dot(a, b, ca, cb):
    return lax.dot_general(a, b, (((ca,), (cb,)), ((), ())), preferred_element_type=F32)


def gelu_slope(values):
    return (
        0.5 * (1.0 + lax.erf(values * 0.7071067811865476))
        + values * jnp.exp(-0.5 * values * values) * 0.3989422804014327
    )


def block_mask():
    row = lax.broadcasted_iota(jnp.int32, (CHUNK, CHUNK), 0) // BLOCK
    col = lax.broadcasted_iota(jnp.int32, (CHUNK, CHUNK), 1) // BLOCK
    return row == col


def spread(factor, mask):
    tall = jnp.concatenate([factor] * (CHUNK // BLOCK), axis=0)
    return jnp.where(mask, tall, jnp.zeros_like(tall))


def main_kernel(tok, m1, m2, m4, m8, cot, diag, sec, latent, up, *refs):
    slope_out, lat_out, grads = refs[-3:]
    mask = block_mask()
    lat = latent[...]
    group = CHUNK // BLOCK
    lat_sum = jnp.zeros((lat.shape[0], up.shape[0]), F32)
    for c in range(MAIN_STEP // CHUNK):
        cs = slice(c * CHUNK, (c + 1) * CHUNK)
        up_c = up[:, cs]
        sides = [tok[:, cs], m1[:, cs], m2[:, cs], m4[:, cs], m8[:, cs]]
        factors = [spread(diag[:, cs], mask)] + [spread(sec[b, :, cs], mask) for b in range(4)]
        left = jnp.concatenate(sides + [lat], axis=1)
        right = jnp.concatenate(factors + [up_c], axis=0)
        pre = dot(left, right, 1, 0)
        slope = (cot[:, cs].astype(F32) * gelu_slope(pre)).astype(BF16)
        slope_out[:, cs] = slope
        lat_sum = lat_sum + dot(slope, up_c, 1, 1)
        for k, side in enumerate(sides):
            full = dot(side, slope, 0, 0)
            kept = jnp.where(mask, full, jnp.zeros_like(full))
            part = sum(kept[i * BLOCK : (i + 1) * BLOCK] for i in range(group))
            grads[c, 0, k * BLOCK : (k + 1) * BLOCK, :] = part.astype(BF16)
        grads[c, 0, 5 * BLOCK :, :] = dot(lat, slope, 0, 0).astype(BF16)

    @pl.when(pl.program_id(0) == 0)
    def _():
        lat_out[...] = lat_sum

    @pl.when(pl.program_id(0) > 0)
    def _():
        lat_out[...] += lat_sum


def run_main(part, tokens, moved, cotangent, diag, section, latent, up, held):
    rows, width = moved[2].shape
    rank = up.shape[0]
    steps = width // MAIN_STEP
    base = part * steps
    whole = lambda r: pl.BlockSpec((r, MAIN_STEP), lambda i: (0, base + i))
    local = pl.BlockSpec((rows, MAIN_STEP), lambda i: (0, i))
    square = pl.BlockSpec((rows, rank), lambda i: (0, 0))
    section_spec = pl.BlockSpec((4, BLOCK, MAIN_STEP), lambda i: (0, 0, base + i))
    grad_rows = 5 * BLOCK + rank
    in_specs = [whole(rows), whole(rows), local, local, local, whole(rows), whole(BLOCK), section_spec, square, whole(rank)]
    args = [tokens, *moved, cotangent, diag, section, latent, up]
    if held is not None:
        in_specs.append(pl.BlockSpec(memory_space=pl.ANY))
        args.append(held)
    return pl.pallas_call(
        main_kernel,
        grid=(steps,),
        in_specs=in_specs,
        out_specs=[local, square, pl.BlockSpec((MAIN_STEP // CHUNK, 1, grad_rows, CHUNK), lambda i: (i, part, 0, 0))],
        out_shape=[
            jax.ShapeDtypeStruct((rows, width), BF16),
            jax.ShapeDtypeStruct((rows, rank), F32),
            jax.ShapeDtypeStruct((RING, 2, grad_rows, CHUNK), BF16),
        ],
        input_output_aliases={} if held is None else {10: 2},
        compiler_params=pltpu.CompilerParams(vmem_limit_bytes=VMEM),
        cost_estimate=pl.CostEstimate(flops=2_000_000_000, bytes_accessed=28 << 20, transcendentals=0),
        name="main_part",
    )(*args)


def pick_half(low, high):
    first = pl.program_id(0) < pl.num_programs(0) // 2
    return jnp.where(first, low[...], high[...])


def half_specs(rows, steps):
    half = steps // 2
    return [
        pl.BlockSpec((rows, FINAL_STEP), lambda i: (0, jnp.minimum(i, half - 1))),
        pl.BlockSpec((rows, FINAL_STEP), lambda i: (0, jnp.maximum(i - half, 0))),
    ]


def back_kernel(low, high, sec, b1, *halves):
    mask = block_mask()

    def fill(slope, outs):
        for c in range(slope.shape[1] // CHUNK):
            cs = slice(c * CHUNK, (c + 1) * CHUNK)
            for b, out in enumerate(outs):
                out[:, cs] = dot(slope[:, cs], spread(sec[b, :, cs], mask), 1, 1).astype(BF16)

    pl.when(pl.program_id(0) == 0)(lambda: fill(low, (b1, *halves[0::2])))
    pl.when(pl.program_id(0) == 1)(lambda: fill(high, (b1, *halves[1::2])))


def run_back(slopes, section):
    rows, half = slopes[0].shape
    fixed = pl.BlockSpec((rows, half), lambda i: (0, 0))
    moving = pl.BlockSpec((rows, half), lambda i: (0, i))
    return pl.pallas_call(
        back_kernel,
        grid=(2,),
        in_specs=[fixed, fixed, pl.BlockSpec((4, BLOCK, half), lambda i: (0, 0, i))],
        out_specs=[moving] + [fixed] * 6,
        out_shape=[jax.ShapeDtypeStruct((rows, 2 * half), BF16)] + [jax.ShapeDtypeStruct((rows, half), BF16)] * 6,
        compiler_params=pltpu.CompilerParams(vmem_limit_bytes=VMEM),
        cost_estimate=pl.CostEstimate(flops=2_000_000_000, bytes_accessed=20 << 20, transcendentals=0),
        name="back_products",
    )(*slopes, section)


def down_kernel(side, tok, lat, keep, send):
    def fill(out):
        for c in range(tok.shape[1] // CHUNK):
            out[c] = dot(lat[...], tok[:, c * CHUNK : (c + 1) * CHUNK], 0, 0).astype(BF16)

    pl.when(pl.program_id(0) == 0)(lambda: fill(send))
    pl.when(pl.program_id(0) == 1)(lambda: fill(keep))


def run_down(x, tokens, latent_grad):
    rows, width = tokens.shape
    rank = latent_grad.shape[1]
    half = width // 2
    block = pl.BlockSpec((RING, rank, CHUNK), lambda i, side: (0, 0, 0))
    return pl.pallas_call(
        down_kernel,
        grid_spec=pltpu.PrefetchScalarGridSpec(
            num_scalar_prefetch=1,
            grid=(2,),
            in_specs=[
                pl.BlockSpec((rows, half), lambda i, side: (0, (1 + i + side[0]) % 2)),
                pl.BlockSpec((rows, rank), lambda i, side: (0, 0)),
            ],
            out_specs=[block, block],
        ),
        out_shape=[jax.ShapeDtypeStruct((RING, rank, CHUNK), BF16)] * 2,
        cost_estimate=pl.CostEstimate(flops=300_000_000, bytes_accessed=10 << 20, transcendentals=0),
        name="down_part",
    )(jnp.full((1,), x, jnp.int32), tokens, latent_grad)


def final_kernel(*refs):
    pairs, (r1, diag, down, lat, out) = refs[:6], refs[6:]
    mask = block_mask()
    slope, r2, r48 = (pick_half(pairs[2 * k], pairs[2 * k + 1]) for k in range(3))
    for c in range(FINAL_STEP // CHUNK):
        cs = slice(c * CHUNK, (c + 1) * CHUNK)
        total = dot(slope[:, cs], spread(diag[:, cs], mask), 1, 1)
        total = total + dot(lat[...], down[cs, :], 1, 1)
        for value in (r1, r2, r48):
            total = total + value[:, cs].astype(F32)
        out[:, cs] = total.astype(BF16)


def run_final(pairs, r1, diag, low_down, latent_grad):
    rows, half_width = pairs[0][0].shape
    width = 2 * half_width
    rank = latent_grad.shape[1]
    steps = width // FINAL_STEP
    col = lambda r: pl.BlockSpec((r, FINAL_STEP), lambda i: (0, i))
    return pl.pallas_call(
        final_kernel,
        grid=(steps,),
        in_specs=half_specs(rows, steps) * 3
        + [
            col(rows),
            col(BLOCK),
            pl.BlockSpec((FINAL_STEP, rank), lambda i: (i, 0)),
            pl.BlockSpec((rows, rank), lambda i: (0, 0)),
        ],
        out_specs=col(rows),
        out_shape=jax.ShapeDtypeStruct((rows, width), BF16),
        compiler_params=pltpu.CompilerParams(vmem_limit_bytes=VMEM),
        cost_estimate=pl.CostEstimate(flops=2_000_000_000, bytes_accessed=17 << 20, transcendentals=0),
        name="token_grad",
    )(*[value for pair in pairs for value in pair], r1, diag, low_down, latent_grad)


def finish_kernel(scale, side, summed, arrived, diag, section, up):
    total = (summed[0].astype(F32) + arrived[...].astype(F32)) * scale
    diag[...] = total[:BLOCK]
    for b in range(4):
        section[b] = total[(b + 1) * BLOCK : (b + 2) * BLOCK]
    up[...] = total[5 * BLOCK :]


def run_finish(x, summed, arrived, scale):
    _, rows, width = summed.shape
    rank = rows - 5 * BLOCK
    return pl.pallas_call(
        functools.partial(finish_kernel, scale),
        grid_spec=pltpu.PrefetchScalarGridSpec(
            num_scalar_prefetch=1,
            grid=(1,),
            in_specs=[
                pl.BlockSpec((1, rows, width), lambda i, side: (side[0], 0, 0)),
                pl.BlockSpec((rows, width), lambda i, side: (0, 0)),
            ],
            out_specs=[
                pl.BlockSpec((BLOCK, width), lambda i, side: (0, 0)),
                pl.BlockSpec((4, BLOCK, width), lambda i, side: (0, 0, 0)),
                pl.BlockSpec((rank, width), lambda i, side: (0, 0)),
            ],
        ),
        out_shape=[
            jax.ShapeDtypeStruct((BLOCK, width), F32),
            jax.ShapeDtypeStruct((4, BLOCK, width), F32),
            jax.ShapeDtypeStruct((rank, width), F32),
        ],
        cost_estimate=pl.CostEstimate(flops=300_000, bytes_accessed=4 << 20, transcendentals=0),
        name="finish",
    )(jnp.full((1,), x, jnp.int32), summed, arrived)


def flip(value, mask):
    return lax.ppermute(value, "tensor", [(i, i ^ mask) for i in range(16)])


def after(value, *events):
    return lax.optimization_barrier((value, *events))[0]


def ring_sum(grads):
    ring, sides, rows, width = grads.shape
    groups = [[x * RING + z for z in range(RING)] for x in range(2)]
    total = lax.psum_scatter(
        grads.reshape(ring * sides * rows, width), "dp", scatter_dimension=0, axis_index_groups=groups, tiled=True
    )
    return total.reshape(sides, rows, width)


def cross(value):
    return lax.ppermute(value, "dp", [(i, i ^ RING) for i in range(2 * RING)])


def per_device(tokens, cotangent, diag_factor, section_factors, low_down, low_up):
    rows, width = tokens.shape
    scale = (rows * lax.axis_size("dp")) ** -0.5
    x = lax.axis_index("dp") // RING
    half = width // 2

    h0 = tokens[:, :half]
    m4_0, m2_0 = flip(h0, 4), flip(h0, 2)
    m1 = flip(tokens, 1)
    part = jnp.dot(tokens, low_down, preferred_element_type=F32)
    part = part + flip(part, 12)
    h1 = after(tokens, part)[:, half:]
    part = part + flip(part, 4)
    m8_0 = flip(after(m4_0, part), 12)
    m4_1 = flip(after(h1, m4_0, part), 4)
    part = part + flip(part, 1)
    part = part + flip(part, 2)
    m2_1 = flip(after(h1, m2_0, part), 2)
    m8_1 = flip(after(m4_1, part), 12)
    latent = part.astype(BF16)

    factors = (cotangent, diag_factor, section_factors, latent, low_up)
    slope0, lat0, grads = run_main(0, tokens, (m1, m2_0, m4_0, m8_0), *factors, None)
    slope1, lat1, grads = run_main(1, tokens, (m1, m2_1, m4_1, m8_1), *factors, grads)
    summed = ring_sum(grads)

    part = lat0 + lat1
    arrived = flip(part, 2)
    b1, b2_0, b2_1, b4_0, b4_1, b8_0, b8_1 = run_back((slope0, slope1), section_factors)
    part = part + after(arrived, b1)
    r2_0, r1 = flip(after(b2_0, part), 2), flip(after(b1, part), 1)
    part = part + flip(part, 12)
    q0, q1 = flip(after(b8_0, part), 12), flip(after(b8_1, part), 12)
    part = part + flip(part, 4)
    part = part + after(flip(part, 1), r2_0, r1)
    latent_grad = part.astype(BF16)

    keep, send = run_down(x, tokens, latent_grad)
    s0 = flip(b4_0 + after(q0, send), 4)
    pair = (keep.astype(F32) + after(cross(send), q1, s0).astype(F32)).astype(BF16)
    r2_1 = flip(after(b2_1, send), 2)
    groups = [[side * RING + z for z in range(RING)] for side in range(2)]
    pair = lax.all_to_all(pair, "dp", 0, 0, axis_index_groups=groups, tiled=True)
    s1 = flip(b4_1 + q1, 4)
    arrived = cross(lax.dynamic_index_in_dim(summed, 1 - x, 0, keepdims=False))
    down_grad = (jnp.sum(after(pair, arrived).astype(F32), axis=0) * scale).T
    pairs = ((slope0, slope1), (r2_0, r2_1), (s0, after(s1, arrived)))
    token_grad = run_final(pairs, r1, diag_factor, low_down, latent_grad)
    diag_grad, section_grad, up_grad = run_finish(x, summed, arrived, scale)
    return token_grad, diag_grad, section_grad, down_grad, up_grad


def solution(mesh):
    placed = (
        P("dp", "tensor"),
        P("dp", "tensor"),
        P(None, "tensor"),
        P(None, None, "tensor"),
        P("tensor", None),
        P(None, "tensor"),
    )
    return jax.shard_map(
        per_device,
        mesh=mesh,
        in_specs=placed,
        out_specs=(
            P("dp", "tensor"),
            P(None, ("tensor", "dp")),
            P(None, None, ("tensor", "dp")),
            P(("tensor", "dp"), None),
            P(None, ("tensor", "dp")),
        ),
        check_vma=False,
    )
```

```python
import functools

import jax
import jax.numpy as jnp
from jax import lax
from jax.experimental import pallas as pl
from jax.experimental.pallas import tpu as pltpu
from jax.sharding import PartitionSpec as P

BLOCK = 64
CHUNK = 256
MAIN_STEP, FINAL_STEP = 512, 2048
RING = 8
VMEM = 62 << 20
F32 = jnp.float32
BF16 = jnp.bfloat16


def dot(a, b, ca, cb):
    return lax.dot_general(a, b, (((ca,), (cb,)), ((), ())), preferred_element_type=F32)


def gelu_slope(values):
    return (
        0.5 * (1.0 + lax.erf(values * 0.7071067811865476))
        + values * jnp.exp(-0.5 * values * values) * 0.3989422804014327
    )


def block_mask():
    row = lax.broadcasted_iota(jnp.int32, (CHUNK, CHUNK), 0) // BLOCK
    col = lax.broadcasted_iota(jnp.int32, (CHUNK, CHUNK), 1) // BLOCK
    return row == col


def spread(factor, mask):
    tall = jnp.concatenate([factor] * (CHUNK // BLOCK), axis=0)
    return jnp.where(mask, tall, jnp.zeros_like(tall))


def main_kernel(tok, m1, m2, m4, m8, cot, diag, sec, latent, up, *refs):
    slope_out, lat_out, grads = refs[-3:]
    mask = block_mask()
    lat = latent[...]
    group = CHUNK // BLOCK
    lat_sum = jnp.zeros((lat.shape[0], up.shape[0]), F32)
    for c in range(MAIN_STEP // CHUNK):
        cs = slice(c * CHUNK, (c + 1) * CHUNK)
        up_c = up[:, cs]
        sides = [tok[:, cs], m1[:, cs], m2[:, cs], m4[:, cs], m8[:, cs]]
        factors = [spread(diag[:, cs], mask)] + [spread(sec[b, :, cs], mask) for b in range(4)]
        left = jnp.concatenate(sides + [lat], axis=1)
        right = jnp.concatenate(factors + [up_c], axis=0)
        pre = dot(left, right, 1, 0)
        slope = (cot[:, cs].astype(F32) * gelu_slope(pre)).astype(BF16)
        slope_out[:, cs] = slope
        lat_sum = lat_sum + dot(slope, up_c, 1, 1)
        for k, side in enumerate(sides):
            full = dot(side, slope, 0, 0)
            kept = jnp.where(mask, full, jnp.zeros_like(full))
            part = sum(kept[i * BLOCK : (i + 1) * BLOCK] for i in range(group))
            grads[c, 0, k * BLOCK : (k + 1) * BLOCK, :] = part.astype(BF16)
        grads[c, 0, 5 * BLOCK :, :] = dot(lat, slope, 0, 0).astype(BF16)

    @pl.when(pl.program_id(0) == 0)
    def _():
        lat_out[...] = lat_sum

    @pl.when(pl.program_id(0) > 0)
    def _():
        lat_out[...] += lat_sum


def run_main(part, tokens, moved, cotangent, diag, section, latent, up, held):
    rows, width = moved[2].shape
    rank = up.shape[0]
    steps = width // MAIN_STEP
    base = part * steps
    whole = lambda r: pl.BlockSpec((r, MAIN_STEP), lambda i: (0, base + i))
    local = pl.BlockSpec((rows, MAIN_STEP), lambda i: (0, i))
    square = pl.BlockSpec((rows, rank), lambda i: (0, 0))
    section_spec = pl.BlockSpec((4, BLOCK, MAIN_STEP), lambda i: (0, 0, base + i))
    grad_rows = 5 * BLOCK + rank
    in_specs = [whole(rows), whole(rows), local, local, local, whole(rows), whole(BLOCK), section_spec, square, whole(rank)]
    args = [tokens, *moved, cotangent, diag, section, latent, up]
    if held is not None:
        in_specs.append(pl.BlockSpec(memory_space=pl.ANY))
        args.append(held)
    return pl.pallas_call(
        main_kernel,
        grid=(steps,),
        in_specs=in_specs,
        out_specs=[local, square, pl.BlockSpec((MAIN_STEP // CHUNK, 1, grad_rows, CHUNK), lambda i: (i, part, 0, 0))],
        out_shape=[
            jax.ShapeDtypeStruct((rows, width), BF16),
            jax.ShapeDtypeStruct((rows, rank), F32),
            jax.ShapeDtypeStruct((RING, 2, grad_rows, CHUNK), BF16),
        ],
        input_output_aliases={} if held is None else {10: 2},
        compiler_params=pltpu.CompilerParams(vmem_limit_bytes=VMEM),
        cost_estimate=pl.CostEstimate(flops=2_000_000_000, bytes_accessed=28 << 20, transcendentals=0),
        name="main_part",
    )(*args)


def pick_half(low, high):
    first = pl.program_id(0) < pl.num_programs(0) // 2
    return jnp.where(first, low[...], high[...])


def half_specs(rows, steps):
    half = steps // 2
    return [
        pl.BlockSpec((rows, FINAL_STEP), lambda i: (0, jnp.minimum(i, half - 1))),
        pl.BlockSpec((rows, FINAL_STEP), lambda i: (0, jnp.maximum(i - half, 0))),
    ]


def back_kernel(low, high, sec, b1, b2, *halves):
    mask = block_mask()

    def fill(slope, outs):
        for c in range(slope.shape[1] // CHUNK):
            cs = slice(c * CHUNK, (c + 1) * CHUNK)
            for b, out in enumerate(outs):
                out[:, cs] = dot(slope[:, cs], spread(sec[b, :, cs], mask), 1, 1).astype(BF16)

    pl.when(pl.program_id(0) == 0)(lambda: fill(low, (b1, b2, *halves[0::2])))
    pl.when(pl.program_id(0) == 1)(lambda: fill(high, (b1, b2, *halves[1::2])))


def run_back(slopes, section):
    rows, half = slopes[0].shape
    fixed = pl.BlockSpec((rows, half), lambda i: (0, 0))
    moving = pl.BlockSpec((rows, half), lambda i: (0, i))
    return pl.pallas_call(
        back_kernel,
        grid=(2,),
        in_specs=[fixed, fixed, pl.BlockSpec((4, BLOCK, half), lambda i: (0, 0, i))],
        out_specs=[moving] * 2 + [fixed] * 4,
        out_shape=[jax.ShapeDtypeStruct((rows, 2 * half), BF16)] * 2 + [jax.ShapeDtypeStruct((rows, half), BF16)] * 4,
        compiler_params=pltpu.CompilerParams(vmem_limit_bytes=VMEM),
        cost_estimate=pl.CostEstimate(flops=2_000_000_000, bytes_accessed=20 << 20, transcendentals=0),
        name="back_products",
    )(*slopes, section)


def down_kernel(side, tok, lat, keep, send):
    def fill(out):
        for c in range(tok.shape[1] // CHUNK):
            out[c] = dot(lat[...], tok[:, c * CHUNK : (c + 1) * CHUNK], 0, 0).astype(BF16)

    pl.when(pl.program_id(0) == 0)(lambda: fill(send))
    pl.when(pl.program_id(0) == 1)(lambda: fill(keep))


def run_down(x, tokens, latent_grad):
    rows, width = tokens.shape
    rank = latent_grad.shape[1]
    half = width // 2
    block = pl.BlockSpec((RING, rank, CHUNK), lambda i, side: (0, 0, 0))
    return pl.pallas_call(
        down_kernel,
        grid_spec=pltpu.PrefetchScalarGridSpec(
            num_scalar_prefetch=1,
            grid=(2,),
            in_specs=[
                pl.BlockSpec((rows, half), lambda i, side: (0, (1 + i + side[0]) % 2)),
                pl.BlockSpec((rows, rank), lambda i, side: (0, 0)),
            ],
            out_specs=[block, block],
        ),
        out_shape=[jax.ShapeDtypeStruct((RING, rank, CHUNK), BF16)] * 2,
        cost_estimate=pl.CostEstimate(flops=300_000_000, bytes_accessed=10 << 20, transcendentals=0),
        name="down_part",
    )(jnp.full((1,), x, jnp.int32), tokens, latent_grad)


def final_kernel(*refs):
    pairs, (r1, r2, diag, down, lat, out) = refs[:4], refs[4:]
    mask = block_mask()
    slope, r48 = (pick_half(pairs[2 * k], pairs[2 * k + 1]) for k in range(2))
    for c in range(FINAL_STEP // CHUNK):
        cs = slice(c * CHUNK, (c + 1) * CHUNK)
        total = dot(slope[:, cs], spread(diag[:, cs], mask), 1, 1)
        total = total + dot(lat[...], down[cs, :], 1, 1)
        for value in (r1, r2, r48):
            total = total + value[:, cs].astype(F32)
        out[:, cs] = total.astype(BF16)


def run_final(pairs, r1, r2, diag, low_down, latent_grad):
    rows, half_width = pairs[0][0].shape
    width = 2 * half_width
    rank = latent_grad.shape[1]
    steps = width // FINAL_STEP
    col = lambda r: pl.BlockSpec((r, FINAL_STEP), lambda i: (0, i))
    return pl.pallas_call(
        final_kernel,
        grid=(steps,),
        in_specs=half_specs(rows, steps) * 2
        + [
            col(rows),
            col(rows),
            col(BLOCK),
            pl.BlockSpec((FINAL_STEP, rank), lambda i: (i, 0)),
            pl.BlockSpec((rows, rank), lambda i: (0, 0)),
        ],
        out_specs=col(rows),
        out_shape=jax.ShapeDtypeStruct((rows, width), BF16),
        compiler_params=pltpu.CompilerParams(vmem_limit_bytes=VMEM),
        cost_estimate=pl.CostEstimate(flops=2_000_000_000, bytes_accessed=17 << 20, transcendentals=0),
        name="token_grad",
    )(*[value for pair in pairs for value in pair], r1, r2, diag, low_down, latent_grad)


def finish_kernel(scale, side, summed, arrived, diag, section, up):
    total = (summed[0].astype(F32) + arrived[...].astype(F32)) * scale
    diag[...] = total[:BLOCK]
    for b in range(4):
        section[b] = total[(b + 1) * BLOCK : (b + 2) * BLOCK]
    up[...] = total[5 * BLOCK :]


def run_finish(x, summed, arrived, scale):
    _, rows, width = summed.shape
    rank = rows - 5 * BLOCK
    return pl.pallas_call(
        functools.partial(finish_kernel, scale),
        grid_spec=pltpu.PrefetchScalarGridSpec(
            num_scalar_prefetch=1,
            grid=(1,),
            in_specs=[
                pl.BlockSpec((1, rows, width), lambda i, side: (side[0], 0, 0)),
                pl.BlockSpec((rows, width), lambda i, side: (0, 0)),
            ],
            out_specs=[
                pl.BlockSpec((BLOCK, width), lambda i, side: (0, 0)),
                pl.BlockSpec((4, BLOCK, width), lambda i, side: (0, 0, 0)),
                pl.BlockSpec((rank, width), lambda i, side: (0, 0)),
            ],
        ),
        out_shape=[
            jax.ShapeDtypeStruct((BLOCK, width), F32),
            jax.ShapeDtypeStruct((4, BLOCK, width), F32),
            jax.ShapeDtypeStruct((rank, width), F32),
        ],
        cost_estimate=pl.CostEstimate(flops=300_000, bytes_accessed=4 << 20, transcendentals=0),
        name="finish",
    )(jnp.full((1,), x, jnp.int32), summed, arrived)


def flip(value, mask):
    return lax.ppermute(value, "tensor", [(i, i ^ mask) for i in range(16)])


def after(value, *events):
    return lax.optimization_barrier((value, *events))[0]


def ring_sum(grads):
    ring, sides, rows, width = grads.shape
    groups = [[x * RING + z for z in range(RING)] for x in range(2)]
    total = lax.psum_scatter(
        grads.reshape(ring * sides * rows, width), "dp", scatter_dimension=0, axis_index_groups=groups, tiled=True
    )
    return total.reshape(sides, rows, width)


def cross(value):
    return lax.ppermute(value, "dp", [(i, i ^ RING) for i in range(2 * RING)])


def per_device(tokens, cotangent, diag_factor, section_factors, low_down, low_up):
    rows, width = tokens.shape
    scale = (rows * lax.axis_size("dp")) ** -0.5
    x = lax.axis_index("dp") // RING
    half = width // 2

    h0 = tokens[:, :half]
    m4_0, m2_0 = flip(h0, 4), flip(h0, 2)
    m1 = flip(tokens, 1)
    part = jnp.dot(tokens, low_down, preferred_element_type=F32)
    part = part + flip(part, 12)
    h1 = after(tokens, part)[:, half:]
    part = part + flip(part, 4)
    m8_0 = flip(after(m4_0, part), 12)
    m4_1 = flip(after(h1, m4_0, part), 4)
    part = part + flip(part, 1)
    part = part + flip(part, 2)
    m2_1 = flip(after(h1, m2_0, part), 2)
    m8_1 = flip(after(m4_1, part), 12)
    latent = part.astype(BF16)

    factors = (cotangent, diag_factor, section_factors, latent, low_up)
    slope0, lat0, grads = run_main(0, tokens, (m1, m2_0, m4_0, m8_0), *factors, None)
    slope1, lat1, grads = run_main(1, tokens, (m1, m2_1, m4_1, m8_1), *factors, grads)
    summed = ring_sum(grads)

    part = lat0 + lat1
    arrived = flip(part, 2)
    b1, b2, b4_0, b4_1, b8_0, b8_1 = run_back((slope0, slope1), section_factors)
    part = part + after(arrived, b1)
    r2, r1 = flip(after(b2, part), 2), flip(after(b1, part), 1)
    part = part + flip(part, 12)
    q0, q1 = flip(after(b8_0, part), 12), flip(after(b8_1, part), 12)
    part = part + flip(part, 4)
    part = part + after(flip(part, 1), r1)
    latent_grad = part.astype(BF16)

    keep, send = run_down(x, tokens, latent_grad)
    s0 = flip(b4_0 + after(q0, send), 4)
    pair = (keep.astype(F32) + after(cross(send), r2, q1, s0).astype(F32)).astype(BF16)
    groups = [[side * RING + z for z in range(RING)] for side in range(2)]
    pair = lax.all_to_all(pair, "dp", 0, 0, axis_index_groups=groups, tiled=True)
    s1 = flip(b4_1 + q1, 4)
    other = lax.dynamic_index_in_dim(after(summed, s1), 1 - x, 0, keepdims=False)
    arrived = cross(other)
    down_grad = (jnp.sum(after(pair, arrived).astype(F32), axis=0) * scale).T
    pairs = ((slope0, slope1), (s0, after(s1, other)))
    token_grad = run_final(pairs, r1, r2, diag_factor, low_down, latent_grad)
    diag_grad, section_grad, up_grad = run_finish(x, summed, arrived, scale)
    return token_grad, diag_grad, section_grad, down_grad, up_grad


def solution(mesh):
    placed = (
        P("dp", "tensor"),
        P("dp", "tensor"),
        P(None, "tensor"),
        P(None, None, "tensor"),
        P("tensor", None),
        P(None, "tensor"),
    )
    return jax.shard_map(
        per_device,
        mesh=mesh,
        in_specs=placed,
        out_specs=(
            P("dp", "tensor"),
            P(None, ("tensor", "dp")),
            P(None, None, ("tensor", "dp")),
            P(("tensor", "dp"), None),
            P(None, ("tensor", "dp")),
        ),
        check_vma=False,
    )
```

```python
import functools

import jax
import jax.numpy as jnp
from jax import lax
from jax.experimental import pallas as pl
from jax.experimental.pallas import tpu as pltpu
from jax.sharding import PartitionSpec as P

BLOCK = 64
CHUNK = 256
MAIN_STEP, FINAL_STEP = 512, 1024
RING = 8
VMEM = 62 << 20
F32 = jnp.float32
BF16 = jnp.bfloat16


def dot(a, b, ca, cb):
    return lax.dot_general(a, b, (((ca,), (cb,)), ((), ())), preferred_element_type=F32)


def gelu_slope(values):
    return (
        0.5 * (1.0 + lax.erf(values * 0.7071067811865476))
        + values * jnp.exp(-0.5 * values * values) * 0.3989422804014327
    )


def block_mask():
    row = lax.broadcasted_iota(jnp.int32, (CHUNK, CHUNK), 0) // BLOCK
    col = lax.broadcasted_iota(jnp.int32, (CHUNK, CHUNK), 1) // BLOCK
    return row == col


def spread(factor, mask):
    tall = jnp.concatenate([factor] * (CHUNK // BLOCK), axis=0)
    return jnp.where(mask, tall, jnp.zeros_like(tall))


def main_kernel(tok, m1, m2, m4, m8, cot, diag, sec, latent, up, *refs):
    slope_out, lat_out, grads = refs[-3:]
    mask = block_mask()
    lat = latent[...]
    group = CHUNK // BLOCK
    lat_sum = jnp.zeros((lat.shape[0], up.shape[0]), F32)
    for c in range(MAIN_STEP // CHUNK):
        cs = slice(c * CHUNK, (c + 1) * CHUNK)
        up_c = up[:, cs]
        sides = [tok[:, cs], m1[:, cs], m2[:, cs], m4[:, cs], m8[:, cs]]
        factors = [spread(diag[:, cs], mask)] + [spread(sec[b, :, cs], mask) for b in range(4)]
        left = jnp.concatenate(sides + [lat], axis=1)
        right = jnp.concatenate(factors + [up_c], axis=0)
        pre = dot(left, right, 1, 0)
        slope = (cot[:, cs].astype(F32) * gelu_slope(pre)).astype(BF16)
        slope_out[:, cs] = slope
        lat_sum = lat_sum + dot(slope, up_c, 1, 1)
        for k, side in enumerate(sides):
            full = dot(side, slope, 0, 0)
            kept = jnp.where(mask, full, jnp.zeros_like(full))
            part = sum(kept[i * BLOCK : (i + 1) * BLOCK] for i in range(group))
            grads[c, 0, k * BLOCK : (k + 1) * BLOCK, :] = part.astype(BF16)
        grads[c, 0, 5 * BLOCK :, :] = dot(lat, slope, 0, 0).astype(BF16)

    @pl.when(pl.program_id(0) == 0)
    def _():
        lat_out[...] = lat_sum

    @pl.when(pl.program_id(0) > 0)
    def _():
        lat_out[...] += lat_sum


def run_main(part, tokens, moved, cotangent, diag, section, latent, up, held):
    rows, width = moved[2].shape
    rank = up.shape[0]
    steps = width // MAIN_STEP
    base = part * steps
    whole = lambda r: pl.BlockSpec((r, MAIN_STEP), lambda i: (0, base + i))
    local = pl.BlockSpec((rows, MAIN_STEP), lambda i: (0, i))
    square = pl.BlockSpec((rows, rank), lambda i: (0, 0))
    section_spec = pl.BlockSpec((4, BLOCK, MAIN_STEP), lambda i: (0, 0, base + i))
    grad_rows = 5 * BLOCK + rank
    in_specs = [whole(rows), whole(rows), local, local, local, whole(rows), whole(BLOCK), section_spec, square, whole(rank)]
    args = [tokens, *moved, cotangent, diag, section, latent, up]
    if held is not None:
        in_specs.append(pl.BlockSpec(memory_space=pl.ANY))
        args.append(held)
    return pl.pallas_call(
        main_kernel,
        grid=(steps,),
        in_specs=in_specs,
        out_specs=[local, square, pl.BlockSpec((MAIN_STEP // CHUNK, 1, grad_rows, CHUNK), lambda i: (i, part, 0, 0))],
        out_shape=[
            jax.ShapeDtypeStruct((rows, width), BF16),
            jax.ShapeDtypeStruct((rows, rank), F32),
            jax.ShapeDtypeStruct((RING, 2, grad_rows, CHUNK), BF16),
        ],
        input_output_aliases={} if held is None else {10: 2},
        compiler_params=pltpu.CompilerParams(vmem_limit_bytes=VMEM),
        cost_estimate=pl.CostEstimate(flops=2_000_000_000, bytes_accessed=28 << 20, transcendentals=0),
        name="main_part",
    )(*args)


def back_kernel(low, high, sec, b1, *halves):
    mask = block_mask()

    def fill(slope, outs):
        for c in range(slope.shape[1] // CHUNK):
            cs = slice(c * CHUNK, (c + 1) * CHUNK)
            for b, out in enumerate(outs):
                out[:, cs] = dot(slope[:, cs], spread(sec[b, :, cs], mask), 1, 1).astype(BF16)

    pl.when(pl.program_id(0) == 0)(lambda: fill(low, (b1, *halves[0::2])))
    pl.when(pl.program_id(0) == 1)(lambda: fill(high, (b1, *halves[1::2])))


def run_back(slopes, section):
    rows, half = slopes[0].shape
    fixed = pl.BlockSpec((rows, half), lambda i: (0, 0))
    moving = pl.BlockSpec((rows, half), lambda i: (0, i))
    return pl.pallas_call(
        back_kernel,
        grid=(2,),
        in_specs=[fixed, fixed, pl.BlockSpec((4, BLOCK, half), lambda i: (0, 0, i))],
        out_specs=[moving] + [fixed] * 6,
        out_shape=[jax.ShapeDtypeStruct((rows, 2 * half), BF16)] + [jax.ShapeDtypeStruct((rows, half), BF16)] * 6,
        compiler_params=pltpu.CompilerParams(vmem_limit_bytes=VMEM),
        cost_estimate=pl.CostEstimate(flops=2_000_000_000, bytes_accessed=20 << 20, transcendentals=0),
        name="back_products",
    )(*slopes, section)


def down_kernel(side, tok, lat, keep, send):
    def fill(out):
        for c in range(tok.shape[1] // CHUNK):
            out[c] = dot(lat[...], tok[:, c * CHUNK : (c + 1) * CHUNK], 0, 0).astype(BF16)

    pl.when(pl.program_id(0) == 0)(lambda: fill(send))
    pl.when(pl.program_id(0) == 1)(lambda: fill(keep))


def run_down(x, tokens, latent_grad):
    rows, width = tokens.shape
    rank = latent_grad.shape[1]
    half = width // 2
    block = pl.BlockSpec((RING, rank, CHUNK), lambda i, side: (0, 0, 0))
    return pl.pallas_call(
        down_kernel,
        grid_spec=pltpu.PrefetchScalarGridSpec(
            num_scalar_prefetch=1,
            grid=(2,),
            in_specs=[
                pl.BlockSpec((rows, half), lambda i, side: (0, (1 + i + side[0]) % 2)),
                pl.BlockSpec((rows, rank), lambda i, side: (0, 0)),
            ],
            out_specs=[block, block],
        ),
        out_shape=[jax.ShapeDtypeStruct((RING, rank, CHUNK), BF16)] * 2,
        cost_estimate=pl.CostEstimate(flops=300_000_000, bytes_accessed=10 << 20, transcendentals=0),
        name="down_part",
    )(jnp.full((1,), x, jnp.int32), tokens, latent_grad)


def final_kernel(slope, r1, r2, r48, diag, down, lat, *refs):
    out = refs[-1]
    mask = block_mask()
    for c in range(slope.shape[1] // CHUNK):
        cs = slice(c * CHUNK, (c + 1) * CHUNK)
        total = dot(slope[:, cs], spread(diag[:, cs], mask), 1, 1)
        total = total + dot(lat[...], down[cs, :], 1, 1)
        for ref in (r1, r2, r48):
            total = total + ref[:, cs].astype(F32)
        out[:, cs] = total.astype(BF16)


def run_final(part, slope, r1, r2, r48, diag, low_down, latent_grad, held):
    rows, half = slope.shape
    rank = latent_grad.shape[1]
    steps = half // FINAL_STEP
    base = part * steps
    local = pl.BlockSpec((rows, FINAL_STEP), lambda i: (0, i))
    whole = lambda r: pl.BlockSpec((r, FINAL_STEP), lambda i: (0, base + i))
    in_specs = [
        local, whole(rows), local, local, whole(BLOCK),
        pl.BlockSpec((FINAL_STEP, rank), lambda i: (base + i, 0)),
        pl.BlockSpec((rows, rank), lambda i: (0, 0)),
    ]
    args = [slope, r1, r2, r48, diag, low_down, latent_grad]
    if held is not None:
        in_specs.append(pl.BlockSpec(memory_space=pl.ANY))
        args.append(held)
    return pl.pallas_call(
        final_kernel,
        grid=(steps,),
        in_specs=in_specs,
        out_specs=whole(rows),
        out_shape=jax.ShapeDtypeStruct((rows, diag.shape[1]), BF16),
        input_output_aliases={} if held is None else {7: 0},
        compiler_params=pltpu.CompilerParams(vmem_limit_bytes=VMEM),
        cost_estimate=pl.CostEstimate(flops=1_000_000_000, bytes_accessed=9 << 20, transcendentals=0),
        name="token_grad",
    )(*args)


def finish_kernel(scale, side, summed, arrived, diag, section, up):
    total = (summed[0].astype(F32) + arrived[...].astype(F32)) * scale
    diag[...] = total[:BLOCK]
    for b in range(4):
        section[b] = total[(b + 1) * BLOCK : (b + 2) * BLOCK]
    up[...] = total[5 * BLOCK :]


def run_finish(x, summed, arrived, scale):
    _, rows, width = summed.shape
    rank = rows - 5 * BLOCK
    return pl.pallas_call(
        functools.partial(finish_kernel, scale),
        grid_spec=pltpu.PrefetchScalarGridSpec(
            num_scalar_prefetch=1,
            grid=(1,),
            in_specs=[
                pl.BlockSpec((1, rows, width), lambda i, side: (side[0], 0, 0)),
                pl.BlockSpec((rows, width), lambda i, side: (0, 0)),
            ],
            out_specs=[
                pl.BlockSpec((BLOCK, width), lambda i, side: (0, 0)),
                pl.BlockSpec((4, BLOCK, width), lambda i, side: (0, 0, 0)),
                pl.BlockSpec((rank, width), lambda i, side: (0, 0)),
            ],
        ),
        out_shape=[
            jax.ShapeDtypeStruct((BLOCK, width), F32),
            jax.ShapeDtypeStruct((4, BLOCK, width), F32),
            jax.ShapeDtypeStruct((rank, width), F32),
        ],
        cost_estimate=pl.CostEstimate(flops=300_000, bytes_accessed=4 << 20, transcendentals=0),
        name="finish",
    )(jnp.full((1,), x, jnp.int32), summed, arrived)


def flip(value, mask):
    return lax.ppermute(value, "tensor", [(i, i ^ mask) for i in range(16)])


def after(value, *events):
    return lax.optimization_barrier((value, *events))[0]


def ring_sum(grads):
    ring, sides, rows, width = grads.shape
    groups = [[x * RING + z for z in range(RING)] for x in range(2)]
    total = lax.psum_scatter(
        grads.reshape(ring * sides * rows, width), "dp", scatter_dimension=0, axis_index_groups=groups, tiled=True
    )
    return total.reshape(sides, rows, width)


def cross(value):
    return lax.ppermute(value, "dp", [(i, i ^ RING) for i in range(2 * RING)])


def per_device(tokens, cotangent, diag_factor, section_factors, low_down, low_up):
    rows, width = tokens.shape
    scale = (rows * lax.axis_size("dp")) ** -0.5
    x = lax.axis_index("dp") // RING
    half = width // 2

    h0 = tokens[:, :half]
    m4_0, m2_0 = flip(h0, 4), flip(h0, 2)
    m1 = flip(tokens, 1)
    part = jnp.dot(tokens, low_down, preferred_element_type=F32)
    part = part + flip(part, 12)
    h1 = after(tokens, part)[:, half:]
    part = part + flip(part, 4)
    m8_0 = flip(after(m4_0, part), 12)
    m4_1 = flip(after(h1, m4_0, part), 4)
    part = part + flip(part, 2)
    m2_1 = flip(after(h1, m2_0, part), 2)
    m8_1 = flip(m4_1, 12)
    part = part + flip(part, 1)
    latent = part.astype(BF16)

    factors = (cotangent, diag_factor, section_factors, latent, low_up)
    slope0, lat0, grads = run_main(0, tokens, (m1, m2_0, m4_0, m8_0), *factors, None)
    slope1, lat1, grads = run_main(1, tokens, (m1, m2_1, m4_1, m8_1), *factors, grads)
    summed = ring_sum(grads)

    part = lat0 + lat1
    arrived = flip(part, 2) + flip(part, 12) + flip(part, 14)
    b1, b2_0, b2_1, b4_0, b4_1, b8_0, b8_1 = run_back((slope0, slope1), section_factors)
    part = part + after(arrived, b1)
    r2_0, q0 = flip(after(b2_0, part), 2), flip(after(b8_0, part), 12)
    part = part + after(flip(part, 4) + flip(part, 1) + flip(part, 5), r2_0)
    r2_1, q1, r1 = flip(after(b2_1, part), 2), flip(after(b8_1, part), 12), flip(after(b1, part), 1)
    latent_grad = part.astype(BF16)

    keep, send = run_down(x, tokens, latent_grad)
    s0 = flip(b4_0 + after(q0, send), 4)
    pair = (keep.astype(F32) + after(cross(after(send, r2_1)), q1, s0, r1).astype(F32)).astype(BF16)
    groups = [[side * RING + z for z in range(RING)] for side in range(2)]
    pair = lax.all_to_all(pair, "dp", 0, 0, axis_index_groups=groups, tiled=True)
    s1 = flip(b4_1 + q1, 4)
    other = lax.dynamic_index_in_dim(summed, 1 - x, 0, keepdims=False)
    arrived = cross(other)
    down_grad = (jnp.sum(after(pair, arrived).astype(F32), axis=0) * scale).T
    token_grad = run_final(0, slope0, r1, r2_0, after(s0, other), diag_factor, low_down, latent_grad, None)
    token_grad = run_final(1, slope1, r1, r2_1, after(s1, other), diag_factor, low_down, latent_grad, token_grad)
    diag_grad, section_grad, up_grad = run_finish(x, summed, arrived, scale)
    return token_grad, diag_grad, section_grad, down_grad, up_grad


def solution(mesh):
    placed = (
        P("dp", "tensor"),
        P("dp", "tensor"),
        P(None, "tensor"),
        P(None, None, "tensor"),
        P("tensor", None),
        P(None, "tensor"),
    )
    return jax.shard_map(
        per_device,
        mesh=mesh,
        in_specs=placed,
        out_specs=(
            P("dp", "tensor"),
            P(None, ("tensor", "dp")),
            P(None, None, ("tensor", "dp")),
            P(("tensor", "dp"), None),
            P(None, ("tensor", "dp")),
        ),
        check_vma=False,
    )
```

```python
import functools

import jax
import jax.numpy as jnp
from jax import lax
from jax.experimental import pallas as pl
from jax.experimental.pallas import tpu as pltpu
from jax.sharding import PartitionSpec as P

BLOCK = 64
CHUNK = 256
MAIN_STEP, FINAL_STEP = 512, 2048
RING = 8
VMEM = 62 << 20
F32 = jnp.float32
BF16 = jnp.bfloat16


def dot(a, b, ca, cb):
    return lax.dot_general(a, b, (((ca,), (cb,)), ((), ())), preferred_element_type=F32)


def gelu_slope(values):
    return (
        0.5 * (1.0 + lax.erf(values * 0.7071067811865476))
        + values * jnp.exp(-0.5 * values * values) * 0.3989422804014327
    )


def block_mask():
    row = lax.broadcasted_iota(jnp.int32, (CHUNK, CHUNK), 0) // BLOCK
    col = lax.broadcasted_iota(jnp.int32, (CHUNK, CHUNK), 1) // BLOCK
    return row == col


def spread(factor, mask):
    tall = jnp.concatenate([factor] * (CHUNK // BLOCK), axis=0)
    return jnp.where(mask, tall, jnp.zeros_like(tall))


def main_kernel(tok, m1, m2, m4, m8, cot, diag, sec, latent, up, *refs):
    slope_out, lat_out, grads = refs[-3:]
    mask = block_mask()
    lat = latent[...]
    group = CHUNK // BLOCK
    lat_sum = jnp.zeros((lat.shape[0], up.shape[0]), F32)
    for c in range(MAIN_STEP // CHUNK):
        cs = slice(c * CHUNK, (c + 1) * CHUNK)
        up_c = up[:, cs]
        sides = [tok[:, cs], m1[:, cs], m2[:, cs], m4[:, cs], m8[:, cs]]
        factors = [spread(diag[:, cs], mask)] + [spread(sec[b, :, cs], mask) for b in range(4)]
        left = jnp.concatenate(sides + [lat], axis=1)
        right = jnp.concatenate(factors + [up_c], axis=0)
        pre = dot(left, right, 1, 0)
        slope = (cot[:, cs].astype(F32) * gelu_slope(pre)).astype(BF16)
        slope_out[:, cs] = slope
        lat_sum = lat_sum + dot(slope, up_c, 1, 1)
        for k, side in enumerate(sides):
            full = dot(side, slope, 0, 0)
            kept = jnp.where(mask, full, jnp.zeros_like(full))
            part = sum(kept[i * BLOCK : (i + 1) * BLOCK] for i in range(group))
            grads[c, 0, k * BLOCK : (k + 1) * BLOCK, :] = part.astype(BF16)
        grads[c, 0, 5 * BLOCK :, :] = dot(lat, slope, 0, 0).astype(BF16)

    @pl.when(pl.program_id(0) == 0)
    def _():
        lat_out[...] = lat_sum

    @pl.when(pl.program_id(0) > 0)
    def _():
        lat_out[...] += lat_sum


def run_main(part, tokens, moved, cotangent, diag, section, latent, up, held):
    rows, width = moved[2].shape
    rank = up.shape[0]
    steps = width // MAIN_STEP
    base = part * steps
    whole = lambda r: pl.BlockSpec((r, MAIN_STEP), lambda i: (0, base + i))
    local = pl.BlockSpec((rows, MAIN_STEP), lambda i: (0, i))
    square = pl.BlockSpec((rows, rank), lambda i: (0, 0))
    section_spec = pl.BlockSpec((4, BLOCK, MAIN_STEP), lambda i: (0, 0, base + i))
    grad_rows = 5 * BLOCK + rank
    in_specs = [whole(rows), whole(rows), local, local, local, whole(rows), whole(BLOCK), section_spec, square, whole(rank)]
    args = [tokens, *moved, cotangent, diag, section, latent, up]
    if held is not None:
        in_specs.append(pl.BlockSpec(memory_space=pl.ANY))
        args.append(held)
    return pl.pallas_call(
        main_kernel,
        grid=(steps,),
        in_specs=in_specs,
        out_specs=[local, square, pl.BlockSpec((MAIN_STEP // CHUNK, 1, grad_rows, CHUNK), lambda i: (i, part, 0, 0))],
        out_shape=[
            jax.ShapeDtypeStruct((rows, width), BF16),
            jax.ShapeDtypeStruct((rows, rank), F32),
            jax.ShapeDtypeStruct((RING, 2, grad_rows, CHUNK), BF16),
        ],
        input_output_aliases={} if held is None else {10: 2},
        compiler_params=pltpu.CompilerParams(vmem_limit_bytes=VMEM),
        cost_estimate=pl.CostEstimate(flops=2_000_000_000, bytes_accessed=28 << 20, transcendentals=0),
        name="main_part",
    )(*args)


def pick_half(low, high):
    first = pl.program_id(0) < pl.num_programs(0) // 2
    return jnp.where(first, low[...], high[...])


def half_specs(rows, steps):
    half = steps // 2
    return [
        pl.BlockSpec((rows, FINAL_STEP), lambda i: (0, jnp.minimum(i, half - 1))),
        pl.BlockSpec((rows, FINAL_STEP), lambda i: (0, jnp.maximum(i - half, 0))),
    ]


def back_kernel(low, high, sec, b1, *halves):
    mask = block_mask()

    def fill(slope, outs):
        for c in range(slope.shape[1] // CHUNK):
            cs = slice(c * CHUNK, (c + 1) * CHUNK)
            for b, out in enumerate(outs):
                out[:, cs] = dot(slope[:, cs], spread(sec[b, :, cs], mask), 1, 1).astype(BF16)

    pl.when(pl.program_id(0) == 0)(lambda: fill(low, (b1, *halves[0::2])))
    pl.when(pl.program_id(0) == 1)(lambda: fill(high, (b1, *halves[1::2])))


def run_back(slopes, section):
    rows, half = slopes[0].shape
    fixed = pl.BlockSpec((rows, half), lambda i: (0, 0))
    moving = pl.BlockSpec((rows, half), lambda i: (0, i))
    return pl.pallas_call(
        back_kernel,
        grid=(2,),
        in_specs=[fixed, fixed, pl.BlockSpec((4, BLOCK, half), lambda i: (0, 0, i))],
        out_specs=[moving] + [fixed] * 6,
        out_shape=[jax.ShapeDtypeStruct((rows, 2 * half), BF16)] + [jax.ShapeDtypeStruct((rows, half), BF16)] * 6,
        compiler_params=pltpu.CompilerParams(vmem_limit_bytes=VMEM),
        cost_estimate=pl.CostEstimate(flops=2_000_000_000, bytes_accessed=20 << 20, transcendentals=0),
        name="back_products",
    )(*slopes, section)


def down_kernel(side, tok, others, lat, lat_others, out):
    both = jnp.concatenate([lat[...], lat_others[...]], axis=0)
    for c in range(tok.shape[1] // CHUNK):
        cs = slice(c * CHUNK, (c + 1) * CHUNK)
        out[c] = dot(both, jnp.concatenate([tok[:, cs], others[:, cs]], axis=0), 0, 0).astype(BF16)


def run_down(x, tokens, others, latent_grad, latent_others):
    rows, half = others.shape
    rank = latent_grad.shape[1]
    step = half // 2
    square = pl.BlockSpec((rows, rank), lambda i, side: (0, 0))
    return pl.pallas_call(
        down_kernel,
        grid_spec=pltpu.PrefetchScalarGridSpec(
            num_scalar_prefetch=1,
            grid=(2,),
            in_specs=[
                pl.BlockSpec((rows, step), lambda i, side: (0, 2 * side[0] + i)),
                pl.BlockSpec((rows, step), lambda i, side: (0, i)),
                square,
                square,
            ],
            out_specs=pl.BlockSpec((RING // 2, rank, CHUNK), lambda i, side: (i, 0, 0)),
        ),
        out_shape=jax.ShapeDtypeStruct((RING, rank, CHUNK), BF16),
        cost_estimate=pl.CostEstimate(flops=300_000_000, bytes_accessed=10 << 20, transcendentals=0),
        name="down_part",
    )(jnp.full((1,), x, jnp.int32), tokens, others, latent_grad, latent_others)


def final_kernel(*refs):
    pairs, (r1, diag, down, lat, out) = refs[:6], refs[6:]
    mask = block_mask()
    slope, r2, r48 = (pick_half(pairs[2 * k], pairs[2 * k + 1]) for k in range(3))
    for c in range(FINAL_STEP // CHUNK):
        cs = slice(c * CHUNK, (c + 1) * CHUNK)
        total = dot(slope[:, cs], spread(diag[:, cs], mask), 1, 1)
        total = total + dot(lat[...], down[cs, :], 1, 1)
        for value in (r1, r2, r48):
            total = total + value[:, cs].astype(F32)
        out[:, cs] = total.astype(BF16)


def run_final(pairs, r1, diag, low_down, latent_grad):
    rows, half_width = pairs[0][0].shape
    width = 2 * half_width
    rank = latent_grad.shape[1]
    steps = width // FINAL_STEP
    col = lambda r: pl.BlockSpec((r, FINAL_STEP), lambda i: (0, i))
    return pl.pallas_call(
        final_kernel,
        grid=(steps,),
        in_specs=half_specs(rows, steps) * 3
        + [
            col(rows),
            col(BLOCK),
            pl.BlockSpec((FINAL_STEP, rank), lambda i: (i, 0)),
            pl.BlockSpec((rows, rank), lambda i: (0, 0)),
        ],
        out_specs=col(rows),
        out_shape=jax.ShapeDtypeStruct((rows, width), BF16),
        compiler_params=pltpu.CompilerParams(vmem_limit_bytes=VMEM),
        cost_estimate=pl.CostEstimate(flops=2_000_000_000, bytes_accessed=17 << 20, transcendentals=0),
        name="token_grad",
    )(*[value for pair in pairs for value in pair], r1, diag, low_down, latent_grad)


def finish_kernel(scale, side, summed, arrived, diag, section, up):
    total = (summed[0].astype(F32) + arrived[...].astype(F32)) * scale
    diag[...] = total[:BLOCK]
    for b in range(4):
        section[b] = total[(b + 1) * BLOCK : (b + 2) * BLOCK]
    up[...] = total[5 * BLOCK :]


def run_finish(x, summed, arrived, scale):
    _, rows, width = summed.shape
    rank = rows - 5 * BLOCK
    return pl.pallas_call(
        functools.partial(finish_kernel, scale),
        grid_spec=pltpu.PrefetchScalarGridSpec(
            num_scalar_prefetch=1,
            grid=(1,),
            in_specs=[
                pl.BlockSpec((1, rows, width), lambda i, side: (side[0], 0, 0)),
                pl.BlockSpec((rows, width), lambda i, side: (0, 0)),
            ],
            out_specs=[
                pl.BlockSpec((BLOCK, width), lambda i, side: (0, 0)),
                pl.BlockSpec((4, BLOCK, width), lambda i, side: (0, 0, 0)),
                pl.BlockSpec((rank, width), lambda i, side: (0, 0)),
            ],
        ),
        out_shape=[
            jax.ShapeDtypeStruct((BLOCK, width), F32),
            jax.ShapeDtypeStruct((4, BLOCK, width), F32),
            jax.ShapeDtypeStruct((rank, width), F32),
        ],
        cost_estimate=pl.CostEstimate(flops=300_000, bytes_accessed=4 << 20, transcendentals=0),
        name="finish",
    )(jnp.full((1,), x, jnp.int32), summed, arrived)


def flip(value, mask):
    return lax.ppermute(value, "tensor", [(i, i ^ mask) for i in range(16)])


def after(value, *events):
    return lax.optimization_barrier((value, *events))[0]


def ring_sum(grads):
    ring, sides, rows, width = grads.shape
    groups = [[x * RING + z for z in range(RING)] for x in range(2)]
    total = lax.psum_scatter(
        grads.reshape(ring * sides * rows, width), "dp", scatter_dimension=0, axis_index_groups=groups, tiled=True
    )
    return total.reshape(sides, rows, width)


def cross(value):
    return lax.ppermute(value, "dp", [(i, i ^ RING) for i in range(2 * RING)])


def per_device(tokens, cotangent, diag_factor, section_factors, low_down, low_up):
    rows, width = tokens.shape
    scale = (rows * lax.axis_size("dp")) ** -0.5
    x = lax.axis_index("dp") // RING
    half = width // 2

    h0 = tokens[:, :half]
    m4_0, m2_0 = flip(h0, 4), flip(h0, 2)
    m1 = flip(tokens, 1)
    part = jnp.dot(tokens, low_down, preferred_element_type=F32)
    part = part + flip(part, 12)
    h1 = after(tokens, part)[:, half:]
    part = part + flip(part, 4)
    m8_0 = flip(after(m4_0, part), 12)
    m4_1 = flip(after(h1, m4_0, part), 4)
    part = part + flip(part, 2)
    m2_1 = flip(after(h1, m2_0, part), 2)
    m8_1 = flip(m4_1, 12)
    part = part + flip(part, 1)
    latent = part.astype(BF16)
    others = cross(lax.dynamic_slice_in_dim(after(tokens, m2_1), (1 - x) * half, half, axis=1))

    factors = (cotangent, diag_factor, section_factors, latent, low_up)
    slope0, lat0, grads = run_main(0, tokens, (m1, m2_0, m4_0, m8_0), *factors, None)
    slope1, lat1, grads = run_main(1, tokens, (m1, m2_1, m4_1, m8_1), *factors, grads)
    summed = ring_sum(grads)

    part = lat0 + lat1
    arrived = flip(part, 12)
    b1, b2_0, b2_1, b4_0, b4_1, b8_0, b8_1 = run_back((slope0, slope1), section_factors)
    part = part + after(arrived, b1, others)
    q0, q1 = flip(after(b8_0, part), 12), flip(after(b8_1, part), 12)
    part = part + flip(part, 2)
    r2_0, r1 = flip(after(b2_0, part), 2), flip(after(b1, part), 1)
    part = part + flip(part, 4)
    part = part + after(flip(part, 1), r1)
    latent_grad = part.astype(BF16)

    pair = run_down(x, tokens, others, latent_grad, after(cross(latent_grad), r2_0))
    s0 = flip(b4_0 + after(q0, pair), 4)
    r2_1 = flip(after(b2_1, pair), 2)
    pair = after(pair, q0)
    groups = [[side * RING + z for z in range(RING)] for side in range(2)]
    pair = lax.all_to_all(pair, "dp", 0, 0, axis_index_groups=groups, tiled=True)
    s1 = flip(b4_1 + q1, 4)
    other = lax.dynamic_index_in_dim(summed, 1 - x, 0, keepdims=False)
    arrived = cross(other)
    down_grad = (jnp.sum(after(pair, arrived).astype(F32), axis=0) * scale).T
    pairs = ((slope0, slope1), (r2_0, r2_1), (s0, after(s1, other)))
    token_grad = run_final(pairs, r1, diag_factor, low_down, latent_grad)
    diag_grad, section_grad, up_grad = run_finish(x, summed, arrived, scale)
    return token_grad, diag_grad, section_grad, down_grad, up_grad


def solution(mesh):
    placed = (
        P("dp", "tensor"),
        P("dp", "tensor"),
        P(None, "tensor"),
        P(None, None, "tensor"),
        P("tensor", None),
        P(None, "tensor"),
    )
    return jax.shard_map(
        per_device,
        mesh=mesh,
        in_specs=placed,
        out_specs=(
            P("dp", "tensor"),
            P(None, ("tensor", "dp")),
            P(None, None, ("tensor", "dp")),
            P(("tensor", "dp"), None),
            P(None, ("tensor", "dp")),
        ),
        check_vma=False,
    )
```

```python
import functools

import jax
import jax.numpy as jnp
from jax import lax
from jax.experimental import pallas as pl
from jax.experimental.pallas import tpu as pltpu
from jax.sharding import PartitionSpec as P

BLOCK = 64
CHUNK = 256
MAIN_STEP, FINAL_STEP = 512, 2048
RING = 8
VMEM = 62 << 20
F32 = jnp.float32
BF16 = jnp.bfloat16


def dot(a, b, ca, cb):
    return lax.dot_general(a, b, (((ca,), (cb,)), ((), ())), preferred_element_type=F32)


def gelu_slope(values):
    return (
        0.5 * (1.0 + lax.erf(values * 0.7071067811865476))
        + values * jnp.exp(-0.5 * values * values) * 0.3989422804014327
    )


def block_mask():
    row = lax.broadcasted_iota(jnp.int32, (CHUNK, CHUNK), 0) // BLOCK
    col = lax.broadcasted_iota(jnp.int32, (CHUNK, CHUNK), 1) // BLOCK
    return row == col


def spread(factor, mask):
    tall = jnp.concatenate([factor] * (CHUNK // BLOCK), axis=0)
    return jnp.where(mask, tall, jnp.zeros_like(tall))


def main_kernel(tok, m1, m2, m4, m8, cot, diag, sec, latent, up, *refs):
    slope_out, lat_out, grads = refs[-3:]
    mask = block_mask()
    lat = latent[...]
    group = CHUNK // BLOCK
    lat_sum = jnp.zeros((lat.shape[0], up.shape[0]), F32)
    for c in range(MAIN_STEP // CHUNK):
        cs = slice(c * CHUNK, (c + 1) * CHUNK)
        up_c = up[:, cs]
        sides = [tok[:, cs], m1[:, cs], m2[:, cs], m4[:, cs], m8[:, cs]]
        factors = [spread(diag[:, cs], mask)] + [spread(sec[b, :, cs], mask) for b in range(4)]
        left = jnp.concatenate(sides + [lat], axis=1)
        right = jnp.concatenate(factors + [up_c], axis=0)
        pre = dot(left, right, 1, 0)
        slope = (cot[:, cs].astype(F32) * gelu_slope(pre)).astype(BF16)
        slope_out[:, cs] = slope
        lat_sum = lat_sum + dot(slope, up_c, 1, 1)
        for k, side in enumerate(sides):
            full = dot(side, slope, 0, 0)
            kept = jnp.where(mask, full, jnp.zeros_like(full))
            part = sum(kept[i * BLOCK : (i + 1) * BLOCK] for i in range(group))
            grads[c, 0, k * BLOCK : (k + 1) * BLOCK, :] = part.astype(BF16)
        grads[c, 0, 5 * BLOCK :, :] = dot(lat, slope, 0, 0).astype(BF16)

    @pl.when(pl.program_id(0) == 0)
    def _():
        lat_out[...] = lat_sum

    @pl.when(pl.program_id(0) > 0)
    def _():
        lat_out[...] += lat_sum


def run_main(part, tokens, moved, cotangent, diag, section, latent, up, held):
    rows, width = moved[2].shape
    rank = up.shape[0]
    steps = width // MAIN_STEP
    base = part * steps
    whole = lambda r: pl.BlockSpec((r, MAIN_STEP), lambda i: (0, base + i))
    local = pl.BlockSpec((rows, MAIN_STEP), lambda i: (0, i))
    square = pl.BlockSpec((rows, rank), lambda i: (0, 0))
    section_spec = pl.BlockSpec((4, BLOCK, MAIN_STEP), lambda i: (0, 0, base + i))
    grad_rows = 5 * BLOCK + rank
    in_specs = [whole(rows), whole(rows), local, local, local, whole(rows), whole(BLOCK), section_spec, square, whole(rank)]
    args = [tokens, *moved, cotangent, diag, section, latent, up]
    if held is not None:
        in_specs.append(pl.BlockSpec(memory_space=pl.ANY))
        args.append(held)
    return pl.pallas_call(
        main_kernel,
        grid=(steps,),
        in_specs=in_specs,
        out_specs=[local, square, pl.BlockSpec((MAIN_STEP // CHUNK, 1, grad_rows, CHUNK), lambda i: (i, part, 0, 0))],
        out_shape=[
            jax.ShapeDtypeStruct((rows, width), BF16),
            jax.ShapeDtypeStruct((rows, rank), F32),
            jax.ShapeDtypeStruct((RING, 2, grad_rows, CHUNK), BF16),
        ],
        input_output_aliases={} if held is None else {10: 2},
        compiler_params=pltpu.CompilerParams(vmem_limit_bytes=VMEM),
        cost_estimate=pl.CostEstimate(flops=2_000_000_000, bytes_accessed=28 << 20, transcendentals=0),
        name="main_part",
    )(*args)


def pick_half(low, high):
    first = pl.program_id(0) < pl.num_programs(0) // 2
    return jnp.where(first, low[...], high[...])


def half_specs(rows, steps):
    half = steps // 2
    return [
        pl.BlockSpec((rows, FINAL_STEP), lambda i: (0, jnp.minimum(i, half - 1))),
        pl.BlockSpec((rows, FINAL_STEP), lambda i: (0, jnp.maximum(i - half, 0))),
    ]


def back_kernel(low, high, sec, b1, *halves):
    mask = block_mask()

    def fill(slope, outs):
        for c in range(slope.shape[1] // CHUNK):
            cs = slice(c * CHUNK, (c + 1) * CHUNK)
            for b, out in enumerate(outs):
                out[:, cs] = dot(slope[:, cs], spread(sec[b, :, cs], mask), 1, 1).astype(BF16)

    pl.when(pl.program_id(0) == 0)(lambda: fill(low, (b1, *halves[0::2])))
    pl.when(pl.program_id(0) == 1)(lambda: fill(high, (b1, *halves[1::2])))


def run_back(slopes, section):
    rows, half = slopes[0].shape
    fixed = pl.BlockSpec((rows, half), lambda i: (0, 0))
    moving = pl.BlockSpec((rows, half), lambda i: (0, i))
    return pl.pallas_call(
        back_kernel,
        grid=(2,),
        in_specs=[fixed, fixed, pl.BlockSpec((4, BLOCK, half), lambda i: (0, 0, i))],
        out_specs=[moving] + [fixed] * 6,
        out_shape=[jax.ShapeDtypeStruct((rows, 2 * half), BF16)] + [jax.ShapeDtypeStruct((rows, half), BF16)] * 6,
        compiler_params=pltpu.CompilerParams(vmem_limit_bytes=VMEM),
        cost_estimate=pl.CostEstimate(flops=2_000_000_000, bytes_accessed=20 << 20, transcendentals=0),
        name="back_products",
    )(*slopes, section)


def down_kernel(side, tok, others, lat, lat_others, out):
    both = jnp.concatenate([lat[...], lat_others[...]], axis=0)
    for c in range(tok.shape[1] // CHUNK):
        cs = slice(c * CHUNK, (c + 1) * CHUNK)
        out[c] = dot(both, jnp.concatenate([tok[:, cs], others[:, cs]], axis=0), 0, 0).astype(BF16)


def run_down(x, tokens, others, latent_grad, latent_others):
    rows, half = others.shape
    rank = latent_grad.shape[1]
    step = half // 2
    square = pl.BlockSpec((rows, rank), lambda i, side: (0, 0))
    return pl.pallas_call(
        down_kernel,
        grid_spec=pltpu.PrefetchScalarGridSpec(
            num_scalar_prefetch=1,
            grid=(2,),
            in_specs=[
                pl.BlockSpec((rows, step), lambda i, side: (0, 2 * side[0] + i)),
                pl.BlockSpec((rows, step), lambda i, side: (0, i)),
                square,
                square,
            ],
            out_specs=pl.BlockSpec((RING // 2, rank, CHUNK), lambda i, side: (i, 0, 0)),
        ),
        out_shape=jax.ShapeDtypeStruct((RING, rank, CHUNK), BF16),
        cost_estimate=pl.CostEstimate(flops=300_000_000, bytes_accessed=10 << 20, transcendentals=0),
        name="down_part",
    )(jnp.full((1,), x, jnp.int32), tokens, others, latent_grad, latent_others)


def final_kernel(*refs):
    pairs, (r1, diag, down, lat, out) = refs[:6], refs[6:]
    mask = block_mask()
    slope, r2, r48 = (pick_half(pairs[2 * k], pairs[2 * k + 1]) for k in range(3))
    for c in range(FINAL_STEP // CHUNK):
        cs = slice(c * CHUNK, (c + 1) * CHUNK)
        total = dot(slope[:, cs], spread(diag[:, cs], mask), 1, 1)
        total = total + dot(lat[...], down[cs, :], 1, 1)
        for value in (r1, r2, r48):
            total = total + value[:, cs].astype(F32)
        out[:, cs] = total.astype(BF16)


def run_final(pairs, r1, diag, low_down, latent_grad):
    rows, half_width = pairs[0][0].shape
    width = 2 * half_width
    rank = latent_grad.shape[1]
    steps = width // FINAL_STEP
    col = lambda r: pl.BlockSpec((r, FINAL_STEP), lambda i: (0, i))
    return pl.pallas_call(
        final_kernel,
        grid=(steps,),
        in_specs=half_specs(rows, steps) * 3
        + [
            col(rows),
            col(BLOCK),
            pl.BlockSpec((FINAL_STEP, rank), lambda i: (i, 0)),
            pl.BlockSpec((rows, rank), lambda i: (0, 0)),
        ],
        out_specs=col(rows),
        out_shape=jax.ShapeDtypeStruct((rows, width), BF16),
        compiler_params=pltpu.CompilerParams(vmem_limit_bytes=VMEM),
        cost_estimate=pl.CostEstimate(flops=2_000_000_000, bytes_accessed=17 << 20, transcendentals=0),
        name="token_grad",
    )(*[value for pair in pairs for value in pair], r1, diag, low_down, latent_grad)


def finish_kernel(scale, side, summed, arrived, diag, section, up):
    total = (summed[0].astype(F32) + arrived[...].astype(F32)) * scale
    diag[...] = total[:BLOCK]
    for b in range(4):
        section[b] = total[(b + 1) * BLOCK : (b + 2) * BLOCK]
    up[...] = total[5 * BLOCK :]


def run_finish(x, summed, arrived, scale):
    _, rows, width = summed.shape
    rank = rows - 5 * BLOCK
    return pl.pallas_call(
        functools.partial(finish_kernel, scale),
        grid_spec=pltpu.PrefetchScalarGridSpec(
            num_scalar_prefetch=1,
            grid=(1,),
            in_specs=[
                pl.BlockSpec((1, rows, width), lambda i, side: (side[0], 0, 0)),
                pl.BlockSpec((rows, width), lambda i, side: (0, 0)),
            ],
            out_specs=[
                pl.BlockSpec((BLOCK, width), lambda i, side: (0, 0)),
                pl.BlockSpec((4, BLOCK, width), lambda i, side: (0, 0, 0)),
                pl.BlockSpec((rank, width), lambda i, side: (0, 0)),
            ],
        ),
        out_shape=[
            jax.ShapeDtypeStruct((BLOCK, width), F32),
            jax.ShapeDtypeStruct((4, BLOCK, width), F32),
            jax.ShapeDtypeStruct((rank, width), F32),
        ],
        cost_estimate=pl.CostEstimate(flops=300_000, bytes_accessed=4 << 20, transcendentals=0),
        name="finish",
    )(jnp.full((1,), x, jnp.int32), summed, arrived)


def flip(value, mask):
    return lax.ppermute(value, "tensor", [(i, i ^ mask) for i in range(16)])


def after(value, *events):
    return lax.optimization_barrier((value, *events))[0]


def ring_sum(grads):
    ring, sides, rows, width = grads.shape
    groups = [[x * RING + z for z in range(RING)] for x in range(2)]
    total = lax.psum_scatter(
        grads.reshape(ring * sides * rows, width), "dp", scatter_dimension=0, axis_index_groups=groups, tiled=True
    )
    return total.reshape(sides, rows, width)


def cross(value):
    return lax.ppermute(value, "dp", [(i, i ^ RING) for i in range(2 * RING)])


def per_device(tokens, cotangent, diag_factor, section_factors, low_down, low_up):
    rows, width = tokens.shape
    scale = (rows * lax.axis_size("dp")) ** -0.5
    x = lax.axis_index("dp") // RING
    half = width // 2

    h0 = tokens[:, :half]
    m4_0, m2_0 = flip(h0, 4), flip(h0, 2)
    m1 = flip(tokens, 1)
    part = jnp.dot(tokens, low_down, preferred_element_type=F32)
    part = part + flip(part, 12)
    h1 = after(tokens, part)[:, half:]
    part = part + flip(part, 4)
    m8_0 = flip(after(m4_0, part), 12)
    m4_1 = flip(after(h1, m4_0, part), 4)
    part = part + flip(part, 2)
    m2_1 = flip(after(h1, m2_0, part), 2)
    m8_1 = flip(m4_1, 12)
    part = part + flip(part, 1)
    latent = part.astype(BF16)
    others = cross(lax.dynamic_slice_in_dim(after(tokens, m2_1), (1 - x) * half, half, axis=1))

    factors = (cotangent, diag_factor, section_factors, latent, low_up)
    slope0, lat0, grads = run_main(0, tokens, (m1, m2_0, m4_0, m8_0), *factors, None)
    slope1, lat1, grads = run_main(1, tokens, (m1, m2_1, m4_1, m8_1), *factors, grads)
    summed = ring_sum(grads)

    part = lat0 + lat1
    arrived = flip(part, 12)
    b1, b2_0, b2_1, b4_0, b4_1, b8_0, b8_1 = run_back((slope0, slope1), section_factors)
    part = part + after(arrived, b1, others)
    q0, q1 = flip(after(b8_0, part), 12), flip(after(b8_1, part), 12)
    part = part + flip(part, 4)
    s0 = flip(b4_0 + after(q0, part), 4)
    part = part + flip(part, 2)
    r2_0, r1 = flip(after(b2_0, part), 2), flip(after(b1, part), 1)
    part = part + after(flip(part, 1), r1)
    latent_grad = part.astype(BF16)

    pair = run_down(x, tokens, others, latent_grad, after(cross(latent_grad), r2_0, s0, q1))
    r2_1 = flip(after(b2_1, pair), 2)
    groups = [[side * RING + z for z in range(RING)] for side in range(2)]
    pair = lax.all_to_all(pair, "dp", 0, 0, axis_index_groups=groups, tiled=True)
    s1 = flip(b4_1 + q1, 4)
    other = lax.dynamic_index_in_dim(summed, 1 - x, 0, keepdims=False)
    arrived = cross(other)
    down_grad = (jnp.sum(after(pair, arrived).astype(F32), axis=0) * scale).T
    pairs = ((slope0, slope1), (r2_0, r2_1), (s0, after(s1, other)))
    token_grad = run_final(pairs, r1, diag_factor, low_down, latent_grad)
    diag_grad, section_grad, up_grad = run_finish(x, summed, arrived, scale)
    return token_grad, diag_grad, section_grad, down_grad, up_grad


def solution(mesh):
    placed = (
        P("dp", "tensor"),
        P("dp", "tensor"),
        P(None, "tensor"),
        P(None, None, "tensor"),
        P("tensor", None),
        P(None, "tensor"),
    )
    return jax.shard_map(
        per_device,
        mesh=mesh,
        in_specs=placed,
        out_specs=(
            P("dp", "tensor"),
            P(None, ("tensor", "dp")),
            P(None, None, ("tensor", "dp")),
            P(("tensor", "dp"), None),
            P(None, ("tensor", "dp")),
        ),
        check_vma=False,
    )
```

```python
import functools

import jax
import jax.numpy as jnp
from jax import lax
from jax.experimental import pallas as pl
from jax.experimental.pallas import tpu as pltpu
from jax.sharding import PartitionSpec as P

BLOCK = 64
CHUNK = 256
MAIN_STEP, FINAL_STEP = 512, 2048
RING = 8
VMEM = 62 << 20
F32 = jnp.float32
BF16 = jnp.bfloat16


def dot(a, b, ca, cb):
    return lax.dot_general(a, b, (((ca,), (cb,)), ((), ())), preferred_element_type=F32)


def gelu_slope(values):
    return (
        0.5 * (1.0 + lax.erf(values * 0.7071067811865476))
        + values * jnp.exp(-0.5 * values * values) * 0.3989422804014327
    )


def block_mask():
    row = lax.broadcasted_iota(jnp.int32, (CHUNK, CHUNK), 0) // BLOCK
    col = lax.broadcasted_iota(jnp.int32, (CHUNK, CHUNK), 1) // BLOCK
    return row == col


def spread(factor, mask):
    tall = jnp.concatenate([factor] * (CHUNK // BLOCK), axis=0)
    return jnp.where(mask, tall, jnp.zeros_like(tall))


def main_kernel(tok, m1, m2, m4, m8, cot, diag, sec, latent, up, *refs):
    slope_out, lat_out, grads = refs[-3:]
    mask = block_mask()
    lat = latent[...]
    group = CHUNK // BLOCK
    lat_sum = jnp.zeros((lat.shape[0], up.shape[0]), F32)
    for c in range(MAIN_STEP // CHUNK):
        cs = slice(c * CHUNK, (c + 1) * CHUNK)
        up_c = up[:, cs]
        sides = [tok[:, cs], m1[:, cs], m2[:, cs], m4[:, cs], m8[:, cs]]
        factors = [spread(diag[:, cs], mask)] + [spread(sec[b, :, cs], mask) for b in range(4)]
        left = jnp.concatenate(sides + [lat], axis=1)
        right = jnp.concatenate(factors + [up_c], axis=0)
        pre = dot(left, right, 1, 0)
        slope = (cot[:, cs].astype(F32) * gelu_slope(pre)).astype(BF16)
        slope_out[:, cs] = slope
        lat_sum = lat_sum + dot(slope, up_c, 1, 1)
        for k, side in enumerate(sides):
            full = dot(side, slope, 0, 0)
            kept = jnp.where(mask, full, jnp.zeros_like(full))
            part = sum(kept[i * BLOCK : (i + 1) * BLOCK] for i in range(group))
            grads[c, 0, k * BLOCK : (k + 1) * BLOCK, :] = part.astype(BF16)
        grads[c, 0, 5 * BLOCK :, :] = dot(lat, slope, 0, 0).astype(BF16)

    @pl.when(pl.program_id(0) == 0)
    def _():
        lat_out[...] = lat_sum

    @pl.when(pl.program_id(0) > 0)
    def _():
        lat_out[...] += lat_sum


def run_main(part, tokens, moved, cotangent, diag, section, latent, up, held):
    rows, width = moved[2].shape
    rank = up.shape[0]
    steps = width // MAIN_STEP
    base = part * steps
    whole = lambda r: pl.BlockSpec((r, MAIN_STEP), lambda i: (0, base + i))
    local = pl.BlockSpec((rows, MAIN_STEP), lambda i: (0, i))
    square = pl.BlockSpec((rows, rank), lambda i: (0, 0))
    section_spec = pl.BlockSpec((4, BLOCK, MAIN_STEP), lambda i: (0, 0, base + i))
    grad_rows = 5 * BLOCK + rank
    in_specs = [whole(rows), whole(rows), local, local, local, whole(rows), whole(BLOCK), section_spec, square, whole(rank)]
    args = [tokens, *moved, cotangent, diag, section, latent, up]
    if held is not None:
        in_specs.append(pl.BlockSpec(memory_space=pl.ANY))
        args.append(held)
    return pl.pallas_call(
        main_kernel,
        grid=(steps,),
        in_specs=in_specs,
        out_specs=[local, square, pl.BlockSpec((MAIN_STEP // CHUNK, 1, grad_rows, CHUNK), lambda i: (i, part, 0, 0))],
        out_shape=[
            jax.ShapeDtypeStruct((rows, width), BF16),
            jax.ShapeDtypeStruct((rows, rank), F32),
            jax.ShapeDtypeStruct((RING, 2, grad_rows, CHUNK), BF16),
        ],
        input_output_aliases={} if held is None else {10: 2},
        compiler_params=pltpu.CompilerParams(vmem_limit_bytes=VMEM),
        cost_estimate=pl.CostEstimate(flops=2_000_000_000, bytes_accessed=28 << 20, transcendentals=0),
        name="main_part",
    )(*args)


def pick_half(low, high):
    first = pl.program_id(0) < pl.num_programs(0) // 2
    return jnp.where(first, low[...], high[...])


def half_specs(rows, steps):
    half = steps // 2
    return [
        pl.BlockSpec((rows, FINAL_STEP), lambda i: (0, jnp.minimum(i, half - 1))),
        pl.BlockSpec((rows, FINAL_STEP), lambda i: (0, jnp.maximum(i - half, 0))),
    ]


def back_kernel(low, high, sec, b1, *halves):
    mask = block_mask()

    def fill(slope, outs):
        for c in range(slope.shape[1] // CHUNK):
            cs = slice(c * CHUNK, (c + 1) * CHUNK)
            for b, out in enumerate(outs):
                out[:, cs] = dot(slope[:, cs], spread(sec[b, :, cs], mask), 1, 1).astype(BF16)

    pl.when(pl.program_id(0) == 0)(lambda: fill(low, (b1, *halves[0::2])))
    pl.when(pl.program_id(0) == 1)(lambda: fill(high, (b1, *halves[1::2])))


def run_back(slopes, section):
    rows, half = slopes[0].shape
    fixed = pl.BlockSpec((rows, half), lambda i: (0, 0))
    moving = pl.BlockSpec((rows, half), lambda i: (0, i))
    return pl.pallas_call(
        back_kernel,
        grid=(2,),
        in_specs=[fixed, fixed, pl.BlockSpec((4, BLOCK, half), lambda i: (0, 0, i))],
        out_specs=[moving] + [fixed] * 6,
        out_shape=[jax.ShapeDtypeStruct((rows, 2 * half), BF16)] + [jax.ShapeDtypeStruct((rows, half), BF16)] * 6,
        compiler_params=pltpu.CompilerParams(vmem_limit_bytes=VMEM),
        cost_estimate=pl.CostEstimate(flops=2_000_000_000, bytes_accessed=20 << 20, transcendentals=0),
        name="back_products",
    )(*slopes, section)


def down_kernel(place, tok, others, lat, lat_others, out):
    both = jnp.concatenate([lat[...], lat_others[...]], axis=0)
    count = tok.shape[1] // CHUNK
    for c in range(count):
        cs = slice(c * CHUNK, (c + 1) * CHUNK)
        bits = (pl.program_id(0) * count + c) ^ place[1]
        slot = (bits & 1) * 4 + (bits & 2) + bits // 4
        out[slot] = dot(both, jnp.concatenate([tok[:, cs], others[:, cs]], axis=0), 0, 0).astype(BF16)


def run_down(x, z, tokens, others, latent_grad, latent_others):
    rows, half = others.shape
    rank = latent_grad.shape[1]
    step = half // 2
    square = pl.BlockSpec((rows, rank), lambda i, place: (0, 0))
    return pl.pallas_call(
        down_kernel,
        grid_spec=pltpu.PrefetchScalarGridSpec(
            num_scalar_prefetch=1,
            grid=(2,),
            in_specs=[
                pl.BlockSpec((rows, step), lambda i, place: (0, 2 * place[0] + i)),
                pl.BlockSpec((rows, step), lambda i, place: (0, i)),
                square,
                square,
            ],
            out_specs=pl.BlockSpec((RING, rank, CHUNK), lambda i, place: (0, 0, 0)),
        ),
        out_shape=jax.ShapeDtypeStruct((RING, rank, CHUNK), BF16),
        cost_estimate=pl.CostEstimate(flops=300_000_000, bytes_accessed=10 << 20, transcendentals=0),
        name="down_part",
    )(jnp.stack([x, z]).astype(jnp.int32), tokens, others, latent_grad, latent_others)


def final_kernel(*refs):
    pairs, (r1, diag, down, lat, out) = refs[:6], refs[6:]
    mask = block_mask()
    slope, r2, r48 = (pick_half(pairs[2 * k], pairs[2 * k + 1]) for k in range(3))
    for c in range(FINAL_STEP // CHUNK):
        cs = slice(c * CHUNK, (c + 1) * CHUNK)
        total = dot(slope[:, cs], spread(diag[:, cs], mask), 1, 1)
        total = total + dot(lat[...], down[cs, :], 1, 1)
        for value in (r1, r2, r48):
            total = total + value[:, cs].astype(F32)
        out[:, cs] = total.astype(BF16)


def run_final(pairs, r1, diag, low_down, latent_grad):
    rows, half_width = pairs[0][0].shape
    width = 2 * half_width
    rank = latent_grad.shape[1]
    steps = width // FINAL_STEP
    col = lambda r: pl.BlockSpec((r, FINAL_STEP), lambda i: (0, i))
    return pl.pallas_call(
        final_kernel,
        grid=(steps,),
        in_specs=half_specs(rows, steps) * 3
        + [
            col(rows),
            col(BLOCK),
            pl.BlockSpec((FINAL_STEP, rank), lambda i: (i, 0)),
            pl.BlockSpec((rows, rank), lambda i: (0, 0)),
        ],
        out_specs=col(rows),
        out_shape=jax.ShapeDtypeStruct((rows, width), BF16),
        compiler_params=pltpu.CompilerParams(vmem_limit_bytes=VMEM),
        cost_estimate=pl.CostEstimate(flops=2_000_000_000, bytes_accessed=17 << 20, transcendentals=0),
        name="token_grad",
    )(*[value for pair in pairs for value in pair], r1, diag, low_down, latent_grad)


def finish_kernel(scale, side, summed, arrived, diag, section, up):
    total = (summed[0].astype(F32) + arrived[...].astype(F32)) * scale
    diag[...] = total[:BLOCK]
    for b in range(4):
        section[b] = total[(b + 1) * BLOCK : (b + 2) * BLOCK]
    up[...] = total[5 * BLOCK :]


def run_finish(x, summed, arrived, scale):
    _, rows, width = summed.shape
    rank = rows - 5 * BLOCK
    return pl.pallas_call(
        functools.partial(finish_kernel, scale),
        grid_spec=pltpu.PrefetchScalarGridSpec(
            num_scalar_prefetch=1,
            grid=(1,),
            in_specs=[
                pl.BlockSpec((1, rows, width), lambda i, side: (side[0], 0, 0)),
                pl.BlockSpec((rows, width), lambda i, side: (0, 0)),
            ],
            out_specs=[
                pl.BlockSpec((BLOCK, width), lambda i, side: (0, 0)),
                pl.BlockSpec((4, BLOCK, width), lambda i, side: (0, 0, 0)),
                pl.BlockSpec((rank, width), lambda i, side: (0, 0)),
            ],
        ),
        out_shape=[
            jax.ShapeDtypeStruct((BLOCK, width), F32),
            jax.ShapeDtypeStruct((4, BLOCK, width), F32),
            jax.ShapeDtypeStruct((rank, width), F32),
        ],
        cost_estimate=pl.CostEstimate(flops=300_000, bytes_accessed=4 << 20, transcendentals=0),
        name="finish",
    )(jnp.full((1,), x, jnp.int32), summed, arrived)


def flip(value, mask):
    return lax.ppermute(value, "tensor", [(i, i ^ mask) for i in range(16)])


def after(value, *events):
    return lax.optimization_barrier((value, *events))[0]


def ring_sum(grads):
    ring, sides, rows, width = grads.shape
    groups = [[x * RING + z for z in range(RING)] for x in range(2)]
    total = lax.psum_scatter(
        grads.reshape(ring * sides * rows, width), "dp", scatter_dimension=0, axis_index_groups=groups, tiled=True
    )
    return total.reshape(sides, rows, width)


def cross(value):
    return lax.ppermute(value, "dp", [(i, i ^ RING) for i in range(2 * RING)])


def per_device(tokens, cotangent, diag_factor, section_factors, low_down, low_up):
    rows, width = tokens.shape
    scale = (rows * lax.axis_size("dp")) ** -0.5
    x = lax.axis_index("dp") // RING
    half = width // 2

    h0 = tokens[:, :half]
    m4_0, m2_0 = flip(h0, 4), flip(h0, 2)
    m1 = flip(tokens, 1)
    part = jnp.dot(tokens, low_down, preferred_element_type=F32)
    part = part + flip(part, 12)
    h1 = after(tokens, part)[:, half:]
    part = part + flip(part, 4)
    m8_0 = flip(after(m4_0, part), 12)
    m4_1 = flip(after(h1, m4_0, part), 4)
    part = part + flip(part, 2)
    m2_1 = flip(after(h1, m2_0, part), 2)
    m8_1 = flip(m4_1, 12)
    part = part + flip(part, 1)
    latent = part.astype(BF16)
    others = cross(lax.dynamic_slice_in_dim(after(tokens, m2_1), (1 - x) * half, half, axis=1))

    factors = (cotangent, diag_factor, section_factors, latent, low_up)
    slope0, lat0, grads = run_main(0, tokens, (m1, m2_0, m4_0, m8_0), *factors, None)
    slope1, lat1, grads = run_main(1, tokens, (m1, m2_1, m4_1, m8_1), *factors, grads)
    summed = ring_sum(grads)

    part = lat0 + lat1
    arrived = flip(part, 12)
    b1, b2_0, b2_1, b4_0, b4_1, b8_0, b8_1 = run_back((slope0, slope1), section_factors)
    part = part + after(arrived, b1, others)
    q0, q1 = flip(after(b8_0, part), 12), flip(after(b8_1, part), 12)
    part = part + flip(part, 2)
    r2_0, r1 = flip(after(b2_0, part), 2), flip(after(b1, part), 1)
    part = part + flip(part, 4)
    part = part + after(flip(part, 1), r1)
    latent_grad = part.astype(BF16)

    z = lax.axis_index("dp") % RING
    left = run_down(x, z, tokens, others, latent_grad, after(cross(latent_grad), r2_0))
    s0 = flip(b4_0 + after(q0, left), 4)
    r2_1 = flip(after(b2_1, left), 2)
    s1 = flip(b4_1 + after(q1, left), 4)
    other = lax.dynamic_index_in_dim(summed, 1 - x, 0, keepdims=False)
    arrived = cross(other)
    for mask, events in ((1, (q1,)), (2, (s0,)), (4, (s1, r2_1, arrived))):
        count = left.shape[0] // 2
        got = lax.ppermute(left[count:], "dp", [(i, i ^ mask) for i in range(2 * RING)])
        left = left[:count].astype(F32) + after(got, *events).astype(F32)
        if mask < 4:
            left = left.astype(BF16)
    down_grad = (left[0] * scale).T
    pairs = ((slope0, slope1), (r2_0, r2_1), (s0, after(s1, other)))
    token_grad = run_final(pairs, r1, diag_factor, low_down, latent_grad)
    diag_grad, section_grad, up_grad = run_finish(x, summed, arrived, scale)
    return token_grad, diag_grad, section_grad, down_grad, up_grad


def solution(mesh):
    placed = (
        P("dp", "tensor"),
        P("dp", "tensor"),
        P(None, "tensor"),
        P(None, None, "tensor"),
        P("tensor", None),
        P(None, "tensor"),
    )
    return jax.shard_map(
        per_device,
        mesh=mesh,
        in_specs=placed,
        out_specs=(
            P("dp", "tensor"),
            P(None, ("tensor", "dp")),
            P(None, None, ("tensor", "dp")),
            P(("tensor", "dp"), None),
            P(None, ("tensor", "dp")),
        ),
        check_vma=False,
    )
```

```python
import functools

import jax
import jax.numpy as jnp
from jax import lax
from jax.experimental import pallas as pl
from jax.experimental.pallas import tpu as pltpu
from jax.sharding import PartitionSpec as P

BLOCK = 64
CHUNK = 256
MAIN_STEP, FINAL_STEP = 512, 2048
RING = 8
VMEM = 62 << 20
F32 = jnp.float32
BF16 = jnp.bfloat16


def dot(a, b, ca, cb):
    return lax.dot_general(a, b, (((ca,), (cb,)), ((), ())), preferred_element_type=F32)


def gelu_slope(values):
    return (
        0.5 * (1.0 + lax.erf(values * 0.7071067811865476))
        + values * jnp.exp(-0.5 * values * values) * 0.3989422804014327
    )


def block_mask():
    row = lax.broadcasted_iota(jnp.int32, (CHUNK, CHUNK), 0) // BLOCK
    col = lax.broadcasted_iota(jnp.int32, (CHUNK, CHUNK), 1) // BLOCK
    return row == col


def spread(factor, mask):
    tall = jnp.concatenate([factor] * (CHUNK // BLOCK), axis=0)
    return jnp.where(mask, tall, jnp.zeros_like(tall))


def main_kernel(tok, m1, m2, m4, m8, cot, diag, sec, latent, up, *refs):
    slope_out, lat_out, grads = refs[-3:]
    mask = block_mask()
    lat = latent[...]
    group = CHUNK // BLOCK
    lat_sum = jnp.zeros((lat.shape[0], up.shape[0]), F32)
    for c in range(MAIN_STEP // CHUNK):
        cs = slice(c * CHUNK, (c + 1) * CHUNK)
        up_c = up[:, cs]
        sides = [tok[:, cs], m1[:, cs], m2[:, cs], m4[:, cs], m8[:, cs]]
        factors = [spread(diag[:, cs], mask)] + [spread(sec[b, :, cs], mask) for b in range(4)]
        left = jnp.concatenate(sides + [lat], axis=1)
        right = jnp.concatenate(factors + [up_c], axis=0)
        pre = dot(left, right, 1, 0)
        slope = (cot[:, cs].astype(F32) * gelu_slope(pre)).astype(BF16)
        slope_out[:, cs] = slope
        lat_sum = lat_sum + dot(slope, up_c, 1, 1)
        for k, side in enumerate(sides):
            full = dot(side, slope, 0, 0)
            kept = jnp.where(mask, full, jnp.zeros_like(full))
            part = sum(kept[i * BLOCK : (i + 1) * BLOCK] for i in range(group))
            grads[c, 0, k * BLOCK : (k + 1) * BLOCK, :] = part.astype(BF16)
        grads[c, 0, 5 * BLOCK :, :] = dot(lat, slope, 0, 0).astype(BF16)

    @pl.when(pl.program_id(0) == 0)
    def _():
        lat_out[...] = lat_sum

    @pl.when(pl.program_id(0) > 0)
    def _():
        lat_out[...] += lat_sum


def run_main(part, tokens, moved, cotangent, diag, section, latent, up, held):
    rows, width = moved[2].shape
    rank = up.shape[0]
    steps = width // MAIN_STEP
    base = part * steps
    whole = lambda r: pl.BlockSpec((r, MAIN_STEP), lambda i: (0, base + i))
    local = pl.BlockSpec((rows, MAIN_STEP), lambda i: (0, i))
    square = pl.BlockSpec((rows, rank), lambda i: (0, 0))
    section_spec = pl.BlockSpec((4, BLOCK, MAIN_STEP), lambda i: (0, 0, base + i))
    grad_rows = 5 * BLOCK + rank
    in_specs = [whole(rows), whole(rows), local, local, local, whole(rows), whole(BLOCK), section_spec, square, whole(rank)]
    args = [tokens, *moved, cotangent, diag, section, latent, up]
    if held is not None:
        in_specs.append(pl.BlockSpec(memory_space=pl.ANY))
        args.append(held)
    return pl.pallas_call(
        main_kernel,
        grid=(steps,),
        in_specs=in_specs,
        out_specs=[local, square, pl.BlockSpec((MAIN_STEP // CHUNK, 1, grad_rows, CHUNK), lambda i: (i, part, 0, 0))],
        out_shape=[
            jax.ShapeDtypeStruct((rows, width), BF16),
            jax.ShapeDtypeStruct((rows, rank), F32),
            jax.ShapeDtypeStruct((RING, 2, grad_rows, CHUNK), BF16),
        ],
        input_output_aliases={} if held is None else {10: 2},
        compiler_params=pltpu.CompilerParams(vmem_limit_bytes=VMEM),
        cost_estimate=pl.CostEstimate(flops=2_000_000_000, bytes_accessed=28 << 20, transcendentals=0),
        name="main_part",
    )(*args)


def pick_half(low, high):
    first = pl.program_id(0) < pl.num_programs(0) // 2
    return jnp.where(first, low[...], high[...])


def half_specs(rows, steps):
    half = steps // 2
    return [
        pl.BlockSpec((rows, FINAL_STEP), lambda i: (0, jnp.minimum(i, half - 1))),
        pl.BlockSpec((rows, FINAL_STEP), lambda i: (0, jnp.maximum(i - half, 0))),
    ]


def back_kernel(low, high, sec, b1, *halves):
    mask = block_mask()

    def fill(slope, outs):
        for c in range(slope.shape[1] // CHUNK):
            cs = slice(c * CHUNK, (c + 1) * CHUNK)
            for b, out in enumerate(outs):
                out[:, cs] = dot(slope[:, cs], spread(sec[b, :, cs], mask), 1, 1).astype(BF16)

    pl.when(pl.program_id(0) == 0)(lambda: fill(low, (b1, *halves[0::2])))
    pl.when(pl.program_id(0) == 1)(lambda: fill(high, (b1, *halves[1::2])))


def run_back(slopes, section):
    rows, half = slopes[0].shape
    fixed = pl.BlockSpec((rows, half), lambda i: (0, 0))
    moving = pl.BlockSpec((rows, half), lambda i: (0, i))
    return pl.pallas_call(
        back_kernel,
        grid=(2,),
        in_specs=[fixed, fixed, pl.BlockSpec((4, BLOCK, half), lambda i: (0, 0, i))],
        out_specs=[moving] + [fixed] * 6,
        out_shape=[jax.ShapeDtypeStruct((rows, 2 * half), BF16)] + [jax.ShapeDtypeStruct((rows, half), BF16)] * 6,
        compiler_params=pltpu.CompilerParams(vmem_limit_bytes=VMEM),
        cost_estimate=pl.CostEstimate(flops=2_000_000_000, bytes_accessed=20 << 20, transcendentals=0),
        name="back_products",
    )(*slopes, section)


def down_kernel(place, tok, others, lat, lat_others, out):
    both = jnp.concatenate([lat[...], lat_others[...]], axis=0)
    count = tok.shape[1] // CHUNK
    for c in range(count):
        cs = slice(c * CHUNK, (c + 1) * CHUNK)
        bits = (pl.program_id(0) * count + c) ^ place[1]
        slot = (bits & 1) * 4 + (bits & 2) + bits // 4
        out[slot] = dot(both, jnp.concatenate([tok[:, cs], others[:, cs]], axis=0), 0, 0).astype(BF16)


def run_down(x, z, tokens, others, latent_grad, latent_others):
    rows, half = others.shape
    rank = latent_grad.shape[1]
    step = half // 2
    square = pl.BlockSpec((rows, rank), lambda i, place: (0, 0))
    return pl.pallas_call(
        down_kernel,
        grid_spec=pltpu.PrefetchScalarGridSpec(
            num_scalar_prefetch=1,
            grid=(2,),
            in_specs=[
                pl.BlockSpec((rows, step), lambda i, place: (0, 2 * place[0] + i)),
                pl.BlockSpec((rows, step), lambda i, place: (0, i)),
                square,
                square,
            ],
            out_specs=pl.BlockSpec((RING, rank, CHUNK), lambda i, place: (0, 0, 0)),
        ),
        out_shape=jax.ShapeDtypeStruct((RING, rank, CHUNK), BF16),
        cost_estimate=pl.CostEstimate(flops=300_000_000, bytes_accessed=10 << 20, transcendentals=0),
        name="down_part",
    )(jnp.stack([x, z]).astype(jnp.int32), tokens, others, latent_grad, latent_others)


def final_kernel(*refs):
    pairs, (r1, diag, down, lat, out) = refs[:6], refs[6:]
    mask = block_mask()
    slope, r2, r48 = (pick_half(pairs[2 * k], pairs[2 * k + 1]) for k in range(3))
    for c in range(FINAL_STEP // CHUNK):
        cs = slice(c * CHUNK, (c + 1) * CHUNK)
        total = dot(slope[:, cs], spread(diag[:, cs], mask), 1, 1)
        total = total + dot(lat[...], down[cs, :], 1, 1)
        for value in (r1, r2, r48):
            total = total + value[:, cs].astype(F32)
        out[:, cs] = total.astype(BF16)


def run_final(pairs, r1, diag, low_down, latent_grad):
    rows, half_width = pairs[0][0].shape
    width = 2 * half_width
    rank = latent_grad.shape[1]
    steps = width // FINAL_STEP
    col = lambda r: pl.BlockSpec((r, FINAL_STEP), lambda i: (0, i))
    return pl.pallas_call(
        final_kernel,
        grid=(steps,),
        in_specs=half_specs(rows, steps) * 3
        + [
            col(rows),
            col(BLOCK),
            pl.BlockSpec((FINAL_STEP, rank), lambda i: (i, 0)),
            pl.BlockSpec((rows, rank), lambda i: (0, 0)),
        ],
        out_specs=col(rows),
        out_shape=jax.ShapeDtypeStruct((rows, width), BF16),
        compiler_params=pltpu.CompilerParams(vmem_limit_bytes=VMEM),
        cost_estimate=pl.CostEstimate(flops=2_000_000_000, bytes_accessed=17 << 20, transcendentals=0),
        name="token_grad",
    )(*[value for pair in pairs for value in pair], r1, diag, low_down, latent_grad)


def finish_kernel(scale, side, summed, arrived, diag, section, up):
    total = (summed[0].astype(F32) + arrived[...].astype(F32)) * scale
    diag[...] = total[:BLOCK]
    for b in range(4):
        section[b] = total[(b + 1) * BLOCK : (b + 2) * BLOCK]
    up[...] = total[5 * BLOCK :]


def run_finish(x, summed, arrived, scale):
    _, rows, width = summed.shape
    rank = rows - 5 * BLOCK
    return pl.pallas_call(
        functools.partial(finish_kernel, scale),
        grid_spec=pltpu.PrefetchScalarGridSpec(
            num_scalar_prefetch=1,
            grid=(1,),
            in_specs=[
                pl.BlockSpec((1, rows, width), lambda i, side: (side[0], 0, 0)),
                pl.BlockSpec((rows, width), lambda i, side: (0, 0)),
            ],
            out_specs=[
                pl.BlockSpec((BLOCK, width), lambda i, side: (0, 0)),
                pl.BlockSpec((4, BLOCK, width), lambda i, side: (0, 0, 0)),
                pl.BlockSpec((rank, width), lambda i, side: (0, 0)),
            ],
        ),
        out_shape=[
            jax.ShapeDtypeStruct((BLOCK, width), F32),
            jax.ShapeDtypeStruct((4, BLOCK, width), F32),
            jax.ShapeDtypeStruct((rank, width), F32),
        ],
        cost_estimate=pl.CostEstimate(flops=300_000, bytes_accessed=4 << 20, transcendentals=0),
        name="finish",
    )(jnp.full((1,), x, jnp.int32), summed, arrived)


def flip(value, mask):
    return lax.ppermute(value, "tensor", [(i, i ^ mask) for i in range(16)])


def after(value, *events):
    return lax.optimization_barrier((value, *events))[0]


def ring_sum(grads):
    ring, sides, rows, width = grads.shape
    groups = [[x * RING + z for z in range(RING)] for x in range(2)]
    total = lax.psum_scatter(
        grads.reshape(ring * sides * rows, width), "dp", scatter_dimension=0, axis_index_groups=groups, tiled=True
    )
    return total.reshape(sides, rows, width)


def cross(value):
    return lax.ppermute(value, "dp", [(i, i ^ RING) for i in range(2 * RING)])


def per_device(tokens, cotangent, diag_factor, section_factors, low_down, low_up):
    rows, width = tokens.shape
    scale = (rows * lax.axis_size("dp")) ** -0.5
    x = lax.axis_index("dp") // RING
    half = width // 2

    h0 = tokens[:, :half]
    m4_0, m2_0 = flip(h0, 4), flip(h0, 2)
    m1 = flip(tokens, 1)
    part = jnp.dot(tokens, low_down, preferred_element_type=F32)
    part = part + flip(part, 12)
    h1 = after(tokens, part)[:, half:]
    part = part + flip(part, 4)
    m8_0 = flip(after(m4_0, part), 12)
    m4_1 = flip(after(h1, m4_0, part), 4)
    part = part + flip(part, 2)
    m2_1 = flip(after(h1, m2_0, part), 2)
    m8_1 = flip(m4_1, 12)
    part = part + flip(part, 1)
    latent = part.astype(BF16)
    others = cross(lax.dynamic_slice_in_dim(after(tokens, m2_1), (1 - x) * half, half, axis=1))

    factors = (cotangent, diag_factor, section_factors, latent, low_up)
    slope0, lat0, grads = run_main(0, tokens, (m1, m2_0, m4_0, m8_0), *factors, None)
    slope1, lat1, grads = run_main(1, tokens, (m1, m2_1, m4_1, m8_1), *factors, grads)
    summed = ring_sum(grads)

    part = lat0 + lat1
    arrived = flip(part, 12)
    b1, b2_0, b2_1, b4_0, b4_1, b8_0, b8_1 = run_back((slope0, slope1), section_factors)
    part = part + after(arrived, b1, others)
    q0, q1 = flip(after(b8_0, part), 12), flip(after(b8_1, part), 12)
    part = part + flip(part, 2)
    r2_0, r1 = flip(after(b2_0, part), 2), flip(after(b1, part), 1)
    part = part + flip(part, 4)
    part = part + after(flip(part, 1), r1, q0)
    latent_grad = part.astype(BF16)

    z = lax.axis_index("dp") % RING
    left = run_down(x, z, tokens, others, latent_grad, after(cross(latent_grad), r2_0))
    s0 = flip(b4_0 + after(q0, left), 4)
    r2_1 = flip(after(b2_1, left), 2)
    s1 = flip(b4_1 + after(q1, left), 4)
    other = lax.dynamic_index_in_dim(summed, 1 - x, 0, keepdims=False)
    arrived = cross(other)
    for mask, events in ((1, (q1,)), (2, (s0,)), (4, (s1, r2_1, arrived))):
        count = left.shape[0] // 2
        got = lax.ppermute(left[count:], "dp", [(i, i ^ mask) for i in range(2 * RING)])
        left = left[:count].astype(F32) + after(got, *events).astype(F32)
        if mask < 4:
            left = left.astype(BF16)
    down_grad = (left[0] * scale).T
    pairs = ((slope0, slope1), (r2_0, r2_1), (s0, after(s1, other)))
    token_grad = run_final(pairs, r1, diag_factor, low_down, latent_grad)
    diag_grad, section_grad, up_grad = run_finish(x, summed, arrived, scale)
    return token_grad, diag_grad, section_grad, down_grad, up_grad


def solution(mesh):
    placed = (
        P("dp", "tensor"),
        P("dp", "tensor"),
        P(None, "tensor"),
        P(None, None, "tensor"),
        P("tensor", None),
        P(None, "tensor"),
    )
    return jax.shard_map(
        per_device,
        mesh=mesh,
        in_specs=placed,
        out_specs=(
            P("dp", "tensor"),
            P(None, ("tensor", "dp")),
            P(None, None, ("tensor", "dp")),
            P(("tensor", "dp"), None),
            P(None, ("tensor", "dp")),
        ),
        check_vma=False,
    )
```

```python
import functools

import jax
import jax.numpy as jnp
from jax import lax
from jax.experimental import pallas as pl
from jax.experimental.pallas import tpu as pltpu
from jax.sharding import PartitionSpec as P

BLOCK = 64
CHUNK = 256
MAIN_STEP, FINAL_STEP = 512, 2048
RING = 8
VMEM = 62 << 20
F32 = jnp.float32
BF16 = jnp.bfloat16


def dot(a, b, ca, cb):
    return lax.dot_general(a, b, (((ca,), (cb,)), ((), ())), preferred_element_type=F32)


def gelu_slope(values):
    return (
        0.5 * (1.0 + lax.erf(values * 0.7071067811865476))
        + values * jnp.exp(-0.5 * values * values) * 0.3989422804014327
    )


def block_mask():
    row = lax.broadcasted_iota(jnp.int32, (CHUNK, CHUNK), 0) // BLOCK
    col = lax.broadcasted_iota(jnp.int32, (CHUNK, CHUNK), 1) // BLOCK
    return row == col


def spread(factor, mask):
    tall = jnp.concatenate([factor] * (CHUNK // BLOCK), axis=0)
    return jnp.where(mask, tall, jnp.zeros_like(tall))


def main_kernel(tok, m1, m2, m4, m8, cot, diag, sec, latent, up, *refs):
    slope_out, lat_out, grads = refs[-3:]
    mask = block_mask()
    lat = latent[...]
    group = CHUNK // BLOCK
    lat_sum = jnp.zeros((lat.shape[0], up.shape[0]), F32)
    for c in range(MAIN_STEP // CHUNK):
        cs = slice(c * CHUNK, (c + 1) * CHUNK)
        up_c = up[:, cs]
        sides = [tok[:, cs], m1[:, cs], m2[:, cs], m4[:, cs], m8[:, cs]]
        factors = [spread(diag[:, cs], mask)] + [spread(sec[b, :, cs], mask) for b in range(4)]
        left = jnp.concatenate(sides + [lat], axis=1)
        right = jnp.concatenate(factors + [up_c], axis=0)
        pre = dot(left, right, 1, 0)
        slope = (cot[:, cs].astype(F32) * gelu_slope(pre)).astype(BF16)
        slope_out[:, cs] = slope
        lat_sum = lat_sum + dot(slope, up_c, 1, 1)
        for k, side in enumerate(sides):
            full = dot(side, slope, 0, 0)
            kept = jnp.where(mask, full, jnp.zeros_like(full))
            part = sum(kept[i * BLOCK : (i + 1) * BLOCK] for i in range(group))
            grads[c, 0, k * BLOCK : (k + 1) * BLOCK, :] = part.astype(BF16)
        grads[c, 0, 5 * BLOCK :, :] = dot(lat, slope, 0, 0).astype(BF16)

    @pl.when(pl.program_id(0) == 0)
    def _():
        lat_out[...] = lat_sum

    @pl.when(pl.program_id(0) > 0)
    def _():
        lat_out[...] += lat_sum


def run_main(part, tokens, moved, cotangent, diag, section, latent, up, held):
    rows, width = moved[2].shape
    rank = up.shape[0]
    steps = width // MAIN_STEP
    base = part * steps
    whole = lambda r: pl.BlockSpec((r, MAIN_STEP), lambda i: (0, base + i))
    local = pl.BlockSpec((rows, MAIN_STEP), lambda i: (0, i))
    square = pl.BlockSpec((rows, rank), lambda i: (0, 0))
    section_spec = pl.BlockSpec((4, BLOCK, MAIN_STEP), lambda i: (0, 0, base + i))
    grad_rows = 5 * BLOCK + rank
    in_specs = [whole(rows), whole(rows), local, local, local, whole(rows), whole(BLOCK), section_spec, square, whole(rank)]
    args = [tokens, *moved, cotangent, diag, section, latent, up]
    if held is not None:
        in_specs.append(pl.BlockSpec(memory_space=pl.ANY))
        args.append(held)
    return pl.pallas_call(
        main_kernel,
        grid=(steps,),
        in_specs=in_specs,
        out_specs=[local, square, pl.BlockSpec((MAIN_STEP // CHUNK, 1, grad_rows, CHUNK), lambda i: (i, part, 0, 0))],
        out_shape=[
            jax.ShapeDtypeStruct((rows, width), BF16),
            jax.ShapeDtypeStruct((rows, rank), F32),
            jax.ShapeDtypeStruct((RING, 2, grad_rows, CHUNK), BF16),
        ],
        input_output_aliases={} if held is None else {10: 2},
        compiler_params=pltpu.CompilerParams(vmem_limit_bytes=VMEM),
        cost_estimate=pl.CostEstimate(flops=2_000_000_000, bytes_accessed=28 << 20, transcendentals=0),
        name="main_part",
    )(*args)


def pick_half(low, high):
    first = pl.program_id(0) < pl.num_programs(0) // 2
    return jnp.where(first, low[...], high[...])


def half_specs(rows, steps):
    half = steps // 2
    return [
        pl.BlockSpec((rows, FINAL_STEP), lambda i: (0, jnp.minimum(i, half - 1))),
        pl.BlockSpec((rows, FINAL_STEP), lambda i: (0, jnp.maximum(i - half, 0))),
    ]


def back_kernel(low, high, sec, b1, *halves):
    mask = block_mask()

    def fill(slope, outs):
        for c in range(slope.shape[1] // CHUNK):
            cs = slice(c * CHUNK, (c + 1) * CHUNK)
            for b, out in enumerate(outs):
                out[:, cs] = dot(slope[:, cs], spread(sec[b, :, cs], mask), 1, 1).astype(BF16)

    pl.when(pl.program_id(0) == 0)(lambda: fill(low, (b1, *halves[0::2])))
    pl.when(pl.program_id(0) == 1)(lambda: fill(high, (b1, *halves[1::2])))


def run_back(slopes, section):
    rows, half = slopes[0].shape
    fixed = pl.BlockSpec((rows, half), lambda i: (0, 0))
    moving = pl.BlockSpec((rows, half), lambda i: (0, i))
    return pl.pallas_call(
        back_kernel,
        grid=(2,),
        in_specs=[fixed, fixed, pl.BlockSpec((4, BLOCK, half), lambda i: (0, 0, i))],
        out_specs=[moving] + [fixed] * 6,
        out_shape=[jax.ShapeDtypeStruct((rows, 2 * half), BF16)] + [jax.ShapeDtypeStruct((rows, half), BF16)] * 6,
        compiler_params=pltpu.CompilerParams(vmem_limit_bytes=VMEM),
        cost_estimate=pl.CostEstimate(flops=2_000_000_000, bytes_accessed=20 << 20, transcendentals=0),
        name="back_products",
    )(*slopes, section)


def down_kernel(place, tok, others, lat, lat_others, out):
    both = jnp.concatenate([lat[...], lat_others[...]], axis=0)
    count = tok.shape[1] // CHUNK
    for c in range(count):
        cs = slice(c * CHUNK, (c + 1) * CHUNK)
        bits = (pl.program_id(0) * count + c) ^ place[1]
        slot = (bits & 1) * 4 + (bits & 2) + bits // 4
        out[slot] = dot(both, jnp.concatenate([tok[:, cs], others[:, cs]], axis=0), 0, 0).astype(BF16)


def run_down(x, z, tokens, others, latent_grad, latent_others):
    rows, half = others.shape
    rank = latent_grad.shape[1]
    step = half // 2
    square = pl.BlockSpec((rows, rank), lambda i, place: (0, 0))
    return pl.pallas_call(
        down_kernel,
        grid_spec=pltpu.PrefetchScalarGridSpec(
            num_scalar_prefetch=1,
            grid=(2,),
            in_specs=[
                pl.BlockSpec((rows, step), lambda i, place: (0, 2 * place[0] + i)),
                pl.BlockSpec((rows, step), lambda i, place: (0, i)),
                square,
                square,
            ],
            out_specs=pl.BlockSpec((RING, rank, CHUNK), lambda i, place: (0, 0, 0)),
        ),
        out_shape=jax.ShapeDtypeStruct((RING, rank, CHUNK), BF16),
        cost_estimate=pl.CostEstimate(flops=300_000_000, bytes_accessed=10 << 20, transcendentals=0),
        name="down_part",
    )(jnp.stack([x, z]).astype(jnp.int32), tokens, others, latent_grad, latent_others)


def final_kernel(*refs):
    pairs, (r1, diag, down, lat, out) = refs[:6], refs[6:]
    mask = block_mask()
    slope, r2, r48 = (pick_half(pairs[2 * k], pairs[2 * k + 1]) for k in range(3))
    for c in range(FINAL_STEP // CHUNK):
        cs = slice(c * CHUNK, (c + 1) * CHUNK)
        total = dot(slope[:, cs], spread(diag[:, cs], mask), 1, 1)
        total = total + dot(lat[...], down[cs, :], 1, 1)
        for value in (r1, r2, r48):
            total = total + value[:, cs].astype(F32)
        out[:, cs] = total.astype(BF16)


def run_final(pairs, r1, diag, low_down, latent_grad):
    rows, half_width = pairs[0][0].shape
    width = 2 * half_width
    rank = latent_grad.shape[1]
    steps = width // FINAL_STEP
    col = lambda r: pl.BlockSpec((r, FINAL_STEP), lambda i: (0, i))
    return pl.pallas_call(
        final_kernel,
        grid=(steps,),
        in_specs=half_specs(rows, steps) * 3
        + [
            col(rows),
            col(BLOCK),
            pl.BlockSpec((FINAL_STEP, rank), lambda i: (i, 0)),
            pl.BlockSpec((rows, rank), lambda i: (0, 0)),
        ],
        out_specs=col(rows),
        out_shape=jax.ShapeDtypeStruct((rows, width), BF16),
        compiler_params=pltpu.CompilerParams(vmem_limit_bytes=VMEM),
        cost_estimate=pl.CostEstimate(flops=2_000_000_000, bytes_accessed=17 << 20, transcendentals=0),
        name="token_grad",
    )(*[value for pair in pairs for value in pair], r1, diag, low_down, latent_grad)


def finish_kernel(scale, side, summed, arrived, diag, section, up):
    total = (summed[0].astype(F32) + arrived[...].astype(F32)) * scale
    diag[...] = total[:BLOCK]
    for b in range(4):
        section[b] = total[(b + 1) * BLOCK : (b + 2) * BLOCK]
    up[...] = total[5 * BLOCK :]


def run_finish(x, summed, arrived, scale):
    _, rows, width = summed.shape
    rank = rows - 5 * BLOCK
    return pl.pallas_call(
        functools.partial(finish_kernel, scale),
        grid_spec=pltpu.PrefetchScalarGridSpec(
            num_scalar_prefetch=1,
            grid=(1,),
            in_specs=[
                pl.BlockSpec((1, rows, width), lambda i, side: (side[0], 0, 0)),
                pl.BlockSpec((rows, width), lambda i, side: (0, 0)),
            ],
            out_specs=[
                pl.BlockSpec((BLOCK, width), lambda i, side: (0, 0)),
                pl.BlockSpec((4, BLOCK, width), lambda i, side: (0, 0, 0)),
                pl.BlockSpec((rank, width), lambda i, side: (0, 0)),
            ],
        ),
        out_shape=[
            jax.ShapeDtypeStruct((BLOCK, width), F32),
            jax.ShapeDtypeStruct((4, BLOCK, width), F32),
            jax.ShapeDtypeStruct((rank, width), F32),
        ],
        cost_estimate=pl.CostEstimate(flops=300_000, bytes_accessed=4 << 20, transcendentals=0),
        name="finish",
    )(jnp.full((1,), x, jnp.int32), summed, arrived)


def flip(value, mask):
    return lax.ppermute(value, "tensor", [(i, i ^ mask) for i in range(16)])


def after(value, *events):
    return lax.optimization_barrier((value, *events))[0]


def ring_sum(grads):
    ring, sides, rows, width = grads.shape
    groups = [[x * RING + z for z in range(RING)] for x in range(2)]
    total = lax.psum_scatter(
        grads.reshape(ring * sides * rows, width), "dp", scatter_dimension=0, axis_index_groups=groups, tiled=True
    )
    return total.reshape(sides, rows, width)


def cross(value):
    return lax.ppermute(value, "dp", [(i, i ^ RING) for i in range(2 * RING)])


def per_device(tokens, cotangent, diag_factor, section_factors, low_down, low_up):
    rows, width = tokens.shape
    scale = (rows * lax.axis_size("dp")) ** -0.5
    x = lax.axis_index("dp") // RING
    half = width // 2

    h0 = tokens[:, :half]
    m4_0, m2_0 = flip(h0, 4), flip(h0, 2)
    m1 = flip(tokens, 1)
    part = jnp.dot(tokens, low_down, preferred_element_type=F32)
    part = part + flip(part, 12)
    h1 = after(tokens, part)[:, half:]
    part = part + flip(part, 4)
    m8_0 = flip(after(m4_0, part), 12)
    m4_1 = flip(after(h1, m4_0, part), 4)
    part = part + flip(part, 2)
    m2_1 = flip(after(h1, m2_0, part), 2)
    m8_1 = flip(m4_1, 12)
    part = part + flip(part, 1)
    latent = part.astype(BF16)
    others = cross(lax.dynamic_slice_in_dim(after(tokens, m2_1), (1 - x) * half, half, axis=1))

    factors = (cotangent, diag_factor, section_factors, latent, low_up)
    slope0, lat0, grads = run_main(0, tokens, (m1, m2_0, m4_0, m8_0), *factors, None)
    slope1, lat1, grads = run_main(1, tokens, (m1, m2_1, m4_1, m8_1), *factors, grads)
    summed = ring_sum(grads)

    part = lat0 + lat1
    arrived = flip(part, 12)
    b1, b2_0, b2_1, b4_0, b4_1, b8_0, b8_1 = run_back((slope0, slope1), section_factors)
    part = part + after(arrived, b1, others)
    q0, q1 = flip(after(b8_0, part), 12), flip(after(b8_1, part), 12)
    part = part + flip(part, 2)
    r2_0, r1 = flip(after(b2_0, part), 2), flip(after(b1, part), 1)
    part = part + flip(part, 4)
    part = part + after(flip(part, 1), r1)
    latent_grad = part.astype(BF16)

    z = lax.axis_index("dp") % RING
    left = run_down(x, z, tokens, others, latent_grad, after(cross(latent_grad), r2_0, q0))
    s0 = flip(b4_0 + after(q0, left), 4)
    r2_1 = flip(after(b2_1, left), 2)
    s1 = flip(b4_1 + after(q1, left), 4)
    other = lax.dynamic_index_in_dim(summed, 1 - x, 0, keepdims=False)
    arrived = cross(other)
    for mask, events in ((1, (q1, other)), (2, (s0,)), (4, (s1, r2_1, arrived))):
        count = left.shape[0] // 2
        got = lax.ppermute(left[count:], "dp", [(i, i ^ mask) for i in range(2 * RING)])
        left = left[:count].astype(F32) + after(got, *events).astype(F32)
        if mask < 4:
            left = left.astype(BF16)
    down_grad = (left[0] * scale).T
    pairs = ((slope0, slope1), (r2_0, r2_1), (s0, after(s1, other)))
    token_grad = run_final(pairs, r1, diag_factor, low_down, latent_grad)
    diag_grad, section_grad, up_grad = run_finish(x, summed, arrived, scale)
    return token_grad, diag_grad, section_grad, down_grad, up_grad


def solution(mesh):
    placed = (
        P("dp", "tensor"),
        P("dp", "tensor"),
        P(None, "tensor"),
        P(None, None, "tensor"),
        P("tensor", None),
        P(None, "tensor"),
    )
    return jax.shard_map(
        per_device,
        mesh=mesh,
        in_specs=placed,
        out_specs=(
            P("dp", "tensor"),
            P(None, ("tensor", "dp")),
            P(None, None, ("tensor", "dp")),
            P(("tensor", "dp"), None),
            P(None, ("tensor", "dp")),
        ),
        check_vma=False,
    )
```
